32 devices in a mesh: dp: 2 (over x), ctx: 16 (over z, y, core).
Axes of the slice: x: 2, y: 2, z: 4, core: 2. Of those that a mesh axis runs over, the one named last changes fastest.
Arguments:
- tokens: bfloat16 [2, 2, 1024, 1536], P(None, 'dp', 'ctx'), may hold values from -6 to 6
- lengths: int32 [2, 2], P(None, 'dp'), may hold values from 256 to 1024, as said below
- routes: int32 [2, 2, 1024, 2], P(None, 'dp', 'ctx'), may hold values from 0 to 3, all different within a row
- cotangent: bfloat16 [2, 2, 1024, 1536], P(None, 'dp', 'ctx'), may hold values from -6 to 6
- attn_gain: bfloat16 [1536], P(('dp', 'ctx')), may hold values from 0.5 to 1.5
- qkv_weight: bfloat16 [1536, 2560], P(('dp', 'ctx')), may hold values from -0.15625 to 0.15625
- out_weight: bfloat16 [1536, 1536], P(None, ('dp', 'ctx')), may hold values from -1.75 to 1.75
- moe_gain: bfloat16 [1536], P(('dp', 'ctx')), may hold values from 0.5 to 1.5
- router: bfloat16 [1536, 4], P(('dp', 'ctx')), may hold values from -0.109375 to 0.109375
- gateup_weight: bfloat16 [4, 1536, 2048], P(None, ('dp', 'ctx')), may hold values from -0.15625 to 0.15625
- down_weight: bfloat16 [4, 1024, 1536], P(None, None, ('dp', 'ctx')), may hold values from -0.1875 to 0.1875
Outputs:
- output: bfloat16 [2, 2, 1024, 1536], P(None, 'dp', 'ctx')
- grad_tokens: bfloat16 [2, 2, 1024, 1536], P(None, 'dp', 'ctx')
- grad_attn_gain: float32 [1536], P(('dp', 'ctx'))
- grad_qkv_weight: float32 [1536, 2560], P(('dp', 'ctx'))
- grad_out_weight: float32 [1536, 1536], P(None, ('dp', 'ctx'))
- grad_moe_gain: float32 [1536], P(('dp', 'ctx'))
- grad_router: float32 [1536, 4], P(('dp', 'ctx'))
- grad_gateup_weight: float32 [4, 1536, 2048], P(None, ('dp', 'ctx'))
- grad_down_weight: float32 [4, 1024, 1536], P(None, None, ('dp', 'ctx'))
The draws below stay inside these ranges and needn't reach their ends.
Inputs may be any that keep to these rules, and one draw needn't show every extreme that they name: `lengths`: in every draw some sequence fills all 1024 slots. `routes`: each slot names 2 different experts.
All inputs are finite; a program needn't handle non-finite values.
Results may differ from the reference program's by a relative error of at most 0.014.
Values may be sent and summed in bfloat16 or wider, within the bound.
No kernel may reach another device: no remote copies, remote signals or barrier semaphores. Data moves between devices by JAX's collectives and lax.ppermute only.
A program may use at most 448 MiB of HBM per device.

```python
import jax
import jax.numpy as jnp
from jax import lax

D = 1536
H = 24
KVH = 8
HD = 64
FF = 1024
E = 4
TOPK = 2
MB = 2
NSEQ = 2
LENGTH = 1024
QW = 1536
KW = 512


def draw_lengths(key, part):
    first_key, second_key = jax.random.split(jax.random.fold_in(key, 11))
    drawn = jax.random.randint(first_key, (MB * NSEQ,), LENGTH // 4, LENGTH + 1)
    picked = jax.random.randint(second_key, (), 0, MB * NSEQ)
    filled = jnp.where(jnp.arange(MB * NSEQ) == picked, LENGTH, drawn)
    return filled.reshape(MB, NSEQ).astype(jnp.int32)


def level_of(key, extent, cuts, least, top_value):
    level = 1.0
    for dim, parts in cuts:
        heights = jax.random.uniform(jax.random.fold_in(jax.random.fold_in(key, 6), dim), (parts,), jnp.float32, least / len(cuts), top_value / len(cuts))
        level = level * jnp.repeat(jnp.exp(heights), extent[dim] // parts).reshape((-1,) + (1,) * (len(extent) - 1 - dim))
    return level


def picks_of(rng, rows, amount, top, lift):
    ranking = jax.random.permutation(jax.random.fold_in(rng, 1), amount)
    boost = ranking
    for power in range(3):
        boost = boost * boost // amount
    boost = boost * lift // amount
    chance = jax.random.randint(jax.random.fold_in(rng, 2), (rows, amount), 0, 4096) + boost
    fixed_rows = jax.random.permutation(jax.random.fold_in(rng, 3), rows)[jnp.arange(amount) % rows]
    chance = jnp.where(jnp.arange(rows)[:, None] == fixed_rows[None, :], 1 << 14, chance)
    priority = chance * amount + jnp.arange(amount)
    return lax.top_k(priority.astype(jnp.int32), top)[1].astype(jnp.int32)


def normal_values(own_key, extent, width, most, cuts=(), kind=jnp.bfloat16):
    array = jax.random.normal(own_key, extent, jnp.float32) * width
    if len(cuts) > 0:
        array = level_of(own_key, extent, cuts, -0.22, 0.18) * array
    return jnp.clip(array, min=-most, max=most).astype(kind)


def setup_inputs(seed: int = 0) -> dict:
    key_of = jax.random.split(jax.random.key(seed), 12)
    return {
        "tokens": normal_values(key_of[0], (MB, NSEQ, LENGTH, D), 1.0, 6.0, ((1, 2), (2, 16))),
        "lengths": draw_lengths(jax.random.fold_in(key_of[11], 71), 0),
        "routes": picks_of(key_of[2], MB * NSEQ * LENGTH, E, TOPK, 4096).reshape((MB, NSEQ, LENGTH, TOPK)),
        "cotangent": normal_values(key_of[3], (MB, NSEQ, LENGTH, D), 1.0, 6.0, ((1, 2), (2, 16))),
        "attn_gain": jnp.clip(1.0 + 0.1 * jax.random.normal(key_of[4], (D,), jnp.float32), 0.5, 1.5).astype(jnp.bfloat16),
        "qkv_weight": normal_values(key_of[5], (D, QW + 2 * KW), D ** -0.5, 0.15625, ((0, 32),)),
        "out_weight": normal_values(key_of[6], (QW, D), (max(1, QW * 8 // LENGTH)) ** -0.5, 1.75, ((1, 32),)),
        "moe_gain": jnp.clip(1.0 + 0.1 * jax.random.normal(key_of[7], (D,), jnp.float32), 0.5, 1.5).astype(jnp.bfloat16),
        "router": normal_values(key_of[8], (D, E), (2 * D) ** -0.5, 0.109375, ((0, 32),)),
        "gateup_weight": normal_values(key_of[9], (E, D, 2 * FF), D ** -0.5, 0.15625, ((1, 32),)),
        "down_weight": normal_values(key_of[10], (E, FF, D), FF ** -0.5, 0.1875, ((2, 32),)),
    }


@jax.custom_vjp
def low(v):
    return lax.optimization_barrier(v.astype(jnp.bfloat16)).astype(jnp.float32)

@jax.custom_vjp
def low_back(v):
    return v

def low_keep(v):
    return (low(v), None)

def low_pass(kept, grad):
    return (grad,)

def back_keep(v):
    return (v, None)

def back_low(kept, grad):
    return (low(grad),)
low.defvjp(low_keep, low_pass)
low_back.defvjp(back_keep, back_low)

def rms_scale(values, gain):
    return values * lax.rsqrt(lax.optimization_barrier(jnp.mean(values * values, axis=-1, keepdims=True)) + 1e-05) * gain

def gate_mix(logits, chosen):
    picked = lax.optimization_barrier(jnp.sum(chosen * logits[:, None, :], axis=-1))
    shares = jax.nn.softmax(picked, axis=-1)
    return lax.optimization_barrier(jnp.sum(shares[:, :, None] * chosen, axis=1))

def swiglu(gate_up):
    half_cols = gate_up.shape[1] // 2
    return jax.nn.silu(gate_up[:, :half_cols]) * gate_up[:, half_cols:]

def matmul(left, right):
    return jnp.dot(left, right, precision=lax.Precision.HIGHEST)

def attention(queries, keys, values, length):
    block_rows = min(512, LENGTH)
    key_pos = jnp.arange(LENGTH, dtype=jnp.int32)
    blocks = queries.reshape(LENGTH // block_rows, block_rows, KVH, H // KVH, HD)
    starts = jnp.arange(LENGTH // block_rows, dtype=jnp.int32) * block_rows
    keys_t = keys.transpose(1, 0, 2)
    values_t = values.transpose(1, 0, 2)

    def one_block(operands):
        query_block, start = operands
        query_pos = start + jnp.arange(block_rows, dtype=jnp.int32)
        allowed = (key_pos[None, :] <= query_pos[:, None]) & (key_pos[None, :] < length)

        def one_head(head_ops):
            head_query, head_keys, head_values = head_ops
            scores = jnp.einsum('sgd,td->gst', head_query, head_keys, precision=lax.Precision.HIGHEST) * 0.125
            scores = jnp.where(allowed[None], low_back(scores), -1e+30)
            attn_probs = low(jax.nn.softmax(scores, axis=-1))
            return jnp.einsum('gst,td->sgd', attn_probs, head_values, precision=lax.Precision.HIGHEST)
        outcome = lax.map(one_head, (query_block.transpose(1, 0, 2, 3), keys_t, values_t))
        return outcome.transpose(1, 0, 2, 3).reshape(block_rows, QW)
    return lax.map(jax.checkpoint(one_block), (blocks, starts)).reshape(LENGTH, QW)

def layer(token_rows, length, route_rows, attn_gain, qkv_weight, out_weight, moe_gain, router, gateup_weight, down_weight):
    groups = H // KVH
    valid_rows = (jnp.arange(LENGTH, dtype=jnp.int32) < length).astype(jnp.float32)[:, None]
    packed = low(rms_scale(token_rows, attn_gain))
    qkv = low(low_back(matmul(packed, qkv_weight)))
    queries = qkv[:, :QW].reshape(LENGTH, KVH, groups, HD)
    keys = qkv[:, QW:QW + KW].reshape(LENGTH, KVH, HD)
    values = qkv[:, QW + KW:].reshape(LENGTH, KVH, HD)
    attended = low_back(low(attention(queries, keys, values, length)))
    branch = low_back(matmul(attended, out_weight))
    mixed = token_rows + valid_rows * branch
    normed = low(rms_scale(mixed, moe_gain))
    logits = low_back(matmul(normed, router))
    chosen = (route_rows[:, :, None] == jnp.arange(E, dtype=jnp.int32)[None, None, :]).astype(jnp.float32)
    combine = gate_mix(logits, chosen)
    mixture = jnp.zeros((LENGTH, D), jnp.float32)
    for expert in range(E):
        gate_up = low_back(matmul(normed, gateup_weight[expert]))
        activated = low(swiglu(gate_up))
        expert_out = low_back(matmul(activated, down_weight[expert]))
        mixture = mixture + combine[:, expert:expert + 1] * expert_out
    return mixed + valid_rows * mixture

def forward(tokens, lengths, routes, attn_gain, qkv_weight, out_weight, moe_gain, router, gateup_weight, down_weight):
    count = MB * NSEQ
    seq_tokens = tokens.reshape(count, LENGTH, D)
    seq_lengths = lengths.reshape(count).astype(jnp.int32)
    seq_routes = routes.reshape(count, LENGTH, TOPK).astype(jnp.int32)
    checked = jax.checkpoint(layer)

    def step(carry, operands):
        rows, length, route_rows = operands
        return (carry, checked(rows, length, route_rows, attn_gain, qkv_weight, out_weight, moe_gain, router, gateup_weight, down_weight))
    carry, outcome = lax.scan(step, jnp.zeros((), jnp.float32), (seq_tokens, seq_lengths, seq_routes))
    return outcome.reshape(MB, NSEQ, LENGTH, D)

def reference(tokens, lengths, routes, cotangent, attn_gain, qkv_weight, out_weight, moe_gain, router, gateup_weight, down_weight):

    def apply(token_f, attn_f, qkv_f, out_f, moe_f, router_f, gateup_f, down_f):
        return forward(token_f, lengths, routes, attn_f, qkv_f, out_f, moe_f, router_f, gateup_f, down_f)
    result, pull_back = jax.vjp(apply, tokens.astype(jnp.float32), attn_gain.astype(jnp.float32), qkv_weight.astype(jnp.float32), out_weight.astype(jnp.float32), moe_gain.astype(jnp.float32), router.astype(jnp.float32), gateup_weight.astype(jnp.float32), down_weight.astype(jnp.float32))
    grads = pull_back(cotangent.astype(jnp.float32))
    return (result.astype(jnp.bfloat16), grads[0].astype(jnp.bfloat16), grads[1], grads[2], grads[3], grads[4], grads[5], grads[6], grads[7])
```

```python
import functools

import jax
import jax.numpy as jnp
from jax import lax
from jax.experimental import pallas as pl
from jax.experimental.pallas import tpu as pltpu
from jax.sharding import PartitionSpec as P

D = 1536
H = 24
KVH = 8
HD = 64
FF = 1024
E = 4
MB = 2
QW = 1536
KW = 512
CUBE = 8
GROUP = H // KVH
HALF = FF // 2
QH = GROUP * HD
SHARD = QH + 2 * HD
EXTRA = 128
WIDE = D + EXTRA
ORDER = (0, 4, 2, 6, 1, 5, 3, 7)
LOG2E = 1.4426950408889634
F32 = jnp.float32
BF16 = jnp.bfloat16
NN = (((1,), (0,)), ((), ()))
NT = (((1,), (1,)), ((), ()))
TN = (((0,), (0,)), ((), ()))
AXES = ("dp", "ctx")


def dot(left, right, dims=NN):
    return lax.dot_general(left, right, dims, preferred_element_type=F32)


def kernel_call(kernel, outs, ins, scratch=(), flops=0, scalars=True):
    vmem = pl.BlockSpec(memory_space=pltpu.VMEM)
    smem = pl.BlockSpec(memory_space=pltpu.SMEM)
    specs = [vmem] * len(ins)
    if scalars:
        specs[0] = smem
    moved = sum(a.size * a.dtype.itemsize for a in list(ins) + list(outs))
    return pl.pallas_call(
        kernel,
        out_shape=list(outs),
        in_specs=specs,
        out_specs=[vmem] * len(outs),
        scratch_shapes=list(scratch),
        compiler_params=pltpu.CompilerParams(vmem_limit_bytes=56 * 1024 * 1024),
        cost_estimate=pl.CostEstimate(flops=flops, bytes_accessed=moved, transcendentals=0),
    )(*ins)


def shape(dims, dtype=BF16):
    return jax.ShapeDtypeStruct(dims, dtype)


class Links:
    def __init__(self, nx, nc):
        self.nx, self.nc, self.ng = nx, nc, nc // CUBE

    def _pairs(self, move):
        pairs = []
        for x in range(self.nx):
            for g in range(self.ng):
                for t in range(CUBE):
                    goal = move(x, g, t)
                    if goal is not None:
                        gx, gg, gt = goal
                        pairs.append((x * self.nc + g * CUBE + t, gx * self.nc + gg * CUBE + gt))
        return pairs

    def cube(self, value, bits):
        return lax.ppermute(value, AXES, self._pairs(lambda x, g, t: (x, g, t ^ bits)))

    def outer(self, value, dx, dg):
        return lax.ppermute(value, AXES, self._pairs(lambda x, g, t: (x ^ dx, g ^ dg, t)))

    def climb(self, value, step):
        def move(x, g, t):
            return (x, g + step, t) if 0 <= g + step < self.ng else None

        return lax.ppermute(value, AXES, self._pairs(move))

    def cubes(self):
        return [
            [x * self.nc + g * CUBE + t for t in range(CUBE)]
            for x in range(self.nx)
            for g in range(self.ng)
        ]

    def swap(self, value):
        return lax.all_to_all(
            value, AXES, split_axis=0, concat_axis=0, tiled=True, axis_index_groups=self.cubes()
        )

    def cube_gather(self, rows):
        half = rows.shape[0] // 2
        far = self.cube(rows, 4)
        side = self.cube(rows, 2)
        low = self.cube(far[:half], 2)
        high = self.cube(side[half:], 4)
        near = [rows, far, side, low, high]
        return near + [self.cube(block, 1) for block in near]

    def outer_gather(self, rows):
        own = [rows] + [self.outer(rows, 0, dg) for dg in range(1, self.ng)]
        for dx in range(1, self.nx):
            own = own + [self.outer(block, dx, 0) for block in own[: self.ng]]
        return own

    def outer_scatter(self, parts, x, g):
        total = parts[0].astype(F32)
        for dx in range(1, self.nx):
            total = total + self.outer(parts[dx], dx, 0).astype(F32)
        rows = total.shape[0] // self.ng
        total = total.reshape(self.ng, rows, total.shape[1])
        own = lax.dynamic_index_in_dim(total, g, 0, keepdims=False)
        low = total.astype(BF16)
        for dg in range(1, self.ng):
            part = lax.dynamic_index_in_dim(low, g ^ dg, 0, keepdims=False)
            own = own + self.outer(part, 0, dg).astype(F32)
        return own


def cube_rows(refs, out, width=None):
    rows = refs[0].shape[0]
    half = rows // 2
    spots = (0, rows, 2 * rows, 3 * rows, 3 * rows + half)
    for base, group in ((0, refs[:5]), (4 * rows, refs[5:])):
        for spot, ref in zip(spots, group):
            out[base + spot : base + spot + ref.shape[0], :] = ref[...]


def outer_rows(refs, out, x, g, ng):
    rows = refs[0].shape[0]
    for j, ref in enumerate(refs):
        place = (x ^ (j // ng)) * ng + (g ^ (j % ng))
        out[pl.ds(pl.multiple_of(place * rows, 16), rows), :] = ref[...]


def qkv_kernel(ng, n_outer, scal, *refs):
    x, g = scal[0], scal[1]
    blocks, refs = refs[:10], refs[10:]
    weights, refs = refs[:n_outer], refs[n_outer:]
    xg, q_out, kv_out, w_full = refs
    cube_rows(blocks, xg)
    outer_rows(weights, w_full, x, g, ng)
    rows = blocks[0].shape[0]
    slots = rows // MB
    blank = jnp.zeros((slots, HD), BF16)
    for p, k in enumerate(ORDER):
        y = dot(xg[p * rows : (p + 1) * rows, :], w_full[...]).astype(BF16)
        for m in range(MB):
            part = y[m * slots : (m + 1) * slots]
            spot = slice(k * slots, (k + 1) * slots)
            for h in range(GROUP):
                q_out[m, h, spot, :] = jnp.concatenate(
                    [part[:, h * HD : (h + 1) * HD], blank], axis=1
                )
            kv_out[m, spot, :] = part[:, QH:]


def key_bias(block, slots, extent, g, t, step, length):
    local = lax.broadcasted_iota(jnp.int32, (extent, 1), 0) ^ (t * slots)
    seen = ((g - step) * extent + local < length) & (g >= step)
    return jnp.where(seen, 0.0, -1e30).astype(F32)


def causal_bias(slots, extent, t):
    keys = lax.broadcasted_iota(jnp.int32, (extent, extent), 0) ^ (t * slots)
    rows = lax.broadcasted_iota(jnp.int32, (extent, extent), 1) ^ (t * slots)
    return jnp.where(keys <= rows, 0.0, -1e30).astype(F32)


def attend_kernel(slots, scal, *refs):
    g, t = scal[1], scal[2]
    n_keys = len(refs) - 1 - CUBE - 2
    q_ref, kv_refs, refs = refs[0], refs[1 : 1 + n_keys], refs[1 + n_keys :]
    att_refs, (ot_ref, lse_ref) = refs[:CUBE], refs[CUBE:]
    extent = q_ref.shape[2]
    causal = causal_bias(slots, extent, t)
    for m in range(MB):
        length = scal[3 + m]
        biases = [key_bias(s, slots, extent, g, t, s, length) for s in range(n_keys)]
        for h in range(GROUP):
            q = q_ref[m, h]
            top = total = acc = None
            for s in range(n_keys):
                kv = kv_refs[s][m]
                st = dot(kv, q, NT) * (0.125 * LOG2E) + biases[s]
                if s == 0:
                    st = st + causal
                peak = jnp.max(st, axis=0, keepdims=True)
                if s == 0:
                    pt = jnp.exp2(st - peak)
                    top, total = peak, jnp.sum(pt, axis=0, keepdims=True)
                    acc = dot(kv, pt.astype(BF16), TN)
                else:
                    fresh = jnp.maximum(top, peak)
                    scale = jnp.exp2(top - fresh)
                    pt = jnp.exp2(st - fresh)
                    total = total * scale + jnp.sum(pt, axis=0, keepdims=True)
                    acc = acc * scale + dot(kv, pt.astype(BF16), TN)
                    top = fresh
            ot = acc[HD:, :] / total
            ot_ref[m, h] = ot
            lse_ref[m, h : h + 1, :] = top + jnp.log2(total)
            o = ot.T.astype(BF16)
            for k in range(CUBE):
                att_refs[k][m * slots : (m + 1) * slots, h * HD : (h + 1) * HD] = o[
                    k * slots : (k + 1) * slots
                ]


def row_valid(scal, rows):
    slots = rows // MB
    spot = lax.broadcasted_iota(jnp.int32, (rows, 1), 0)
    place = (scal[1] * CUBE + scal[2]) * slots
    length = jnp.where(spot < slots, scal[3], scal[4])
    inner = jnp.where(spot < slots, spot, spot - slots)
    return jnp.where(place + inner < length, 1.0, 0.0).astype(F32)


def mix_kernel(scal, x_ref, routes_ref, wo_ref, rt_ref, *refs):
    t = scal[2]
    att_refs, (mixed_ref, wide_ref, comb_ref) = refs[:CUBE], refs[CUBE:]
    rows = x_ref.shape[0]
    branch = jnp.zeros((rows, D), F32)
    for k in range(CUBE):
        spot = pl.ds(pl.multiple_of((t ^ k) * QH, 64), QH)
        branch = branch + dot(att_refs[k][...], wo_ref[spot, :])
    valid = row_valid(scal, rows)
    mixed = x_ref[...].astype(F32) + valid * branch
    mixed_ref[...] = mixed
    scale = lax.rsqrt(jnp.mean(mixed * mixed, axis=-1, keepdims=True) + 1e-05)
    low = (mixed * scale).astype(BF16)
    logits = dot(low, rt_ref[...])
    lane = lax.broadcasted_iota(jnp.int32, (rows, EXTRA), 1)
    expert = lane & (E - 1)
    chosen = ((expert == routes_ref[:, 0:1]) | (expert == routes_ref[:, 1:2])) & (lane < 2 * E)
    peak = jnp.max(jnp.where(chosen, logits, -3e38), axis=-1, keepdims=True)
    expo = jnp.where(chosen, jnp.exp(logits - peak), 0.0)
    comb = expo / (0.5 * jnp.sum(expo, axis=-1, keepdims=True))
    comb_ref[...] = jnp.where(lane < E, comb, 0.0)
    comb = comb * valid
    high = comb.astype(BF16)
    rest = (comb - high.astype(F32)).astype(BF16)
    wide_ref[:, :D] = low
    wide_ref[:, D:] = jnp.where(lane < E, high, rest)


def cot_kernel(ng, n_outer, scal, *refs):
    x, g = scal[0], scal[1]
    blocks, refs = refs[:10], refs[10:]
    weights, (dyg, q_ref, w_full) = refs[:n_outer], refs[n_outer:]
    cube_rows(blocks, dyg)
    outer_rows(weights, w_full, x, g, ng)
    step = dyg.shape[0] // 4

    @pl.loop(0, 4)
    def _(i):
        spot = pl.ds(pl.multiple_of(i * step, 128), step)
        q_ref[spot, :] = dot(dyg[spot, :], w_full[...])


def own_share(wide, scal):
    lane = lax.broadcasted_iota(jnp.int32, wide.shape, 1)
    expert = scal[2] // 2
    mine = (lane == expert) | (lane == expert + E)
    return jnp.sum(jnp.where(mine, wide.astype(F32), 0.0), axis=-1, keepdims=True)


def expert_kernel(ng, n_outer, scal, *refs):
    x, g = scal[0], scal[1]
    blocks, refs = refs[:10], refs[10:]
    weights, refs = refs[:n_outer], refs[n_outer:]
    q_ref, ngw, act_ref, ggu_ref, even_ref, odd_ref, w_full = refs
    cube_rows(blocks, ngw)
    outer_rows(weights, w_full, x, g, ng)
    half_rows = ngw.shape[0] // 2
    step = half_rows // 2
    expert = scal[2] // 2
    for part, out_ref in enumerate((even_ref, odd_ref)):

        @pl.loop(0, 2)
        def _(i):
            local = pl.ds(pl.multiple_of(i * step, 128), step)
            spot = pl.ds(pl.multiple_of(part * half_rows + i * step, 128), step)
            share = own_share(ngw[spot, D:], scal)
            gu = dot(ngw[spot, :D], w_full[...])
            gate, up = gu[:, :HALF], gu[:, HALF:]
            sig = 1.0 / (1.0 + jnp.exp(-gate))
            soft = gate * sig
            act = (soft * up).astype(BF16)
            act_ref[spot, :] = act
            back = q_ref[spot, :]
            dots = jnp.sum(act.astype(F32) * back, axis=-1, keepdims=True)
            back = back * share
            ggu_ref[spot, :HALF] = (back * up * (sig * (1.0 + gate * (1.0 - sig)))).astype(BF16)
            ggu_ref[spot, HALF:] = (back * soft).astype(BF16)
            out_ref[local, :D] = dot(ggu_ref[spot, :], w_full[...], NT).astype(BF16)
            high = dots.astype(BF16)
            rest = (dots - high.astype(F32)).astype(BF16)
            lane = lax.broadcasted_iota(jnp.int32, (step, EXTRA), 1)
            out_ref[local, D:] = jnp.where(
                lane == expert, high, jnp.where(lane == expert + E, rest, jnp.zeros_like(rest))
            )


def spread_kernel(ng, n_outer, scal, ngw, dyg, act_ref, ggu_ref, *refs):
    x, g = scal[0], scal[1]
    weights, (other_ref, mine_ref, even_ref, odd_ref, w_full, ca_ref) = refs[:n_outer], refs[n_outer:]
    outer_rows(weights, w_full, x, g, ng)
    rows = ngw.shape[0]
    step = rows // 4

    @pl.loop(0, 4)
    def _(i):
        spot = pl.ds(pl.multiple_of(i * step, 128), step)
        share = own_share(ngw[spot, D:], scal)
        ca_ref[spot, :] = (act_ref[spot, :].astype(F32) * share).astype(BF16)

    cut = D // 6
    for flip, out_ref in ((1, other_ref), (0, mine_ref)):

        @pl.loop(0, 3)
        def _(i):
            cols = pl.ds(pl.multiple_of((x ^ flip) * (D // 2) + i * cut, 128), cut)
            spot = pl.ds(pl.multiple_of(i * cut, 128), cut)
            out_ref[spot, : 2 * HALF] = dot(ngw[:, cols], ggu_ref[...], TN).astype(BF16)
            out_ref[spot, 2 * HALF :] = dot(dyg[:, cols], ca_ref[...], TN).astype(BF16)

    for part, out_ref in enumerate((even_ref, odd_ref)):

        @pl.loop(0, 2)
        def _(i):
            local = pl.ds(pl.multiple_of(i * step, 128), step)
            spot = pl.ds(pl.multiple_of(part * 2 * step + i * step, 128), step)
            share = own_share(ngw[spot, D:], scal)
            out_ref[local, :] = (dot(act_ref[spot, :], w_full[...], NT) * share).astype(BF16)


def pair_kernel(even_ref, odd_ref, *outs):
    rows = outs[0].shape[0]
    for p, out in enumerate(outs):
        spot = slice(p * rows, (p + 1) * rows)
        out[...] = (even_ref[spot, :].astype(F32) + odd_ref[spot, :].astype(F32)).astype(BF16)


def norm_back(grad, values, scale):
    unit = values * scale
    return scale * (grad - unit * jnp.mean(grad * unit, axis=-1, keepdims=True))


def turn_kernel(scal, a0, a1, a2, a3, mixed_ref, cot_ref, comb_ref, wo_ref, rt_ref, *refs):
    t = scal[2]
    (grad_ref, wide_ref), ga_refs = refs[:2], refs[2:]
    rows = mixed_ref.shape[0]
    total = (
        a0[...].astype(F32) + a1[...].astype(F32) + a2[...].astype(F32) + a3[...].astype(F32)
    )
    valid = row_valid(scal, rows)
    lane = lax.broadcasted_iota(jnp.int32, (rows, EXTRA), 1)
    dots = total[:, D:]
    dots = (dots + pltpu.roll(dots, EXTRA - E, 1)) * valid
    comb = comb_ref[...]
    inner = jnp.sum(comb * dots, axis=-1, keepdims=True)
    grad_logits = jnp.where(lane < E, comb * (dots - inner), 0.0).astype(BF16)
    grad_normed = total[:, :D] + dot(grad_logits, rt_ref[...], NT)
    mixed = mixed_ref[...]
    scale = lax.rsqrt(jnp.mean(mixed * mixed, axis=-1, keepdims=True) + 1e-05)
    grad_mixed = cot_ref[...].astype(F32) + norm_back(grad_normed, mixed, scale)
    grad_ref[...] = grad_mixed
    branch = (valid * grad_mixed).astype(BF16)
    wide_ref[:, :D] = branch
    wide_ref[:, D:] = grad_logits
    for k in range(CUBE):
        spot = pl.ds(pl.multiple_of((t ^ k) * QH, 64), QH)
        ga_refs[k][...] = dot(branch, wo_ref[spot, :], NT).astype(BF16)


def attend_back_kernel(slots, n_keys, scal, *refs):
    g, t = scal[1], scal[2]
    q_ref, kv_refs, refs = refs[0], refs[1 : 1 + n_keys], refs[1 + n_keys :]
    ot_ref, lse_ref, refs = refs[0], refs[1], refs[2:]
    ga_refs, refs = refs[:CUBE], refs[CUBE:]
    gq_ref, gkv_refs, (do_ref,) = refs[0], refs[1 : 1 + n_keys], refs[1 + n_keys :]
    extent = q_ref.shape[2]
    causal = causal_bias(slots, extent, t)
    blank = jnp.zeros((slots, HD), BF16)
    place = {k: p for p, k in enumerate(ORDER)}
    for m in range(MB):
        length = scal[3 + m]
        biases = [key_bias(s, slots, extent, g, t, s, length) for s in range(n_keys)]
        sums = [None] * n_keys
        for h in range(GROUP):
            for k in range(CUBE):
                part = ga_refs[k][m * slots : (m + 1) * slots, h * HD : (h + 1) * HD]
                do_ref[k * slots : (k + 1) * slots, :] = jnp.concatenate([blank, part], axis=1)
            q = q_ref[m, h]
            do = do_ref[...]
            dot_t = do.astype(F32).T[HD:, :]
            delta = jnp.sum(dot_t * ot_ref[m, h], axis=0, keepdims=True)
            lse = lse_ref[m, h : h + 1, :]
            grad_q = None
            for s in range(n_keys):
                kv = kv_refs[s][m]
                st = dot(kv, q, NT) * (0.125 * LOG2E) + biases[s]
                if s == 0:
                    st = st + causal
                pt = jnp.exp2(st - lse)
                dpt = dot(kv, do, NT)
                dst = (pt * (dpt - delta) * 0.125).astype(BF16)
                part = dot(dst, q) + dot(pt.astype(BF16), do)
                sums[s] = part if sums[s] is None else sums[s] + part
                part = dot(kv, dst, TN)
                grad_q = part if grad_q is None else grad_q + part
            gq = grad_q[:HD, :].T.astype(BF16)
            for k in range(CUBE):
                base = place[k] * MB * slots + m * slots
                gq_ref[base : base + slots, h * HD : (h + 1) * HD] = gq[k * slots : (k + 1) * slots]
        for s in range(n_keys):
            gkv_refs[s][m] = sums[s].astype(gkv_refs[s].dtype)


def close_kernel(ng, n_outer, n_keys, scal, gq_ref, own_ref, *refs):
    x, g = scal[0], scal[1]
    others, refs = refs[: n_keys - 1], refs[n_keys - 1 :]
    weights, refs = refs[:n_outer], refs[n_outer:]
    xg, even_ref, odd_ref, other_ref, mine_ref, w_full, gqkv = refs
    outer_rows(weights, w_full, x, g, ng)
    rows = xg.shape[0] // CUBE
    slots = rows // MB
    gqkv[:, :QH] = gq_ref[...]
    for p, k in enumerate(ORDER):
        for m in range(MB):
            spot = slice(k * slots, (k + 1) * slots)
            total = own_ref[m, spot, :]
            for other in others:
                total = total + other[m, spot, :].astype(F32)
            base = p * rows + m * slots
            gqkv[base : base + slots, QH:] = total.astype(BF16)
    step = 2 * rows
    for part, out_ref in enumerate((even_ref, odd_ref)):

        @pl.loop(0, 2)
        def _(i):
            local = pl.ds(pl.multiple_of(i * step, 128), step)
            spot = pl.ds(pl.multiple_of(part * 2 * step + i * step, 128), step)
            out_ref[local, :] = dot(gqkv[spot, :], w_full[...], NT).astype(BF16)

    cut = D // 6
    for flip, out_ref in ((1, other_ref), (0, mine_ref)):

        @pl.loop(0, 3)
        def _(i):
            cols = pl.ds(pl.multiple_of((x ^ flip) * (D // 2) + i * cut, 128), cut)
            spot = pl.ds(pl.multiple_of(i * cut, 128), cut)
            out_ref[spot, :] = dot(xg[:, cols], gqkv[...], TN).astype(BF16)


def out_grad_kernel(scal, *refs):
    x = scal[0]
    blocks, refs = refs[:10], refs[10:]
    att_refs, (ngw, other_ref, mine_ref, wide, att) = refs[:CUBE], refs[CUBE:]
    cube_rows(blocks, wide)
    rows = att_refs[0].shape[0]
    for p, k in enumerate(ORDER):
        att[p * rows : (p + 1) * rows, :] = att_refs[k][...]
    cut = D // 6
    for flip, out_ref in ((1, other_ref), (0, mine_ref)):

        @pl.loop(0, 3)
        def _(i):
            cols = pl.ds(pl.multiple_of((x ^ flip) * (D // 2) + i * cut, 128), cut)
            spot = pl.ds(pl.multiple_of(i * cut, 128), cut)
            out_ref[spot, :QH] = dot(wide[:, cols], att[...], TN).astype(BF16)
            out_ref[spot, QH:] = dot(ngw[:, cols], wide[:, D:], TN)[:, : 256 - QH].astype(BF16)


def output_kernel(a0, a1, a2, a3, mixed_ref, out_ref):
    total = (
        a0[...].astype(F32) + a1[...].astype(F32) + a2[...].astype(F32) + a3[...].astype(F32)
    )
    out_ref[...] = (mixed_ref[...] + total).astype(BF16)


def tokens_kernel(a0, a1, a2, a3, x_ref, grad_ref, out_ref):
    total = (
        a0[...].astype(F32) + a1[...].astype(F32) + a2[...].astype(F32) + a3[...].astype(F32)
    )
    x = x_ref[...].astype(F32)
    scale = lax.rsqrt(jnp.mean(x * x, axis=-1, keepdims=True) + 1e-05)
    out_ref[...] = (grad_ref[...] + norm_back(total, x, scale)).astype(BF16)


def pair_sums(links, even, odd):
    rows = even.shape[0] // 4
    outs = [shape((rows, even.shape[1]))] * 4
    sums = kernel_call(pair_kernel, outs, [even, links.cube(odd, 1)], scalars=False)
    return [sums[0]] + [links.cube(part, bits) for part, bits in zip(sums[1:], ORDER[1:4])]


def body(
    tokens,
    lengths,
    routes,
    cotangent,
    attn_gain,
    qkv_weight,
    out_weight,
    moe_gain,
    router,
    gateup_weight,
    down_weight,
):
    nx, nc = lax.axis_size("dp"), lax.axis_size("ctx")
    links = Links(nx, nc)
    ng = links.ng
    n_outer = nx * ng
    x = lax.axis_index("dp")
    ctx = lax.axis_index("ctx")
    g, t = ctx // CUBE, ctx % CUBE
    slots = tokens.shape[2]
    rows = MB * slots
    extent = CUBE * slots
    scal = jnp.stack([x, g, t, lengths[0, 0], lengths[1, 0]]).astype(jnp.int32)
    wr = attn_gain.shape[0]
    out_rows = CUBE * rows

    tok = tokens.reshape(rows, D)
    cot = cotangent.reshape(rows, D)
    tok_f = tok.astype(F32)
    first = lax.rsqrt(jnp.mean(tok_f * tok_f, axis=-1, keepdims=True) + 1e-05)
    unit = (tok_f * first).astype(BF16)

    gain1 = attn_gain.astype(F32)[:, None]
    gain2 = moe_gain.astype(F32)[:, None]
    wq = (qkv_weight.astype(F32) * gain1).astype(BF16)
    wq_parts = jnp.concatenate(
        [
            wq[:, :QW].reshape(wr, CUBE, QH),
            wq[:, QW : QW + KW].reshape(wr, CUBE, HD),
            wq[:, QW + KW :].reshape(wr, CUBE, HD),
        ],
        axis=2,
    ).transpose(1, 0, 2)
    wq_blocks = links.outer_gather(links.swap(wq_parts).reshape(CUBE * wr, SHARD))
    unit_blocks = links.cube_gather(unit)

    gu = (gateup_weight.astype(F32) * gain2[None]).astype(BF16)
    gu_parts = (
        gu.reshape(E, wr, 2, 2, HALF).transpose(0, 3, 1, 2, 4).reshape(CUBE, wr, 2 * HALF)
    )
    dn_parts = down_weight.reshape(CUBE, HALF, wr).transpose(0, 2, 1)
    gu_blocks = links.outer_gather(links.swap(gu_parts).reshape(CUBE * wr, 2 * HALF))
    dn_blocks = links.outer_gather(links.swap(dn_parts).reshape(CUBE * wr, HALF))

    rt_low = (router.astype(F32) * gain2).astype(BF16)
    wo_t = jnp.concatenate(
        [out_weight.T, rt_low, rt_low, jnp.zeros((wr, EXTRA - 2 * E), BF16)], axis=1
    )
    wo_all = lax.all_gather(wo_t, AXES, axis=0, tiled=True)
    wo = wo_all[:, :QW].T
    rt = wo_all[:, QW:]

    xg, q, kv = kernel_call(
        functools.partial(qkv_kernel, ng, n_outer),
        [
            shape((out_rows, D)),
            shape((MB, GROUP, extent, 2 * HD)),
            shape((MB, extent, 2 * HD)),
        ],
        [scal] + unit_blocks + wq_blocks,
        [pltpu.VMEM((D, SHARD), BF16)],
        flops=2 * out_rows * D * SHARD,
    )
    kvs = [kv] + [links.climb(kv, step) for step in range(1, ng)]
    attended = kernel_call(
        functools.partial(attend_kernel, slots),
        [shape((rows, QH))] * CUBE
        + [shape((MB, GROUP, HD, extent), F32), shape((MB, GROUP, extent), F32)],
        [scal, q] + kvs,
        flops=8 * MB * GROUP * extent * extent * 2 * HD * ng,
    )
    att_blocks, (ot, lse) = attended[:CUBE], attended[CUBE:]
    att_own = [att_blocks[0]] + [links.cube(att_blocks[k], k) for k in range(1, CUBE)]
    mixed, wide, comb = kernel_call(
        mix_kernel,
        [shape((rows, D), F32), shape((rows, WIDE)), shape((rows, EXTRA), F32)],
        [scal, tok, routes.reshape(rows, 2), wo, rt] + att_own,
        flops=2 * rows * D * QW,
    )
    cot_blocks = links.cube_gather(cot)
    dyg, back = kernel_call(
        functools.partial(cot_kernel, ng, n_outer),
        [shape((out_rows, D)), shape((out_rows, HALF), F32)],
        [scal] + cot_blocks + dn_blocks,
        [pltpu.VMEM((D, HALF), BF16)],
        flops=2 * out_rows * D * HALF,
    )
    ngw, act, ggu, even, odd = kernel_call(
        functools.partial(expert_kernel, ng, n_outer),
        [
            shape((out_rows, WIDE)),
            shape((out_rows, HALF)),
            shape((out_rows, 2 * HALF)),
            shape((out_rows // 2, WIDE)),
            shape((out_rows // 2, WIDE)),
        ],
        [scal] + links.cube_gather(wide) + gu_blocks + [back],
        [pltpu.VMEM((D, 2 * HALF), BF16)],
        flops=8 * out_rows * D * HALF,
    )
    grad_sums = pair_sums(links, even, odd)
    turned = kernel_call(
        turn_kernel,
        [shape((rows, D), F32), shape((rows, WIDE))] + [shape((rows, QH))] * CUBE,
        [scal] + grad_sums + [mixed, cot, comb, wo, rt],
        flops=2 * rows * D * QW,
    )
    grad_mixed, grad_wide, ga_blocks = turned[0], turned[1], turned[2:]
    ga_heads = [ga_blocks[0]] + [links.cube(ga_blocks[k], k) for k in range(1, CUBE)]

    moe_other, moe_mine, out_even, out_odd = kernel_call(
        functools.partial(spread_kernel, ng, n_outer),
        [
            shape((D // 2, 3 * HALF)),
            shape((D // 2, 3 * HALF)),
            shape((out_rows // 2, D)),
            shape((out_rows // 2, D)),
        ],
        [scal, ngw, dyg, act, ggu] + dn_blocks,
        [pltpu.VMEM((D, HALF), BF16), pltpu.VMEM((out_rows, HALF), BF16)],
        flops=8 * out_rows * D * HALF,
    )
    moe_sum = links.outer_scatter([moe_mine, moe_other], x, g)
    moe_grad = links.swap(moe_sum.astype(BF16).reshape(CUBE, wr, 3 * HALF))

    grads = kernel_call(
        functools.partial(attend_back_kernel, slots, ng),
        [shape((out_rows, QH)), shape((MB, extent, 2 * HD), F32)]
        + [shape((MB, extent, 2 * HD))] * (ng - 1),
        [scal, q] + kvs + [ot, lse] + ga_heads,
        [pltpu.VMEM((extent, 2 * HD), BF16)],
        flops=20 * MB * GROUP * extent * extent * 2 * HD * ng,
    )
    gkv_others = [links.climb(grads[1 + step], -step) for step in range(1, ng)]
    even, odd, qkv_other, qkv_mine = kernel_call(
        functools.partial(close_kernel, ng, n_outer, ng),
        [
            shape((out_rows // 2, D)),
            shape((out_rows // 2, D)),
            shape((D // 2, SHARD)),
            shape((D // 2, SHARD)),
        ],
        [scal, grads[0], grads[1]] + gkv_others + wq_blocks + [xg],
        [pltpu.VMEM((D, SHARD), BF16), pltpu.VMEM((out_rows, SHARD), BF16)],
        flops=4 * out_rows * D * SHARD,
    )
    qkv_sum = links.outer_scatter([qkv_mine, qkv_other], x, g)
    qkv_grad = links.swap(qkv_sum.astype(BF16).reshape(CUBE, wr, SHARD)).astype(F32)
    token_sums = pair_sums(links, even, odd)
    grad_tokens = kernel_call(
        tokens_kernel, [shape((rows, D))], token_sums + [tok, grad_mixed], scalars=False
    )[0]

    wo_other, wo_mine = kernel_call(
        out_grad_kernel,
        [shape((D // 2, 256)), shape((D // 2, 256))],
        [scal] + links.cube_gather(grad_wide) + list(att_blocks) + [ngw],
        [pltpu.VMEM((out_rows, WIDE), BF16), pltpu.VMEM((out_rows, QH), BF16)],
        flops=2 * out_rows * D * 256,
    )
    wo_sum = links.outer_scatter([wo_mine, wo_other], x, g)
    wo_grad = links.swap(wo_sum.astype(BF16).reshape(CUBE, wr, 256)).astype(F32)

    output = kernel_call(
        output_kernel,
        [shape((rows, D))],
        pair_sums(links, out_even, out_odd) + [mixed],
        scalars=False,
    )[0]

    qkv_unit = jnp.concatenate(
        [
            qkv_grad[:, :, :QH].transpose(1, 0, 2).reshape(wr, QW),
            qkv_grad[:, :, QH : QH + HD].transpose(1, 0, 2).reshape(wr, KW),
            qkv_grad[:, :, QH + HD :].transpose(1, 0, 2).reshape(wr, KW),
        ],
        axis=1,
    )
    grad_attn_gain = jnp.sum(qkv_unit * qkv_weight.astype(F32), axis=1)
    grad_out = wo_grad[:, :, :QH].transpose(0, 2, 1).reshape(QW, wr)
    router_unit = wo_grad[0, :, QH : QH + E]
    moe_f = moe_grad.astype(F32)
    gu_unit = (
        moe_f[:, :, : 2 * HALF]
        .reshape(E, 2, wr, 2, HALF)
        .transpose(0, 2, 3, 1, 4)
        .reshape(E, wr, 2 * FF)
    )
    grad_down = moe_f[:, :, 2 * HALF :].transpose(0, 2, 1).reshape(E, FF, wr)
    grad_moe_gain = jnp.sum(gu_unit * gateup_weight.astype(F32), axis=(0, 2)) + jnp.sum(
        router_unit * router.astype(F32), axis=1
    )
    return (
        output.reshape(MB, 1, slots, D),
        grad_tokens.reshape(MB, 1, slots, D),
        grad_attn_gain,
        qkv_unit * gain1,
        grad_out,
        grad_moe_gain,
        router_unit * gain2,
        gu_unit * gain2[None],
        grad_down,
    )


def solution(mesh):
    in_specs = (
        P(None, "dp", "ctx", None),
        P(None, "dp"),
        P(None, "dp", "ctx", None),
        P(None, "dp", "ctx", None),
        P(("dp", "ctx")),
        P(("dp", "ctx"), None),
        P(None, ("dp", "ctx")),
        P(("dp", "ctx")),
        P(("dp", "ctx"), None),
        P(None, ("dp", "ctx"), None),
        P(None, None, ("dp", "ctx")),
    )
    out_specs = (
        P(None, "dp", "ctx", None),
        P(None, "dp", "ctx", None),
        P(("dp", "ctx")),
        P(("dp", "ctx"), None),
        P(None, ("dp", "ctx")),
        P(("dp", "ctx")),
        P(("dp", "ctx"), None),
        P(None, ("dp", "ctx"), None),
        P(None, None, ("dp", "ctx")),
    )
    return jax.shard_map(body, mesh=mesh, in_specs=in_specs, out_specs=out_specs, check_vma=False)
```

```python
import functools
import math

import jax
import jax.numpy as jnp
from jax import lax
from jax.experimental import pallas as pl
from jax.experimental.pallas import tpu as pltpu
from jax.sharding import PartitionSpec as P

D = 1536
H = 24
KVH = 8
HD = 64
FF = 1024
E = 4
MB = 2
QW = 1536
KW = 512
CUBE = 8
GROUP = H // KVH
HALF = FF // 2
QH = GROUP * HD
SHARD = QH + 2 * HD
SLAB = 384
OUT_SLAB = 256
PAIR = 2 * QH
EXTRA = 128
WIDE = D + EXTRA
ORDER = (0, 4, 2, 6, 1, 5, 3, 7)
LOG2E = 1.4426950408889634
F32 = jnp.float32
BF16 = jnp.bfloat16
NN = (((1,), (0,)), ((), ()))
NT = (((1,), (1,)), ((), ()))
TN = (((0,), (0,)), ((), ()))
AXES = ("dp", "ctx")


def dot(left, right, dims=NN):
    return lax.dot_general(left, right, dims, preferred_element_type=F32)


class Kernels:
    def __init__(self, lengths):
        self.lengths = lengths

    def __call__(self, kernel, outs, ins, far=(), scratch=(), room=0, after=(), busy=0):
        ins, far, after = list(ins), list(far), list(after)
        n_in, n_after = 1 + len(ins) + len(far), len(after)
        vmem = pl.BlockSpec(memory_space=pltpu.VMEM)
        anywhere = pl.BlockSpec(memory_space=pl.ANY)

        def run(lengths, *refs):
            ctx = lax.axis_index("ctx")
            scal = [lax.axis_index("dp"), ctx >> 3, ctx & 7, lengths[0, 0], lengths[1, 0]]
            kernel(scal, *refs[: n_in - 1], *refs[n_in - 1 + n_after :])

        moved = sum(math.prod(a.shape) * a.dtype.itemsize for a in ins + list(outs))
        held = sum(2 * math.prod(s.shape) for s in scratch if hasattr(s, "shape"))
        grant = int(1.1 * moved) + held + (room + 4) * 1024 * 1024
        results = pl.pallas_call(
            run,
            out_shape=list(outs),
            in_specs=[pl.BlockSpec(memory_space=pltpu.SMEM)]
            + [vmem] * len(ins)
            + [anywhere] * (len(far) + n_after),
            out_specs=[vmem] * len(outs),
            scratch_shapes=list(scratch),
            compiler_params=pltpu.CompilerParams(vmem_limit_bytes=min(grant, 56 * 1024 * 1024)),
            cost_estimate=pl.CostEstimate(
                flops=1000 + busy * 10**9, bytes_accessed=1000, transcendentals=0
            ),
        )(
            self.lengths,
            *ins,
            *[pltpu.with_memory_space_constraint(value, pltpu.HBM) for value in far],
            *after,
        )
        return results


def sems(count):
    return pltpu.SemaphoreType.DMA((count,))


def shape(dims, dtype=BF16):
    return jax.ShapeDtypeStruct(dims, dtype)


class Links:
    def __init__(self, nx, nc):
        self.nx, self.nc, self.ng = nx, nc, nc // CUBE

    def _pairs(self, move):
        pairs = []
        for x in range(self.nx):
            for g in range(self.ng):
                for t in range(CUBE):
                    goal = move(x, g, t)
                    if goal is not None:
                        gx, gg, gt = goal
                        pairs.append((x * self.nc + g * CUBE + t, gx * self.nc + gg * CUBE + gt))
        return pairs

    def cube(self, value, bits):
        return lax.ppermute(value, AXES, self._pairs(lambda x, g, t: (x, g, t ^ bits)))

    def outer(self, value, dx, dg):
        return lax.ppermute(value, AXES, self._pairs(lambda x, g, t: (x ^ dx, g ^ dg, t)))

    def climb(self, value, step):
        def move(x, g, t):
            return (x, g + step, t) if 0 <= g + step < self.ng else None

        return lax.ppermute(value, AXES, self._pairs(move))

    def cubes(self):
        return [
            [x * self.nc + g * CUBE + t for t in range(CUBE)]
            for x in range(self.nx)
            for g in range(self.ng)
        ]

    def swap(self, value):
        return lax.all_to_all(
            value, AXES, split_axis=0, concat_axis=0, tiled=True, axis_index_groups=self.cubes()
        )

    def swap_all(self, value):
        return lax.all_to_all(value, AXES, split_axis=0, concat_axis=0, tiled=True)

    def near(self, rows):
        return [self.cube(rows, bits) for bits in ORDER[1:4]]

    def core(self, rows):
        return self.cube(rows, 1)

    def cores(self):
        return [list(range(core, self.nx * self.nc, 2)) for core in range(2)]

    def outers(self):
        return [
            [x * self.nc + g * CUBE + t for x in range(self.nx) for g in range(self.ng)]
            for t in range(CUBE)
        ]

    def outer_direct(self, rows):
        return [rows] + [
            self.outer(rows, dx, dg)
            for dx in range(self.nx)
            for dg in range(self.ng)
            if dx or dg
        ]


def fence(*values):
    return lax.optimization_barrier(values)


def stack_copies(refs, out, sem):
    rows = refs[0].shape[0]
    return [
        pltpu.make_async_copy(ref, out.at[pl.ds(n * rows, rows)], sem.at[n])
        for n, ref in enumerate(refs)
    ]


def outer_copies(refs, out, sem, scal, ng):
    rows = refs[0].shape[0]
    copies = []
    for j, ref in enumerate(refs):
        place = (scal[0] ^ (j // ng)) * ng + (scal[1] ^ (j % ng))
        spot = pl.ds(pl.multiple_of(place * rows, 16), rows)
        copies.append(pltpu.make_async_copy(ref, out.at[spot], sem.at[j]))
    return copies


def start_all(copies):
    for copy in copies:
        copy.start()


def wait_all(copies):
    for copy in copies:
        copy.wait()


def prep_kernel(scal, w_ref, gain_ref, tok_ref, routes_ref, out_ref, tok_out):
    wr = w_ref.shape[0]
    fill = column(gain_ref, SLAB - SHARD).astype(BF16)
    for k in range(CUBE):
        out_ref[k] = jnp.concatenate(
            [
                w_ref[:, k * QH : (k + 1) * QH],
                w_ref[:, QW + k * HD : QW + (k + 1) * HD],
                w_ref[:, QW + KW + k * HD : QW + KW + (k + 1) * HD],
                fill,
            ],
            axis=1,
        )
    rows = tok_ref.shape[0]
    tok_out[:, :D] = tok_ref[...]
    lane = lax.broadcasted_iota(jnp.int32, (rows, EXTRA), 1)
    names = jnp.where(lane == 0, routes_ref[:, 0:1], routes_ref[:, 1:2])
    tok_out[:, D:] = names.astype(F32).astype(BF16)


def column(row_ref, width):
    return jnp.broadcast_to(row_ref[...].astype(F32), (width, row_ref.shape[1])).T


def as_row(values):
    return jnp.broadcast_to(values, (values.shape[0], EXTRA)).T[0:1, :]


def prep_rest_kernel(scal, gu_ref, dn_ref, wo_ref, rt_ref, gain_ref, moe_out, wo_out):
    for k in range(CUBE):
        e, h = k // 2, k % 2
        moe_out[k, :, :HALF] = gu_ref[e, :, h * HALF : (h + 1) * HALF]
        moe_out[k, :, HALF : 2 * HALF] = gu_ref[e, :, FF + h * HALF : FF + (h + 1) * HALF]
        moe_out[k, :, 2 * HALF :] = dn_ref[e, :, h * HALF : (h + 1) * HALF]
    wr = wo_ref.shape[0]
    rt = rt_ref[...].astype(F32)
    rows = jnp.concatenate(
        [rt, rt, gain_ref[...].astype(F32), jnp.zeros((EXTRA - 2 * E - 1, wr), F32)], axis=0
    )
    wo_out[:, :QW] = wo_ref[...]
    wo_out[:, QW:] = rows.T.astype(BF16)


def split_kernel(scal, both_ref, gu_ref, dn_ref):
    gu_ref[...] = both_ref[:, : 2 * HALF]
    dn_ref[...] = both_ref[:, 2 * HALF :]


def pack_kernel(scal, *refs):
    rows = refs[0].shape[0]
    for n, ref in enumerate(refs[:-1]):
        refs[-1][n * rows : (n + 1) * rows, :] = ref[...]


def qkv_kernel(ng, n_outer, scal, even_ref, odd_ref, *refs):
    t = scal[2]
    weights, (xg, q_out, kv_out, gain_ref, w_ref, sem) = refs[:n_outer], refs[n_outer:]
    copies = outer_copies(weights, w_ref, sem, scal, ng)
    start_all(copies)
    wait_all(copies)
    rows = even_ref.shape[0] // 4
    slots = rows // MB
    blank = jnp.zeros((slots, HD), BF16)
    gain = w_ref[:, 256:].astype(F32).T[SHARD - 256 : SHARD - 248, :]
    gain_ref[...] = gain
    gain = gain[0:1]
    for p, k in enumerate(ORDER):
        source = even_ref if p < 4 else odd_ref
        values = source[(p % 4) * rows : (p % 4 + 1) * rows, :D].astype(F32)
        scale = lax.rsqrt(jnp.mean(values * values, axis=-1, keepdims=True) + 1e-05)
        packed = (values * scale * gain).astype(BF16)
        xg[p * rows : (p + 1) * rows, :] = packed
        y = dot(packed, w_ref[...]).astype(BF16)
        for m in range(MB):
            part = y[m * slots : (m + 1) * slots]
            spot = pl.ds(pl.multiple_of((t ^ k) * slots, 64), slots)
            for h in range(GROUP):
                q_out[m, h, spot, :] = jnp.concatenate(
                    [part[:, h * HD : (h + 1) * HD], blank], axis=1
                )
            kv_out[m, spot, :] = part[:, QH:SHARD]


def key_bias(extent, g, step, length):
    local = lax.broadcasted_iota(jnp.int32, (extent, 1), 0)
    seen = ((g - step) * extent + local < length) & (g >= step)
    return jnp.where(seen, 0.0, -1e30).astype(F32)


def causal_bias(extent):
    keys = lax.broadcasted_iota(jnp.int32, (extent, extent), 0)
    rows = lax.broadcasted_iota(jnp.int32, (extent, extent), 1)
    return jnp.where(keys <= rows, 0.0, -1e30).astype(F32)


def attend_kernel(slots, scal, *refs):
    g = scal[1]
    n_keys = len(refs) - 4
    q_ref, kv_refs, (att_ref, ot_ref, lse_ref) = refs[0], refs[1 : 1 + n_keys], refs[1 + n_keys :]
    extent = q_ref.shape[2]
    causal = causal_bias(extent)
    for m in range(MB):
        length = scal[3 + m]
        biases = [key_bias(extent, g, s, length) for s in range(n_keys)]
        for h in range(GROUP):
            q = q_ref[m, h]
            top = total = acc = None
            for s in range(n_keys):
                kv = kv_refs[s][m]
                st = dot(kv, q, NT) * (0.125 * LOG2E) + biases[s]
                if s == 0:
                    st = st + causal
                peak = jnp.max(st, axis=0, keepdims=True)
                if s == 0:
                    pt = jnp.exp2(st - peak)
                    top, total = peak, jnp.sum(pt, axis=0, keepdims=True)
                    acc = dot(kv, pt.astype(BF16), TN)
                else:
                    fresh = jnp.maximum(top, peak)
                    scale = jnp.exp2(top - fresh)
                    pt = jnp.exp2(st - fresh)
                    total = total * scale + jnp.sum(pt, axis=0, keepdims=True)
                    acc = acc * scale + dot(kv, pt.astype(BF16), TN)
                    top = fresh
            ot = acc[HD:, :] / total
            ot_ref[m, h] = ot
            lse_ref[m, h : h + 1, :] = top + jnp.log2(total)
            o = ot.T.astype(BF16)
            for k in range(CUBE):
                place = (k // 4) * QH + h * HD
                base = (k % 4) * MB * slots + m * slots
                att_ref[base : base + slots, place : place + HD] = o[k * slots : (k + 1) * slots]


def row_valid(scal, rows):
    slots = rows // MB
    spot = lax.broadcasted_iota(jnp.int32, (rows, 1), 0)
    place = (scal[1] * CUBE + scal[2]) * slots
    length = jnp.where(spot < slots, scal[3], scal[4])
    inner = jnp.where(spot < slots, spot, spot - slots)
    return jnp.where(place + inner < length, 1.0, 0.0).astype(F32)


def gain_row(rest):
    return rest.astype(F32).T[2 * E : 2 * E + 1, :]


def att_block(ref, base, rows, j):
    spot = pl.ds(pl.multiple_of(base + (j & 3) * rows, 16), rows)
    both = ref[spot, :]
    return jnp.where(j >= 4, both[:, QH:], both[:, :QH])


def mix_kernel(scal, even_ref, odd_ref, toke_ref, toko_ref, wo_ref, *refs):
    t = scal[2]
    nge, ngo, mixed_ref, comb_ref, att = refs
    rows = mixed_ref.shape[0]
    slots = rows // MB
    for q in range(4):
        head = t ^ ORDER[q]
        lanes = pl.ds(pl.multiple_of((head >> 1) * PAIR, 128), PAIR)
        for p, k in enumerate(ORDER):
            low = att_block(even_ref, q * 4 * rows, rows, t ^ k)
            high = att_block(odd_ref, q * 4 * rows, rows, t ^ k)
            flip = (head & 1) == 1
            att[p * rows : (p + 1) * rows, lanes] = jnp.concatenate(
                [jnp.where(flip, high, low), jnp.where(flip, low, high)], axis=1
            )
    rest = wo_ref[:, QW:]
    gain = gain_row(rest)
    lane = lax.broadcasted_iota(jnp.int32, (2 * rows, EXTRA), 1)
    spot = lax.broadcasted_iota(jnp.int32, (2 * rows, 1), 0)
    inner = spot & (rows - 1)
    second = inner >= slots
    length = jnp.where(second, scal[4], scal[3])
    slot = jnp.where(second, inner - slots, inner)
    for p in range(0, CUBE, 2):
        tok_ref, out_ref = (toke_ref, nge) if p < 4 else (toko_ref, ngo)
        local = slice((p % 4) * rows, (p % 4 + 2) * rows)
        owner = jnp.where(spot < rows, t ^ ORDER[p], t ^ ORDER[p + 1])
        place = (scal[1] * CUBE + owner) * slots + slot
        valid = jnp.where(place < length, 1.0, 0.0).astype(F32)
        branch = dot(att[p * rows : (p + 2) * rows, :], wo_ref[:, :QW], NT)
        mixed = tok_ref[local, :D].astype(F32) + valid * branch
        scale = lax.rsqrt(jnp.mean(mixed * mixed, axis=-1, keepdims=True) + 1e-05)
        low = (mixed * scale * gain).astype(BF16)
        logits = dot(low, rest)
        names = tok_ref[local, D:].astype(F32)
        expert = (lane & (E - 1)).astype(F32)
        chosen = ((expert == names[:, 0:1]) | (expert == names[:, 1:2])) & (lane < 2 * E)
        peak = jnp.max(jnp.where(chosen, logits, -3e38), axis=-1, keepdims=True)
        expo = jnp.where(chosen, jnp.exp(logits - peak), 0.0)
        comb = expo / (0.5 * jnp.sum(expo, axis=-1, keepdims=True))
        if p == 0:
            mixed_ref[...] = mixed[:rows]
            comb_ref[...] = jnp.where(lane < E, comb, 0.0)[:rows]
        comb = comb * valid
        high = comb.astype(BF16)
        tail = (comb - high.astype(F32)).astype(BF16)
        out_ref[local, :D] = low
        out_ref[local, D:] = jnp.where(lane < E, high, tail)


def row_valid(scal, rows):
    slots = rows // MB
    spot = lax.broadcasted_iota(jnp.int32, (rows, 1), 0)
    place = (scal[1] * CUBE + scal[2]) * slots
    length = jnp.where(spot < slots, scal[3], scal[4])
    inner = jnp.where(spot < slots, spot, spot - slots)
    return jnp.where(place + inner < length, 1.0, 0.0).astype(F32)


def cot_kernel(ng, n_outer, scal, even_ref, odd_ref, *refs):
    dn_blocks, (q_ref, w_dn, sem) = refs[:n_outer], refs[n_outer:]
    copies = outer_copies(dn_blocks, w_dn, sem, scal, ng)
    start_all(copies)
    wait_all(copies)
    step = even_ref.shape[0] // 2
    for part, source in enumerate((even_ref, odd_ref)):

        @pl.loop(0, 2)
        def _(i):
            local = pl.ds(pl.multiple_of(i * step, 128), step)
            spot = pl.ds(pl.multiple_of((2 * part + i) * step, 128), step)
            q_ref[spot, :] = dot(source[local, :], w_dn[...])


def own_share(wide, scal):
    lane = lax.broadcasted_iota(jnp.int32, wide.shape, 1)
    expert = scal[2] // 2
    mine = (lane == expert) | (lane == expert + E)
    return jnp.sum(jnp.where(mine, wide.astype(F32), 0.0), axis=-1, keepdims=True)


def expert_kernel(base, ng, n_outer, scal, ngw, q_ref, *refs):
    if base:
        blocks, (act_ref, ggu_ref, out_ref, w_ref, sem) = refs[:n_outer], refs[n_outer:]
        copies = outer_copies(blocks, w_ref, sem, scal, ng)
        start_all(copies)
        wait_all(copies)
    else:
        w_ref, act_ref, ggu_ref, out_ref = refs
    step = ngw.shape[0] // 2
    expert = scal[2] // 2

    @pl.loop(0, 2)
    def _(i):
        spot = pl.ds(pl.multiple_of(i * step, 128), step)
        share = own_share(ngw[spot, D:], scal)
        gu = dot(ngw[spot, :D], w_ref[...])
        gate, up = gu[:, :HALF], gu[:, HALF:]
        sig = 1.0 / (1.0 + jnp.exp(-gate))
        soft = gate * sig
        act = (soft * up).astype(BF16)
        act_ref[spot, :] = act
        back = q_ref[pl.ds(pl.multiple_of(base + i * step, 128), step), :]
        dots = jnp.sum(act.astype(F32) * back, axis=-1, keepdims=True)
        back = back * share
        ggu_ref[spot, :HALF] = (back * up * (sig * (1.0 + gate * (1.0 - sig)))).astype(BF16)
        ggu_ref[spot, HALF:] = (back * soft).astype(BF16)
        out_ref[spot, :D] = dot(ggu_ref[spot, :], w_ref[...], NT).astype(BF16)
        high = dots.astype(BF16)
        rest = (dots - high.astype(F32)).astype(BF16)
        lane = lax.broadcasted_iota(jnp.int32, (step, EXTRA), 1)
        out_ref[spot, D:] = jnp.where(
            lane == expert, high, jnp.where(lane == expert + E, rest, jnp.zeros_like(rest))
        )


def expert_grad_kernel(
    scal, dye, dyo, nge, ngo, acte, acto, ggue, gguo, gu_other, dn_other, gu_mine, dn_mine, cae, cao
):
    for wide, act, out in ((nge, acte, cae), (ngo, acto, cao)):
        out[...] = (act[...].astype(F32) * own_share(wide[:, D:], scal)).astype(BF16)
    cut = D // 6
    for flip, gu_ref, dn_ref in ((1, gu_other, dn_other), (0, gu_mine, dn_mine)):

        @pl.loop(0, 3)
        def _(i):
            cols = pl.ds(pl.multiple_of((scal[0] ^ flip) * (D // 2) + i * cut, 128), cut)
            spot = pl.ds(pl.multiple_of(i * cut, 128), cut)
            total = dot(nge[:, cols], ggue[...], TN) + dot(ngo[:, cols], gguo[...], TN)
            gu_ref[spot, :] = total.astype(BF16)
            total = dot(dye[:, cols], cae[...], TN) + dot(dyo[:, cols], cao[...], TN)
            dn_ref[spot, :] = total.astype(BF16)


def expert_out_kernel(scal, w_ref, nge, ngo, acte, acto, even_ref, odd_ref):
    step = acte.shape[0] // 2
    for wide, act, out_ref in ((nge, acte, even_ref), (ngo, acto, odd_ref)):

        @pl.loop(0, 2)
        def _(i):
            spot = pl.ds(pl.multiple_of(i * step, 128), step)
            share = own_share(wide[spot, D:], scal)
            out_ref[spot, :] = (dot(act[spot, :], w_ref[...], NT) * share).astype(BF16)


def fold_kernel(ng, scal, mine_ref, got_ref, *refs):
    rows = mine_ref.shape[0] // ng
    for dg, out in enumerate(refs):
        spot = pl.ds(pl.multiple_of((scal[1] ^ dg) * rows, 16), rows)
        total = mine_ref[spot, :].astype(F32) + got_ref[spot, :].astype(F32)
        out[...] = total.astype(out.dtype)


def fold_last_kernel(n_in, scal, *refs):
    base = 0
    for ins in (refs[:n_in], refs[n_in:-1]):
        total = ins[0][...]
        for ref in ins[1:]:
            total = total + ref[...].astype(F32)
        refs[-1][:, base : base + total.shape[1]] = total.astype(BF16)
        base += total.shape[1]


def fold_parts_kernel(n_in, scal, *refs):
    ins, outs = refs[:n_in], refs[n_in:]
    wr = outs[0].shape[0]
    for j in range(CUBE):
        spot = slice(j * wr, (j + 1) * wr)
        total = ins[0][spot, :]
        for ref in ins[1:]:
            total = total + ref[spot, :].astype(F32)
        outs[-1][j] = total.astype(BF16)
    for k, out in enumerate(outs[:-1]):
        out[...] = outs[-1][scal[2] ^ k]


def pair_kernel(scal, even_ref, odd_ref, *outs):
    rows = outs[0].shape[0]
    for p, out in enumerate(outs):
        spot = slice(p * rows, (p + 1) * rows)
        out[...] = (even_ref[spot, :].astype(F32) + odd_ref[spot, :].astype(F32)).astype(BF16)


def norm_back(grad, values, scale):
    unit = values * scale
    return scale * (grad - unit * jnp.mean(grad * unit, axis=-1, keepdims=True))


def turn_kernel(scal, a0, a1, a2, a3, mixed_ref, cot_ref, comb_ref, wo_ref, grad_ref, wide_ref):
    rest = wo_ref[:, QW:]
    rows = mixed_ref.shape[0]
    total = (
        a0[...].astype(F32) + a1[...].astype(F32) + a2[...].astype(F32) + a3[...].astype(F32)
    )
    valid = row_valid(scal, rows)
    lane = lax.broadcasted_iota(jnp.int32, (rows, EXTRA), 1)
    dots = total[:, D:]
    dots = (dots + pltpu.roll(dots, EXTRA - E, 1)) * valid
    comb = comb_ref[...]
    inner = jnp.sum(comb * dots, axis=-1, keepdims=True)
    grad_logits = jnp.where(lane < E, comb * (dots - inner), 0.0).astype(BF16)
    grad_normed = (total[:, :D] + dot(grad_logits, rest, NT)) * gain_row(rest)
    mixed = mixed_ref[...]
    scale = lax.rsqrt(jnp.mean(mixed * mixed, axis=-1, keepdims=True) + 1e-05)
    grad_mixed = cot_ref[...].astype(F32) + norm_back(grad_normed, mixed, scale)
    grad_ref[...] = grad_mixed
    branch = (valid * grad_mixed).astype(BF16)
    wide_ref[:, :D] = branch
    wide_ref[:, D:] = grad_logits


def grad_rows_kernel(scal, w_ref, even_ref, odd_ref, ga_ref):
    t = scal[2]
    rows = ga_ref.shape[1]
    window = w_ref[:, pl.ds(pl.multiple_of(((3 * t) >> 1) * 128, 128), 256)]
    weight = jnp.where((t & 1) == 1, window[:, HD:], window[:, :QH])
    for part, wide in enumerate((even_ref, odd_ref)):
        for n in range(2):
            spot = slice(2 * n * rows, 2 * (n + 1) * rows)
            grad = dot(wide[spot, :D], weight).astype(BF16)
            for i in range(2):
                ga_ref[t ^ ORDER[4 * part + 2 * n + i]] = grad[i * rows : (i + 1) * rows]


def attend_back_kernel(slots, n_keys, scal, *refs):
    g = scal[1]
    q_ref, kv_refs, refs = refs[0], refs[1 : 1 + n_keys], refs[1 + n_keys :]
    ot_ref, lse_ref, ga_ref, gq_ref, refs = refs[0], refs[1], refs[2], refs[3], refs[4:]
    gkv_refs, (do_ref,) = refs[:n_keys], refs[n_keys:]
    extent = q_ref.shape[2]
    causal = causal_bias(extent)
    blank = jnp.zeros((slots, HD), BF16)
    for m in range(MB):
        length = scal[3 + m]
        biases = [key_bias(extent, g, s, length) for s in range(n_keys)]
        sums = [None] * n_keys
        for h in range(GROUP):
            for k in range(CUBE):
                part = ga_ref[k, m * slots : (m + 1) * slots, h * HD : (h + 1) * HD]
                do_ref[k * slots : (k + 1) * slots, :] = jnp.concatenate([blank, part], axis=1)
            q = q_ref[m, h]
            do = do_ref[...]
            dot_t = do.astype(F32).T[HD:, :]
            delta = jnp.sum(dot_t * ot_ref[m, h], axis=0, keepdims=True)
            lse = lse_ref[m, h : h + 1, :]
            grad_q = None
            for s in range(n_keys):
                kv = kv_refs[s][m]
                st = dot(kv, q, NT) * (0.125 * LOG2E) + biases[s]
                if s == 0:
                    st = st + causal
                pt = jnp.exp2(st - lse)
                dpt = dot(kv, do, NT)
                dst = (pt * (dpt - delta) * 0.125).astype(BF16)
                part = dot(dst, q) + dot(pt.astype(BF16), do)
                sums[s] = part if sums[s] is None else sums[s] + part
                part = dot(kv, dst, TN)
                grad_q = part if grad_q is None else grad_q + part
            gq = grad_q[:HD, :].T.astype(BF16)
            for k in range(CUBE):
                gq_ref[k, m * slots : (m + 1) * slots, h * HD : (h + 1) * HD] = gq[
                    k * slots : (k + 1) * slots
                ]
        for s in range(n_keys):
            gkv_refs[s][m] = sums[s].astype(gkv_refs[s].dtype)


def close_kernel(n_keys, scal, gq_ref, w_ref, own_ref, *refs):
    t = scal[2]
    others, (gqkv, even_ref, odd_ref) = refs[: n_keys - 1], refs[n_keys - 1 :]
    rows = gq_ref.shape[1]
    slots = rows // MB
    gqkv[:, SHARD:] = jnp.zeros((CUBE * rows, SLAB - SHARD), BF16)
    for p, k in enumerate(ORDER):
        gqkv[p * rows : (p + 1) * rows, :QH] = gq_ref[t ^ k]
        for m in range(MB):
            spot = pl.ds(pl.multiple_of((t ^ k) * slots, 64), slots)
            total = own_ref[m, spot, :]
            for other in others:
                total = total + other[m, spot, :].astype(F32)
            base = p * rows + m * slots
            gqkv[base : base + slots, QH:SHARD] = total.astype(BF16)
    step = 2 * rows
    for part, out_ref in enumerate((even_ref, odd_ref)):

        @pl.loop(0, 2)
        def _(i):
            local = pl.ds(pl.multiple_of(i * step, 128), step)
            spot = pl.ds(pl.multiple_of(part * 2 * step + i * step, 128), step)
            out_ref[local, :] = dot(gqkv[spot, :], w_ref[...], NT).astype(BF16)


def qkv_grad_kernel(scal, xg, gqkv, wo_ref, other_ref, mine_ref):
    cut = D // 6
    for flip, out_ref in ((1, other_ref), (0, mine_ref)):

        @pl.loop(0, 3)
        def _(i):
            cols = pl.ds(pl.multiple_of((scal[0] ^ flip) * (D // 2) + i * cut, 128), cut)
            spot = pl.ds(pl.multiple_of(i * cut, 128), cut)
            out_ref[spot, :SLAB] = dot(xg[:, cols], gqkv[...], TN).astype(BF16)
            out_ref[spot, SLAB:] = wo_ref[cols, :]


def out_grad_kernel(scal, ge_ref, go_ref, att_ref, nge, ngo, w_out, ate, ato):
    rows = ge_ref.shape[0] // 4
    for p, k in enumerate(ORDER):
        out = ate if p < 4 else ato
        out[(p % 4) * rows : (p % 4 + 1) * rows, :] = att_block(att_ref, 0, rows, scal[2] ^ k)
    cut = D // 4

    @pl.loop(0, 4)
    def _(i):
        cols = pl.ds(pl.multiple_of(i * cut, 128), cut)
        total = dot(ge_ref[:, cols], ate[...], TN) + dot(go_ref[:, cols], ato[...], TN)
        w_out[cols, :QH] = total.astype(BF16)
        low = dot(nge[:, cols], ge_ref[:, D:], TN) + dot(ngo[:, cols], go_ref[:, D:], TN)
        w_out[cols, QH:] = low[:, : OUT_SLAB - QH].astype(BF16)


def finish_attention_kernel(scal, w_ref, gain_ref, *refs):
    parts, (out_ref, gain_out, wo_out, rt_out, got) = refs[:CUBE], refs[CUBE:]
    for k, ref in enumerate(parts):
        got[scal[2] ^ k] = ref[...]
    for k in range(CUBE):
        part = got[k].astype(F32)
        out_ref[:, k * QH : (k + 1) * QH] = part[:, :QH]
        out_ref[:, QW + k * HD : QW + (k + 1) * HD] = part[:, QH : QH + HD]
        out_ref[:, QW + KW + k * HD : QW + KW + (k + 1) * HD] = part[:, QH + HD : SHARD]
        wo_out[:, k * QH : (k + 1) * QH] = part[:, SLAB : SLAB + QH]
        if k == 0:
            rt_out[...] = part[:, SLAB + EXTRA :].T[QH - EXTRA : QH - EXTRA + 8]
    total = jnp.sum(out_ref[...] * w_ref[...].astype(F32), axis=-1, keepdims=True)
    gain_out[...] = as_row(total) / gain_ref[...].astype(F32)


def finish_experts_kernel(
    scal, got, w_ref, rg_ref, rt_ref, gain_ref, out_ref, gain_out, dn_out
):
    total = jnp.zeros((out_ref.shape[1], 1), F32)
    for k in range(CUBE):
        e, h = k // 2, k % 2
        for at, base in ((h * HALF, 0), (FF + h * HALF, HALF)):
            part = got[k, :, base : base + HALF].astype(F32)
            out_ref[e, :, at : at + HALF] = part
            weight = w_ref[e, :, at : at + HALF].astype(F32)
            total = total + jnp.sum(part * weight, axis=-1, keepdims=True)
        dn_out[e, :, h * HALF : (h + 1) * HALF] = got[k, :, 2 * HALF :].astype(F32)
    router = jnp.sum(rg_ref[:E] * rt_ref[...].astype(F32), axis=0, keepdims=True)
    gain_out[...] = (as_row(total) + router) / gain_ref[...].astype(F32)


def output_kernel(scal, a0, a1, a2, a3, mixed_ref, out_ref):
    total = (
        a0[...].astype(F32) + a1[...].astype(F32) + a2[...].astype(F32) + a3[...].astype(F32)
    )
    out_ref[...] = (mixed_ref[...] + total).astype(BF16)


def tokens_kernel(scal, a0, a1, a2, a3, x_ref, grad_ref, gain_ref, out_ref):
    total = (
        a0[...].astype(F32) + a1[...].astype(F32) + a2[...].astype(F32) + a3[...].astype(F32)
    )
    x = x_ref[...].astype(F32)
    scale = lax.rsqrt(jnp.mean(x * x, axis=-1, keepdims=True) + 1e-05)
    out_ref[...] = (grad_ref[...] + norm_back(total * gain_ref[0:1, :], x, scale)).astype(BF16)


def body(
    tokens,
    lengths,
    routes,
    cotangent,
    attn_gain,
    qkv_weight,
    out_weight,
    moe_gain,
    router,
    gateup_weight,
    down_weight,
):
    nx, nc = lax.axis_size("dp"), lax.axis_size("ctx")
    links = Links(nx, nc)
    ng = links.ng
    n_outer = nx * ng
    slots = tokens.shape[2]
    rows = MB * slots
    extent = CUBE * slots
    wr = attn_gain.shape[0]
    out_rows = CUBE * rows

    half_rows = out_rows // 2
    tok = tokens.reshape(rows, D)
    cot = cotangent.reshape(rows, D)
    call = Kernels(lengths)
    bf, vm = shape, pltpu.VMEM

    def hbm(dims, dtype=BF16):
        return pltpu.HBM(dims, dtype)

    def f32(*dims):
        return shape(dims, F32)

    def pair(even, got):
        return call(pair_kernel, [bf((rows, even.shape[1]))] * 4, [even, got])

    def spread(parts):
        return [links.cube(part, bits) for part, bits in zip(parts[1:], ORDER[1:4])]

    def fold(mine, got):
        part = (CUBE * wr, mine.shape[1])
        kept = call(
            functools.partial(fold_kernel, ng),
            [shape(part, F32)] + [bf(part)] * (ng - 1),
            [mine, got],
            room=2,
        )
        return list(kept)

    def send_groups(kept):
        return [kept[0]] + [links.outer(kept[dg], 0, dg) for dg in range(1, ng)]

    def pack(blocks):
        own = blocks[0].shape
        return call(pack_kernel, [bf((4 * own[0], own[1]))], blocks)[0]

    wq_parts, tok_wide = call(
        prep_kernel,
        [bf((CUBE, wr, SLAB)), bf((rows, WIDE))],
        [qkv_weight, attn_gain.reshape(1, wr), tok, routes.reshape(rows, 2)],
        room=3,
    )
    tok_wide, wq_parts, gateup_in, down_in = fence(
        tok_wide, wq_parts, gateup_weight, down_weight.transpose(0, 2, 1)
    )
    tok_near = links.near(tok_wide)
    wq_group = links.swap(wq_parts).reshape(CUBE * wr, SLAB)
    moe_parts, wo_part = call(
        prep_rest_kernel,
        [bf((CUBE, wr, 3 * HALF)), bf((wr, WIDE))],
        [gateup_in, down_in, out_weight.T, router.T, moe_gain.reshape(1, wr)],
        room=3,
        busy=20,
    )
    wo = lax.all_gather(wo_part, AXES, axis=0, tiled=True)
    tok_wide, tok_near, wq_group, moe_parts = fence(tok_wide, tok_near, wq_group, moe_parts)
    tok_even = pack([tok_wide] + list(tok_near))
    tok_even, wq_group, moe_parts = fence(tok_even, wq_group, moe_parts)
    tok_odd = links.core(tok_even)
    wq_blocks = links.outer_direct(wq_group)
    moe_group = links.swap(moe_parts).reshape(CUBE * wr, 3 * HALF)
    tok_even, tok_odd, wq_blocks, moe_group, cot = fence(
        tok_even, tok_odd, wq_blocks, moe_group, cot
    )
    xg, q, kv, gain1, wq = call(
        functools.partial(qkv_kernel, ng, n_outer),
        [
            hbm((out_rows, D)),
            bf((MB, GROUP, extent, 2 * HD)),
            bf((MB, extent, 2 * HD)),
            hbm((8, D), F32),
            hbm((D, SLAB)),
        ],
        [tok_even, tok_odd],
        wq_blocks,
        [sems(n_outer)],
        room=4,
    )
    gu_group, dn_group = call(
        split_kernel, [bf((CUBE * wr, 2 * HALF)), bf((CUBE * wr, HALF))], [moe_group], after=[kv]
    )
    kv, dn_group, gu_group, cot = fence(kv, dn_group, gu_group, cot)
    kvs = [links.climb(kv, step) for step in range(1, ng)]
    cot_near = links.near(cot)
    dn_far = [links.outer(dn_group, 0, dg) for dg in range(1, ng)]
    gu_side = [links.outer(gu_group, dx, 0) for dx in range(1, nx)]
    kv, kvs, dn_group, dn_far, gu_group, gu_side, cot, cot_near, wo = fence(
        kv, kvs, dn_group, dn_far, gu_group, gu_side, cot, cot_near, wo
    )
    kvs = [kv] + list(kvs)
    cot_even = pack([cot] + list(cot_near))
    att, ot, lse = call(
        functools.partial(attend_kernel, slots),
        [bf((4 * rows, PAIR)), hbm((MB, GROUP, HD, extent), F32), hbm((MB, GROUP, extent), F32)],
        [q] + kvs,
        room=10,
    )
    att, cot_even, dn_group, dn_far, gu_group = fence(att, cot_even, dn_group, dn_far, gu_group)
    att_near = links.near(att)
    cot_odd = links.core(cot_even)
    dn_blocks = [dn_group] + list(dn_far)
    for dx in range(1, nx):
        dn_blocks += [links.outer(block, dx, 0) for block in dn_blocks[:ng]]
    gu_far = [links.outer(gu_group, 0, dg) for dg in range(1, ng)]
    att, att_near, cot_odd, dn_blocks, gu_far = fence(att, att_near, cot_odd, dn_blocks, gu_far)
    att_even = pack([att] + list(att_near))
    att_even, gu_far = fence(att_even, gu_far)
    att_odd = links.core(att_even)
    gu_blocks = [gu_group] + list(gu_far)
    for dx in range(1, nx):
        gu_blocks += [gu_side[dx - 1]] + [links.outer(block, dx, 0) for block in gu_far]
    back, w_dn = call(
        functools.partial(cot_kernel, ng, n_outer),
        [f32(out_rows, HALF), bf((D, HALF))],
        [cot_even, cot_odd],
        list(dn_blocks),
        [sems(n_outer)],
        room=4,
        busy=20,
    )
    att_odd, back = fence(att_odd, back)
    nge, ngo, mixed, comb = call(
        mix_kernel,
        [bf((half_rows, WIDE)), bf((half_rows, WIDE)), hbm((rows, D), F32), hbm((rows, EXTRA), F32)],
        [att_even, att_odd, tok_even, tok_odd, wo],
        scratch=[vm((out_rows, D), BF16)],
        room=8,
    )
    gu_blocks, nge, ngo = fence(gu_blocks, nge, ngo)

    def experts(wide, weights, base):
        outs = [bf((half_rows, HALF)), bf((half_rows, 2 * HALF)), bf((half_rows, WIDE))]
        kernel = functools.partial(expert_kernel, base, ng, n_outer)
        if base:
            outs.append(bf((D, 2 * HALF)))
            return call(kernel, outs, [wide, back], weights, [sems(n_outer)], room=8)
        return call(kernel, outs, [wide, back, weights], room=8)

    acto, gguo, odd, w_gu = experts(ngo, list(gu_blocks), half_rows)
    odd, nge = fence(odd, nge)
    odd_got = links.core(odd)
    acte, ggue, even = experts(nge, w_gu, 0)
    odd_got, even, acte, ggue = fence(odd_got, even, acte, ggue)
    sums = pair(even, odd_got)
    sums = fence(*sums)
    got = spread(sums)
    sums, got = fence(sums, got)
    grad_mixed, grad_wide = call(
        turn_kernel,
        [f32(rows, D), bf((rows, WIDE))],
        [sums[0]] + list(got) + [mixed, cot, comb, wo],
        room=8,
    )
    grad_wide, nge, ngo, acte, acto = fence(grad_wide, nge, ngo, acte, acto)
    grad_near = links.near(grad_wide)
    gu_other, dn_other, gu_mine, dn_mine = call(
        expert_grad_kernel,
        [bf((D // 2, 2 * HALF)), bf((D // 2, HALF))] * 2,
        [cot_even, cot_odd, nge, ngo, acte, acto, ggue, gguo],
        scratch=[vm((half_rows, HALF), BF16), vm((half_rows, HALF), BF16)],
        room=4,
        busy=20,
    )
    out_even, out_odd = call(
        expert_out_kernel, [bf((half_rows, D))] * 2, [w_dn, nge, ngo, acte, acto], room=4, busy=10
    )
    grad_wide, grad_near, out_odd, gu_other, dn_other, gu_mine, dn_mine = fence(
        grad_wide, grad_near, out_odd, gu_other, dn_other, gu_mine, dn_mine
    )
    dn_got = links.outer(dn_other, 1, 0)
    gu_got = links.outer(gu_other, 1, 0)
    grad_even = pack([grad_wide] + list(grad_near))
    grad_even, out_odd = fence(grad_even, out_odd)
    grad_odd = links.core(grad_even)
    out_got = links.core(out_odd)
    grad_odd, out_got = fence(grad_odd, out_got)
    out_sums = pair(out_even, out_got)
    grad_heads = call(
        grad_rows_kernel, [bf((CUBE, rows, QH))], [wo, grad_even, grad_odd], room=3
    )[0]
    grads = call(
        functools.partial(attend_back_kernel, slots, ng),
        [bf((CUBE, rows, QH)), f32(MB, extent, 2 * HD)] + [bf((MB, extent, 2 * HD))] * (ng - 1),
        [q] + kvs + [ot, lse, grad_heads],
        scratch=[vm((extent, 2 * HD), BF16)],
        room=12,
    )
    gq, gkv, grads = grads[0], grads[1], grads[2:]
    gq, gkv, grads, grad_even, grad_odd, out_sums, dn_got, dn_mine = fence(
        gq, gkv, grads, grad_even, grad_odd, out_sums, dn_got, dn_mine
    )
    out_got = spread(out_sums)
    gkv_others = [links.climb(grads[step - 1], -step) for step in range(1, ng)]
    wo_weight = call(
        out_grad_kernel,
        [hbm((D, OUT_SLAB))],
        [grad_even, grad_odd, att, nge, ngo],
        scratch=[vm((half_rows, QH), BF16), vm((half_rows, QH), BF16)],
        room=3,
        busy=20,
    )[0]
    dn_kept = fold(dn_mine, dn_got)
    gkv_others, gq, gkv, out_got, wo_weight, dn_kept = fence(
        gkv_others, gq, gkv, out_got, wo_weight, dn_kept
    )
    dn_groups = send_groups(dn_kept)
    gqkv, even, odd = call(
        functools.partial(close_kernel, ng),
        [bf((out_rows, SLAB)), bf((half_rows, D)), bf((half_rows, D))],
        [gq, wq, gkv] + list(gkv_others),
        room=3,
    )
    odd, gqkv, even = fence(odd, gqkv, even)
    odd_got = links.core(odd)
    gu_kept = fold(gu_mine, gu_got)
    qkvo_other, qkvo_mine = call(
        qkv_grad_kernel,
        [bf((D // 2, SLAB + OUT_SLAB))] * 2,
        [xg, gqkv, wo_weight],
        room=3,
    )
    odd_got, gu_kept, qkvo_other, even, dn_groups = fence(
        odd_got, gu_kept, qkvo_other, even, dn_groups
    )
    gu_groups = send_groups(gu_kept)
    qkvo_got = links.outer(qkvo_other, 1, 0)
    sums = pair(even, odd_got)
    got = spread(sums)
    qkvo_kept = fold(qkvo_mine, qkvo_got)
    sums, got, qkvo_kept = fence(sums, got, qkvo_kept)
    qkvo_groups = send_groups(qkvo_kept)
    grad_tokens = call(
        tokens_kernel, [bf((rows, D))], [sums[0]] + list(got) + [tok, grad_mixed, gain1]
    )[0]
    gu_groups, grad_tokens = fence(gu_groups, grad_tokens)
    moe_sum = call(
        functools.partial(fold_last_kernel, ng),
        [bf((CUBE * wr, 3 * HALF))],
        list(gu_groups) + list(dn_groups),
        room=2,
    )[0]
    expert_parts = links.swap(moe_sum.reshape(CUBE, wr, 3 * HALF))
    cuts = call(
        functools.partial(fold_parts_kernel, ng),
        [bf((wr, SLAB + OUT_SLAB))] * CUBE,
        qkvo_groups,
        scratch=[vm((CUBE, wr, SLAB + OUT_SLAB), BF16)],
        room=2,
    )
    qkvo_parts = [cuts[0]] + [links.cube(cuts[k], k) for k in range(1, CUBE)]
    output = call(output_kernel, [bf((rows, D))], [out_sums[0]] + list(out_got) + [mixed])[0]
    grad_qkv, grad_attn_gain, grad_out, grad_router = call(
        finish_attention_kernel,
        [f32(wr, QW + 2 * KW), f32(1, wr), f32(wr, QW), f32(8, wr)],
        [qkv_weight, attn_gain.reshape(1, wr)] + qkvo_parts,
        scratch=[vm((CUBE, wr, SLAB + OUT_SLAB), BF16)],
        room=3,
    )
    grad_gateup, grad_moe_gain, grad_down = call(
        finish_experts_kernel,
        [f32(E, wr, 2 * FF), f32(1, wr), f32(E, wr, FF)],
        [expert_parts, gateup_weight, grad_router, router.T, moe_gain.reshape(1, wr)],
        room=3,
    )
    return (
        output.reshape(MB, 1, slots, D),
        grad_tokens.reshape(MB, 1, slots, D),
        grad_attn_gain.reshape(wr),
        grad_qkv,
        grad_out.T,
        grad_moe_gain.reshape(wr),
        grad_router[:E].T,
        grad_gateup,
        grad_down.transpose(0, 2, 1),
    )


def solution(mesh):
    in_specs = (
        P(None, "dp", "ctx", None),
        P(None, "dp"),
        P(None, "dp", "ctx", None),
        P(None, "dp", "ctx", None),
        P(("dp", "ctx")),
        P(("dp", "ctx"), None),
        P(None, ("dp", "ctx")),
        P(("dp", "ctx")),
        P(("dp", "ctx"), None),
        P(None, ("dp", "ctx"), None),
        P(None, None, ("dp", "ctx")),
    )
    out_specs = (
        P(None, "dp", "ctx", None),
        P(None, "dp", "ctx", None),
        P(("dp", "ctx")),
        P(("dp", "ctx"), None),
        P(None, ("dp", "ctx")),
        P(("dp", "ctx")),
        P(("dp", "ctx"), None),
        P(None, ("dp", "ctx"), None),
        P(None, None, ("dp", "ctx")),
    )
    return jax.shard_map(body, mesh=mesh, in_specs=in_specs, out_specs=out_specs, check_vma=False)
```

```python
import functools
import math

import jax
import jax.numpy as jnp
from jax import lax
from jax.experimental import pallas as pl
from jax.experimental.pallas import tpu as pltpu
from jax.sharding import PartitionSpec as P

D = 1536
H = 24
KVH = 8
HD = 64
FF = 1024
E = 4
MB = 2
QW = 1536
KW = 512
CUBE = 8
GROUP = H // KVH
HALF = FF // 2
QH = GROUP * HD
SHARD = QH + 2 * HD
SLAB = 384
OUT_SLAB = 256
PAIR = 2 * QH
EXTRA = 128
WIDE = D + EXTRA
ORDER = (0, 4, 2, 6, 1, 5, 3, 7)
LOG2E = 1.4426950408889634
F32 = jnp.float32
BF16 = jnp.bfloat16
NN = (((1,), (0,)), ((), ()))
NT = (((1,), (1,)), ((), ()))
TN = (((0,), (0,)), ((), ()))
AXES = ("dp", "ctx")


def dot(left, right, dims=NN):
    return lax.dot_general(left, right, dims, preferred_element_type=F32)


class Kernels:
    def __init__(self, lengths):
        self.lengths = lengths

    def __call__(self, kernel, outs, ins, far=(), scratch=(), room=0, after=(), busy=0):
        ins, far, after = list(ins), list(far), list(after)
        n_in, n_after = 1 + len(ins) + len(far), len(after)
        vmem = pl.BlockSpec(memory_space=pltpu.VMEM)
        anywhere = pl.BlockSpec(memory_space=pl.ANY)

        def run(lengths, *refs):
            ctx = lax.axis_index("ctx")
            scal = [lax.axis_index("dp"), ctx >> 3, ctx & 7, lengths[0, 0], lengths[1, 0]]
            kernel(scal, *refs[: n_in - 1], *refs[n_in - 1 + n_after :])

        moved = sum(math.prod(a.shape) * a.dtype.itemsize for a in ins + list(outs))
        held = sum(2 * math.prod(s.shape) for s in scratch if hasattr(s, "shape"))
        grant = int(1.1 * moved) + held + (room + 4) * 1024 * 1024
        results = pl.pallas_call(
            run,
            out_shape=list(outs),
            in_specs=[pl.BlockSpec(memory_space=pltpu.SMEM)]
            + [vmem] * len(ins)
            + [anywhere] * (len(far) + n_after),
            out_specs=[vmem] * len(outs),
            scratch_shapes=list(scratch),
            compiler_params=pltpu.CompilerParams(vmem_limit_bytes=min(grant, 56 * 1024 * 1024)),
            cost_estimate=pl.CostEstimate(
                flops=1000 + busy * 10**9, bytes_accessed=1000, transcendentals=0
            ),
        )(
            self.lengths,
            *ins,
            *[pltpu.with_memory_space_constraint(value, pltpu.HBM) for value in far],
            *after,
        )
        return results


def sems(count):
    return pltpu.SemaphoreType.DMA((count,))


def shape(dims, dtype=BF16):
    return jax.ShapeDtypeStruct(dims, dtype)


class Links:
    def __init__(self, nx, nc):
        self.nx, self.nc, self.ng = nx, nc, nc // CUBE

    def _pairs(self, move):
        pairs = []
        for x in range(self.nx):
            for g in range(self.ng):
                for t in range(CUBE):
                    goal = move(x, g, t)
                    if goal is not None:
                        gx, gg, gt = goal
                        pairs.append((x * self.nc + g * CUBE + t, gx * self.nc + gg * CUBE + gt))
        return pairs

    def cube(self, value, bits):
        return lax.ppermute(value, AXES, self._pairs(lambda x, g, t: (x, g, t ^ bits)))

    def outer(self, value, dx, dg):
        return lax.ppermute(value, AXES, self._pairs(lambda x, g, t: (x ^ dx, g ^ dg, t)))

    def climb(self, value, step):
        def move(x, g, t):
            return (x, g + step, t) if 0 <= g + step < self.ng else None

        return lax.ppermute(value, AXES, self._pairs(move))

    def cubes(self):
        return [
            [x * self.nc + g * CUBE + t for t in range(CUBE)]
            for x in range(self.nx)
            for g in range(self.ng)
        ]

    def swap(self, value):
        return lax.all_to_all(
            value, AXES, split_axis=0, concat_axis=0, tiled=True, axis_index_groups=self.cubes()
        )

    def swap_all(self, value):
        return lax.all_to_all(value, AXES, split_axis=0, concat_axis=0, tiled=True)

    def near(self, rows):
        return [self.cube(rows, bits) for bits in ORDER[1:4]]

    def core(self, rows):
        return self.cube(rows, 1)

    def cores(self):
        return [list(range(core, self.nx * self.nc, 2)) for core in range(2)]

    def outers(self):
        return [
            [x * self.nc + g * CUBE + t for x in range(self.nx) for g in range(self.ng)]
            for t in range(CUBE)
        ]

    def outer_direct(self, rows):
        return [rows] + [
            self.outer(rows, dx, dg)
            for dx in range(self.nx)
            for dg in range(self.ng)
            if dx or dg
        ]


def fence(*values):
    return lax.optimization_barrier(values)


def stack_copies(refs, out, sem):
    rows = refs[0].shape[0]
    return [
        pltpu.make_async_copy(ref, out.at[pl.ds(n * rows, rows)], sem.at[n])
        for n, ref in enumerate(refs)
    ]


def outer_copies(refs, out, sem, scal, ng):
    rows = refs[0].shape[0]
    copies = []
    for j, ref in enumerate(refs):
        place = (scal[0] ^ (j // ng)) * ng + (scal[1] ^ (j % ng))
        spot = pl.ds(pl.multiple_of(place * rows, 16), rows)
        copies.append(pltpu.make_async_copy(ref, out.at[spot], sem.at[j]))
    return copies


def start_all(copies):
    for copy in copies:
        copy.start()


def wait_all(copies):
    for copy in copies:
        copy.wait()


def prep_kernel(scal, w_ref, gain_ref, tok_ref, routes_ref, out_ref, tok_out):
    wr = w_ref.shape[0]
    fill = column(gain_ref, SLAB - SHARD).astype(BF16)
    for k in range(CUBE):
        out_ref[k] = jnp.concatenate(
            [
                w_ref[:, k * QH : (k + 1) * QH],
                w_ref[:, QW + k * HD : QW + (k + 1) * HD],
                w_ref[:, QW + KW + k * HD : QW + KW + (k + 1) * HD],
                fill,
            ],
            axis=1,
        )
    rows = tok_ref.shape[0]
    tok_out[:, :D] = tok_ref[...]
    lane = lax.broadcasted_iota(jnp.int32, (rows, EXTRA), 1)
    names = jnp.where(lane == 0, routes_ref[:, 0:1], routes_ref[:, 1:2])
    tok_out[:, D:] = names.astype(F32).astype(BF16)


def column(row_ref, width):
    return jnp.broadcast_to(row_ref[...].astype(F32), (width, row_ref.shape[1])).T


def as_row(values):
    return jnp.broadcast_to(values, (values.shape[0], EXTRA)).T[0:1, :]


def prep_out_kernel(scal, wo_ref, rt_ref, gain_ref, wo_out):
    wr = wo_ref.shape[0]
    rt = rt_ref[...].astype(F32)
    rows = jnp.concatenate(
        [rt, rt, gain_ref[...].astype(F32), jnp.zeros((EXTRA - 2 * E - 1, wr), F32)], axis=0
    )
    wo_out[:, :QW] = wo_ref[...]
    wo_out[:, QW:] = rows.T.astype(BF16)


def prep_experts_kernel(scal, gu_ref, dn_ref, moe_out):
    for k in range(CUBE):
        e, h = k // 2, k % 2
        moe_out[k, :, :HALF] = gu_ref[e, :, h * HALF : (h + 1) * HALF]
        moe_out[k, :, HALF : 2 * HALF] = gu_ref[e, :, FF + h * HALF : FF + (h + 1) * HALF]
        moe_out[k, :, 2 * HALF :] = dn_ref[e, :, h * HALF : (h + 1) * HALF]


def split_kernel(scal, both_ref, gu_ref, dn_ref):
    gu_ref[...] = both_ref[:, : 2 * HALF]
    dn_ref[...] = both_ref[:, 2 * HALF :]


def pack_kernel(scal, *refs):
    rows = refs[0].shape[0]
    for n, ref in enumerate(refs[:-1]):
        refs[-1][n * rows : (n + 1) * rows, :] = ref[...]


def qkv_kernel(ng, n_outer, scal, even_ref, odd_ref, *refs):
    t = scal[2]
    weights, (xg, q_out, kv_out, gain_ref, w_ref, sem) = refs[:n_outer], refs[n_outer:]
    copies = outer_copies(weights, w_ref, sem, scal, ng)
    start_all(copies)
    wait_all(copies)
    rows = even_ref.shape[0] // 4
    slots = rows // MB
    blank = jnp.zeros((slots, HD), BF16)
    gain = w_ref[:, 256:].astype(F32).T[SHARD - 256 : SHARD - 248, :]
    gain_ref[...] = gain
    gain = gain[0:1]
    for p, k in enumerate(ORDER):
        source = even_ref if p < 4 else odd_ref
        values = source[(p % 4) * rows : (p % 4 + 1) * rows, :D].astype(F32)
        scale = lax.rsqrt(jnp.mean(values * values, axis=-1, keepdims=True) + 1e-05)
        packed = (values * scale * gain).astype(BF16)
        xg[p * rows : (p + 1) * rows, :] = packed
        y = dot(packed, w_ref[...]).astype(BF16)
        for m in range(MB):
            part = y[m * slots : (m + 1) * slots]
            spot = pl.ds(pl.multiple_of((t ^ k) * slots, 64), slots)
            for h in range(GROUP):
                q_out[m, h, spot, :] = jnp.concatenate(
                    [part[:, h * HD : (h + 1) * HD], blank], axis=1
                )
            kv_out[m, spot, :] = part[:, QH:SHARD]


def key_bias(extent, g, step, length):
    local = lax.broadcasted_iota(jnp.int32, (extent, 1), 0)
    seen = ((g - step) * extent + local < length) & (g >= step)
    return jnp.where(seen, 0.0, -1e30).astype(F32)


def causal_bias(extent):
    keys = lax.broadcasted_iota(jnp.int32, (extent, extent), 0)
    rows = lax.broadcasted_iota(jnp.int32, (extent, extent), 1)
    return jnp.where(keys <= rows, 0.0, -1e30).astype(F32)


def attend_kernel(slots, scal, *refs):
    g = scal[1]
    n_keys = len(refs) - 4
    q_ref, kv_refs, (att_ref, ot_ref, lse_ref) = refs[0], refs[1 : 1 + n_keys], refs[1 + n_keys :]
    extent = q_ref.shape[2]
    causal = causal_bias(extent)
    for m in range(MB):
        length = scal[3 + m]
        biases = [key_bias(extent, g, s, length) for s in range(n_keys)]
        for h in range(GROUP):
            q = q_ref[m, h]
            top = total = acc = None
            for s in range(n_keys):
                kv = kv_refs[s][m]
                st = dot(kv, q, NT) * (0.125 * LOG2E) + biases[s]
                if s == 0:
                    st = st + causal
                peak = jnp.max(st, axis=0, keepdims=True)
                if s == 0:
                    pt = jnp.exp2(st - peak)
                    top, total = peak, jnp.sum(pt, axis=0, keepdims=True)
                    acc = dot(kv, pt.astype(BF16), TN)
                else:
                    fresh = jnp.maximum(top, peak)
                    scale = jnp.exp2(top - fresh)
                    pt = jnp.exp2(st - fresh)
                    total = total * scale + jnp.sum(pt, axis=0, keepdims=True)
                    acc = acc * scale + dot(kv, pt.astype(BF16), TN)
                    top = fresh
            ot = acc[HD:, :] / total
            ot_ref[m, h] = ot
            lse_ref[m, h : h + 1, :] = top + jnp.log2(total)
            o = ot.T.astype(BF16)
            for k in range(CUBE):
                place = (k // 4) * QH + h * HD
                base = (k % 4) * MB * slots + m * slots
                att_ref[base : base + slots, place : place + HD] = o[k * slots : (k + 1) * slots]


def row_valid(scal, rows):
    slots = rows // MB
    spot = lax.broadcasted_iota(jnp.int32, (rows, 1), 0)
    place = (scal[1] * CUBE + scal[2]) * slots
    length = jnp.where(spot < slots, scal[3], scal[4])
    inner = jnp.where(spot < slots, spot, spot - slots)
    return jnp.where(place + inner < length, 1.0, 0.0).astype(F32)


def gain_row(rest):
    return rest.astype(F32).T[2 * E : 2 * E + 1, :]


def att_block(ref, base, rows, j):
    spot = pl.ds(pl.multiple_of(base + (j & 3) * rows, 16), rows)
    both = ref[spot, :]
    return jnp.where(j >= 4, both[:, QH:], both[:, :QH])


def mix_kernel(scal, even_ref, odd_ref, toke_ref, toko_ref, wo_ref, *refs):
    t = scal[2]
    nge, ngo, mixed_ref, comb_ref, att = refs
    rows = mixed_ref.shape[0]
    slots = rows // MB
    for q in range(4):
        head = t ^ ORDER[q]
        lanes = pl.ds(pl.multiple_of((head >> 1) * PAIR, 128), PAIR)
        for p, k in enumerate(ORDER):
            low = att_block(even_ref, q * 4 * rows, rows, t ^ k)
            high = att_block(odd_ref, q * 4 * rows, rows, t ^ k)
            flip = (head & 1) == 1
            att[p * rows : (p + 1) * rows, lanes] = jnp.concatenate(
                [jnp.where(flip, high, low), jnp.where(flip, low, high)], axis=1
            )
    rest = wo_ref[:, QW:]
    gain = gain_row(rest)
    lane = lax.broadcasted_iota(jnp.int32, (2 * rows, EXTRA), 1)
    spot = lax.broadcasted_iota(jnp.int32, (2 * rows, 1), 0)
    inner = spot & (rows - 1)
    second = inner >= slots
    length = jnp.where(second, scal[4], scal[3])
    slot = jnp.where(second, inner - slots, inner)
    for p in range(0, CUBE, 2):
        tok_ref, out_ref = (toke_ref, nge) if p < 4 else (toko_ref, ngo)
        local = slice((p % 4) * rows, (p % 4 + 2) * rows)
        owner = jnp.where(spot < rows, t ^ ORDER[p], t ^ ORDER[p + 1])
        place = (scal[1] * CUBE + owner) * slots + slot
        valid = jnp.where(place < length, 1.0, 0.0).astype(F32)
        branch = dot(att[p * rows : (p + 2) * rows, :], wo_ref[:, :QW], NT)
        mixed = tok_ref[local, :D].astype(F32) + valid * branch
        scale = lax.rsqrt(jnp.mean(mixed * mixed, axis=-1, keepdims=True) + 1e-05)
        low = (mixed * scale * gain).astype(BF16)
        logits = dot(low, rest)
        names = tok_ref[local, D:].astype(F32)
        expert = (lane & (E - 1)).astype(F32)
        chosen = ((expert == names[:, 0:1]) | (expert == names[:, 1:2])) & (lane < 2 * E)
        peak = jnp.max(jnp.where(chosen, logits, -3e38), axis=-1, keepdims=True)
        expo = jnp.where(chosen, jnp.exp(logits - peak), 0.0)
        comb = expo / (0.5 * jnp.sum(expo, axis=-1, keepdims=True))
        if p == 0:
            mixed_ref[...] = mixed[:rows]
            comb_ref[...] = jnp.where(lane < E, comb, 0.0)[:rows]
        comb = comb * valid
        high = comb.astype(BF16)
        tail = (comb - high.astype(F32)).astype(BF16)
        out_ref[local, :D] = low
        out_ref[local, D:] = jnp.where(lane < E, high, tail)


def row_valid(scal, rows):
    slots = rows // MB
    spot = lax.broadcasted_iota(jnp.int32, (rows, 1), 0)
    place = (scal[1] * CUBE + scal[2]) * slots
    length = jnp.where(spot < slots, scal[3], scal[4])
    inner = jnp.where(spot < slots, spot, spot - slots)
    return jnp.where(place + inner < length, 1.0, 0.0).astype(F32)


def cot_kernel(ng, n_outer, scal, even_ref, odd_ref, *refs):
    dn_blocks, (q_ref, w_dn, sem) = refs[:n_outer], refs[n_outer:]
    copies = outer_copies(dn_blocks, w_dn, sem, scal, ng)
    start_all(copies)
    wait_all(copies)
    step = even_ref.shape[0] // 2
    for part, source in enumerate((even_ref, odd_ref)):

        @pl.loop(0, 2)
        def _(i):
            local = pl.ds(pl.multiple_of(i * step, 128), step)
            spot = pl.ds(pl.multiple_of((2 * part + i) * step, 128), step)
            q_ref[spot, :] = dot(source[local, :], w_dn[...])


def own_share(wide, scal):
    lane = lax.broadcasted_iota(jnp.int32, wide.shape, 1)
    expert = scal[2] // 2
    mine = (lane == expert) | (lane == expert + E)
    return jnp.sum(jnp.where(mine, wide.astype(F32), 0.0), axis=-1, keepdims=True)


def expert_kernel(base, ng, n_outer, scal, ngw, q_ref, *refs):
    if base:
        blocks, (act_ref, ggu_ref, out_ref, w_ref, sem) = refs[:n_outer], refs[n_outer:]
        copies = outer_copies(blocks, w_ref, sem, scal, ng)
        start_all(copies)
        wait_all(copies)
    else:
        w_ref, act_ref, ggu_ref, out_ref = refs
    step = ngw.shape[0] // 2
    expert = scal[2] // 2

    @pl.loop(0, 2)
    def _(i):
        spot = pl.ds(pl.multiple_of(i * step, 128), step)
        share = own_share(ngw[spot, D:], scal)
        gu = dot(ngw[spot, :D], w_ref[...])
        gate, up = gu[:, :HALF], gu[:, HALF:]
        sig = 1.0 / (1.0 + jnp.exp(-gate))
        soft = gate * sig
        act = (soft * up).astype(BF16)
        act_ref[spot, :] = act
        back = q_ref[pl.ds(pl.multiple_of(base + i * step, 128), step), :]
        dots = jnp.sum(act.astype(F32) * back, axis=-1, keepdims=True)
        back = back * share
        ggu_ref[spot, :HALF] = (back * up * (sig * (1.0 + gate * (1.0 - sig)))).astype(BF16)
        ggu_ref[spot, HALF:] = (back * soft).astype(BF16)
        out_ref[spot, :D] = dot(ggu_ref[spot, :], w_ref[...], NT).astype(BF16)
        high = dots.astype(BF16)
        rest = (dots - high.astype(F32)).astype(BF16)
        lane = lax.broadcasted_iota(jnp.int32, (step, EXTRA), 1)
        out_ref[spot, D:] = jnp.where(
            lane == expert, high, jnp.where(lane == expert + E, rest, jnp.zeros_like(rest))
        )


def expert_grad_kernel(
    scal, dye, dyo, nge, ngo, acte, acto, ggue, gguo, gu_other, dn_other, gu_mine, dn_mine, cae, cao
):
    for wide, act, out in ((nge, acte, cae), (ngo, acto, cao)):
        out[...] = (act[...].astype(F32) * own_share(wide[:, D:], scal)).astype(BF16)
    cut = D // 6
    for flip, gu_ref, dn_ref in ((1, gu_other, dn_other), (0, gu_mine, dn_mine)):

        @pl.loop(0, 3)
        def _(i):
            cols = pl.ds(pl.multiple_of((scal[0] ^ flip) * (D // 2) + i * cut, 128), cut)
            spot = pl.ds(pl.multiple_of(i * cut, 128), cut)
            total = dot(nge[:, cols], ggue[...], TN) + dot(ngo[:, cols], gguo[...], TN)
            gu_ref[spot, :] = total.astype(BF16)
            total = dot(dye[:, cols], cae[...], TN) + dot(dyo[:, cols], cao[...], TN)
            dn_ref[spot, :] = total.astype(BF16)


def expert_out_kernel(scal, w_ref, nge, ngo, acte, acto, even_ref, odd_ref):
    step = acte.shape[0] // 2
    for wide, act, out_ref in ((nge, acte, even_ref), (ngo, acto, odd_ref)):

        @pl.loop(0, 2)
        def _(i):
            spot = pl.ds(pl.multiple_of(i * step, 128), step)
            share = own_share(wide[spot, D:], scal)
            out_ref[spot, :] = (dot(act[spot, :], w_ref[...], NT) * share).astype(BF16)


def fold_kernel(ng, scal, mine_ref, got_ref, *refs):
    rows = mine_ref.shape[0] // ng
    for dg, out in enumerate(refs):
        spot = pl.ds(pl.multiple_of((scal[1] ^ dg) * rows, 16), rows)
        total = mine_ref[spot, :].astype(F32) + got_ref[spot, :].astype(F32)
        out[...] = total.astype(out.dtype)


def fold_last_kernel(n_in, scal, *refs):
    base = 0
    for ins in (refs[:n_in], refs[n_in:-1]):
        total = ins[0][...]
        for ref in ins[1:]:
            total = total + ref[...].astype(F32)
        refs[-1][:, base : base + total.shape[1]] = total.astype(BF16)
        base += total.shape[1]


def fold_parts_kernel(n_in, scal, *refs):
    ins, outs = refs[:n_in], refs[n_in:]
    wr = outs[0].shape[0]
    for j in range(CUBE):
        spot = slice(j * wr, (j + 1) * wr)
        total = ins[0][spot, :]
        for ref in ins[1:]:
            total = total + ref[spot, :].astype(F32)
        outs[-1][j] = total.astype(BF16)
    for k, out in enumerate(outs[:-1]):
        out[...] = outs[-1][scal[2] ^ k]


def pair_kernel(scal, even_ref, odd_ref, *outs):
    rows = outs[0].shape[0]
    for p, out in enumerate(outs):
        spot = slice(p * rows, (p + 1) * rows)
        out[...] = (even_ref[spot, :].astype(F32) + odd_ref[spot, :].astype(F32)).astype(BF16)


def norm_back(grad, values, scale):
    unit = values * scale
    return scale * (grad - unit * jnp.mean(grad * unit, axis=-1, keepdims=True))


def turn_kernel(scal, a0, a1, a2, a3, mixed_ref, cot_ref, comb_ref, wo_ref, grad_ref, wide_ref):
    rest = wo_ref[:, QW:]
    rows = mixed_ref.shape[0]
    total = (
        a0[...].astype(F32) + a1[...].astype(F32) + a2[...].astype(F32) + a3[...].astype(F32)
    )
    valid = row_valid(scal, rows)
    lane = lax.broadcasted_iota(jnp.int32, (rows, EXTRA), 1)
    dots = total[:, D:]
    dots = (dots + pltpu.roll(dots, EXTRA - E, 1)) * valid
    comb = comb_ref[...]
    inner = jnp.sum(comb * dots, axis=-1, keepdims=True)
    grad_logits = jnp.where(lane < E, comb * (dots - inner), 0.0).astype(BF16)
    grad_normed = (total[:, :D] + dot(grad_logits, rest, NT)) * gain_row(rest)
    mixed = mixed_ref[...]
    scale = lax.rsqrt(jnp.mean(mixed * mixed, axis=-1, keepdims=True) + 1e-05)
    grad_mixed = cot_ref[...].astype(F32) + norm_back(grad_normed, mixed, scale)
    grad_ref[...] = grad_mixed
    branch = (valid * grad_mixed).astype(BF16)
    wide_ref[:, :D] = branch
    wide_ref[:, D:] = grad_logits


def grad_rows_kernel(scal, w_ref, even_ref, odd_ref, ga_ref):
    t = scal[2]
    rows = ga_ref.shape[1]
    window = w_ref[:, pl.ds(pl.multiple_of(((3 * t) >> 1) * 128, 128), 256)]
    weight = jnp.where((t & 1) == 1, window[:, HD:], window[:, :QH])
    for part, wide in enumerate((even_ref, odd_ref)):
        for n in range(2):
            spot = slice(2 * n * rows, 2 * (n + 1) * rows)
            grad = dot(wide[spot, :D], weight).astype(BF16)
            for i in range(2):
                ga_ref[t ^ ORDER[4 * part + 2 * n + i]] = grad[i * rows : (i + 1) * rows]


def attend_back_kernel(slots, n_keys, scal, *refs):
    g = scal[1]
    q_ref, kv_refs, refs = refs[0], refs[1 : 1 + n_keys], refs[1 + n_keys :]
    ot_ref, lse_ref, ga_ref, gq_ref, refs = refs[0], refs[1], refs[2], refs[3], refs[4:]
    gkv_refs, (do_ref,) = refs[:n_keys], refs[n_keys:]
    extent = q_ref.shape[2]
    causal = causal_bias(extent)
    blank = jnp.zeros((slots, HD), BF16)
    for m in range(MB):
        length = scal[3 + m]
        biases = [key_bias(extent, g, s, length) for s in range(n_keys)]
        sums = [None] * n_keys
        for h in range(GROUP):
            for k in range(CUBE):
                part = ga_ref[k, m * slots : (m + 1) * slots, h * HD : (h + 1) * HD]
                do_ref[k * slots : (k + 1) * slots, :] = jnp.concatenate([blank, part], axis=1)
            q = q_ref[m, h]
            do = do_ref[...]
            dot_t = do.astype(F32).T[HD:, :]
            delta = jnp.sum(dot_t * ot_ref[m, h], axis=0, keepdims=True)
            lse = lse_ref[m, h : h + 1, :]
            grad_q = None
            for s in range(n_keys):
                kv = kv_refs[s][m]
                st = dot(kv, q, NT) * (0.125 * LOG2E) + biases[s]
                if s == 0:
                    st = st + causal
                pt = jnp.exp2(st - lse)
                dpt = dot(kv, do, NT)
                dst = (pt * (dpt - delta) * 0.125).astype(BF16)
                part = dot(dst, q) + dot(pt.astype(BF16), do)
                sums[s] = part if sums[s] is None else sums[s] + part
                part = dot(kv, dst, TN)
                grad_q = part if grad_q is None else grad_q + part
            gq = grad_q[:HD, :].T.astype(BF16)
            for k in range(CUBE):
                gq_ref[k, m * slots : (m + 1) * slots, h * HD : (h + 1) * HD] = gq[
                    k * slots : (k + 1) * slots
                ]
        for s in range(n_keys):
            gkv_refs[s][m] = sums[s].astype(gkv_refs[s].dtype)


def close_kernel(n_keys, scal, gq_ref, w_ref, own_ref, *refs):
    t = scal[2]
    others, (gqkv, even_ref, odd_ref) = refs[: n_keys - 1], refs[n_keys - 1 :]
    rows = gq_ref.shape[1]
    slots = rows // MB
    gqkv[:, SHARD:] = jnp.zeros((CUBE * rows, SLAB - SHARD), BF16)
    for p, k in enumerate(ORDER):
        gqkv[p * rows : (p + 1) * rows, :QH] = gq_ref[t ^ k]
        for m in range(MB):
            spot = pl.ds(pl.multiple_of((t ^ k) * slots, 64), slots)
            total = own_ref[m, spot, :]
            for other in others:
                total = total + other[m, spot, :].astype(F32)
            base = p * rows + m * slots
            gqkv[base : base + slots, QH:SHARD] = total.astype(BF16)
    step = 2 * rows
    for part, out_ref in enumerate((even_ref, odd_ref)):

        @pl.loop(0, 2)
        def _(i):
            local = pl.ds(pl.multiple_of(i * step, 128), step)
            spot = pl.ds(pl.multiple_of(part * 2 * step + i * step, 128), step)
            out_ref[local, :] = dot(gqkv[spot, :], w_ref[...], NT).astype(BF16)


def qkv_grad_kernel(scal, xg, gqkv, wo_ref, other_ref, mine_ref):
    cut = D // 6
    for flip, out_ref in ((1, other_ref), (0, mine_ref)):

        @pl.loop(0, 3)
        def _(i):
            cols = pl.ds(pl.multiple_of((scal[0] ^ flip) * (D // 2) + i * cut, 128), cut)
            spot = pl.ds(pl.multiple_of(i * cut, 128), cut)
            out_ref[spot, :SLAB] = dot(xg[:, cols], gqkv[...], TN).astype(BF16)
            out_ref[spot, SLAB:] = wo_ref[cols, :]


def out_grad_kernel(scal, ge_ref, go_ref, att_ref, nge, ngo, w_out, ate, ato):
    rows = ge_ref.shape[0] // 4
    for p, k in enumerate(ORDER):
        out = ate if p < 4 else ato
        out[(p % 4) * rows : (p % 4 + 1) * rows, :] = att_block(att_ref, 0, rows, scal[2] ^ k)
    cut = D // 4

    @pl.loop(0, 4)
    def _(i):
        cols = pl.ds(pl.multiple_of(i * cut, 128), cut)
        total = dot(ge_ref[:, cols], ate[...], TN) + dot(go_ref[:, cols], ato[...], TN)
        w_out[cols, :QH] = total.astype(BF16)
        low = dot(nge[:, cols], ge_ref[:, D:], TN) + dot(ngo[:, cols], go_ref[:, D:], TN)
        w_out[cols, QH:] = low[:, : OUT_SLAB - QH].astype(BF16)


def finish_attention_kernel(scal, w_ref, gain_ref, *refs):
    parts, (out_ref, gain_out, wo_out, rt_out, got) = refs[:CUBE], refs[CUBE:]
    for k, ref in enumerate(parts):
        got[scal[2] ^ k] = ref[...]
    for k in range(CUBE):
        part = got[k].astype(F32)
        out_ref[:, k * QH : (k + 1) * QH] = part[:, :QH]
        out_ref[:, QW + k * HD : QW + (k + 1) * HD] = part[:, QH : QH + HD]
        out_ref[:, QW + KW + k * HD : QW + KW + (k + 1) * HD] = part[:, QH + HD : SHARD]
        wo_out[:, k * QH : (k + 1) * QH] = part[:, SLAB : SLAB + QH]
        if k == 0:
            rt_out[...] = part[:, SLAB + EXTRA :].T[QH - EXTRA : QH - EXTRA + 8]
    total = jnp.sum(out_ref[...] * w_ref[...].astype(F32), axis=-1, keepdims=True)
    gain_out[...] = as_row(total) / gain_ref[...].astype(F32)


def finish_experts_kernel(
    scal, got, w_ref, rg_ref, rt_ref, gain_ref, out_ref, gain_out, dn_out
):
    total = jnp.zeros((out_ref.shape[1], 1), F32)
    for k in range(CUBE):
        e, h = k // 2, k % 2
        for at, base in ((h * HALF, 0), (FF + h * HALF, HALF)):
            part = got[k, :, base : base + HALF].astype(F32)
            out_ref[e, :, at : at + HALF] = part
            weight = w_ref[e, :, at : at + HALF].astype(F32)
            total = total + jnp.sum(part * weight, axis=-1, keepdims=True)
        dn_out[e, :, h * HALF : (h + 1) * HALF] = got[k, :, 2 * HALF :].astype(F32)
    router = jnp.sum(rg_ref[:E] * rt_ref[...].astype(F32), axis=0, keepdims=True)
    gain_out[...] = (as_row(total) + router) / gain_ref[...].astype(F32)


def output_kernel(scal, a0, a1, a2, a3, mixed_ref, out_ref):
    total = (
        a0[...].astype(F32) + a1[...].astype(F32) + a2[...].astype(F32) + a3[...].astype(F32)
    )
    out_ref[...] = (mixed_ref[...] + total).astype(BF16)


def tokens_kernel(scal, a0, a1, a2, a3, x_ref, grad_ref, gain_ref, out_ref):
    total = (
        a0[...].astype(F32) + a1[...].astype(F32) + a2[...].astype(F32) + a3[...].astype(F32)
    )
    x = x_ref[...].astype(F32)
    scale = lax.rsqrt(jnp.mean(x * x, axis=-1, keepdims=True) + 1e-05)
    out_ref[...] = (grad_ref[...] + norm_back(total * gain_ref[0:1, :], x, scale)).astype(BF16)


def body(
    tokens,
    lengths,
    routes,
    cotangent,
    attn_gain,
    qkv_weight,
    out_weight,
    moe_gain,
    router,
    gateup_weight,
    down_weight,
):
    nx, nc = lax.axis_size("dp"), lax.axis_size("ctx")
    links = Links(nx, nc)
    ng = links.ng
    n_outer = nx * ng
    slots = tokens.shape[2]
    rows = MB * slots
    extent = CUBE * slots
    wr = attn_gain.shape[0]
    out_rows = CUBE * rows

    half_rows = out_rows // 2
    tok = tokens.reshape(rows, D)
    cot = cotangent.reshape(rows, D)
    call = Kernels(lengths)
    bf, vm = shape, pltpu.VMEM

    def hbm(dims, dtype=BF16):
        return pltpu.HBM(dims, dtype)

    def f32(*dims):
        return shape(dims, F32)

    def pair(even, got):
        return call(pair_kernel, [bf((rows, even.shape[1]))] * 4, [even, got])

    def spread(parts):
        return [links.cube(part, bits) for part, bits in zip(parts[1:], ORDER[1:4])]

    def fold(mine, got):
        part = (CUBE * wr, mine.shape[1])
        kept = call(
            functools.partial(fold_kernel, ng),
            [shape(part, F32)] + [bf(part)] * (ng - 1),
            [mine, got],
            room=2,
        )
        return list(kept)

    def send_groups(kept):
        return [kept[0]] + [links.outer(kept[dg], 0, dg) for dg in range(1, ng)]

    def pack(blocks):
        own = blocks[0].shape
        return call(pack_kernel, [bf((4 * own[0], own[1]))], blocks)[0]

    wq_parts, tok_wide = call(
        prep_kernel,
        [bf((CUBE, wr, SLAB)), bf((rows, WIDE))],
        [qkv_weight, attn_gain.reshape(1, wr), tok, routes.reshape(rows, 2)],
        room=3,
    )
    tok_wide, wq_parts, out_in = fence(tok_wide, wq_parts, out_weight.T)
    tok_near = links.near(tok_wide)
    wq_group = links.swap(wq_parts).reshape(CUBE * wr, SLAB)
    wo_part = call(
        prep_out_kernel,
        [bf((wr, WIDE))],
        [out_in, router.T, moe_gain.reshape(1, wr)],
        room=3,
        busy=20,
    )[0]
    wo = lax.all_gather(wo_part, AXES, axis=0, tiled=True)
    wq_group, gateup_in, down_in = fence(
        wq_group, gateup_weight, down_weight.transpose(0, 2, 1)
    )
    moe_parts = call(
        prep_experts_kernel, [bf((CUBE, wr, 3 * HALF))], [gateup_in, down_in], room=3
    )[0]
    tok_wide, tok_near = fence(tok_wide, tok_near)
    tok_even = pack([tok_wide] + list(tok_near))
    tok_odd = links.core(tok_even)
    wq_far = [links.outer(wq_group, 0, dg) for dg in range(1, ng)]
    wq_blocks = [wq_group] + wq_far
    for dx in range(1, nx):
        wq_blocks += [links.outer(block, dx, 0) for block in wq_blocks[:ng]]
    moe_group = links.swap(moe_parts).reshape(CUBE * wr, 3 * HALF)
    tok_even, tok_odd, wq_blocks, moe_group, cot = fence(
        tok_even, tok_odd, wq_blocks, moe_group, cot
    )
    xg, q, kv, gain1, wq = call(
        functools.partial(qkv_kernel, ng, n_outer),
        [
            hbm((out_rows, D)),
            bf((MB, GROUP, extent, 2 * HD)),
            bf((MB, extent, 2 * HD)),
            hbm((8, D), F32),
            hbm((D, SLAB)),
        ],
        [tok_even, tok_odd],
        wq_blocks,
        [sems(n_outer)],
        room=4,
    )
    gu_group, dn_group = call(
        split_kernel, [bf((CUBE * wr, 2 * HALF)), bf((CUBE * wr, HALF))], [moe_group]
    )
    dn_group, gu_group, cot = fence(dn_group, gu_group, cot)
    kvs = [links.climb(kv, step) for step in range(1, ng)]
    cot_near = links.near(cot)
    dn_far = [links.outer(dn_group, 0, dg) for dg in range(1, ng)]
    gu_side = [links.outer(gu_group, dx, 0) for dx in range(1, nx)]
    kv, kvs, dn_group, dn_far, gu_group, gu_side, cot, cot_near, wo = fence(
        kv, kvs, dn_group, dn_far, gu_group, gu_side, cot, cot_near, wo
    )
    kvs = [kv] + list(kvs)
    cot_even = pack([cot] + list(cot_near))
    att, ot, lse = call(
        functools.partial(attend_kernel, slots),
        [bf((4 * rows, PAIR)), hbm((MB, GROUP, HD, extent), F32), hbm((MB, GROUP, extent), F32)],
        [q] + kvs,
        room=10,
    )
    cot_even, dn_group, dn_far, gu_group = fence(cot_even, dn_group, dn_far, gu_group)
    att_near = links.near(att)
    cot_odd = links.core(cot_even)
    dn_blocks = [dn_group] + list(dn_far)
    for dx in range(1, nx):
        dn_blocks += [links.outer(block, dx, 0) for block in dn_blocks[:ng]]
    gu_far = [links.outer(gu_group, 0, dg) for dg in range(1, ng)]
    att, att_near, cot_odd, dn_blocks, gu_far = fence(att, att_near, cot_odd, dn_blocks, gu_far)
    att_even = pack([att] + list(att_near))
    att_even, gu_far = fence(att_even, gu_far)
    att_odd = links.core(att_even)
    gu_blocks = [gu_group] + list(gu_far)
    for dx in range(1, nx):
        gu_blocks += [gu_side[dx - 1]] + [links.outer(block, dx, 0) for block in gu_far]
    back, w_dn = call(
        functools.partial(cot_kernel, ng, n_outer),
        [f32(out_rows, HALF), bf((D, HALF))],
        [cot_even, cot_odd],
        list(dn_blocks),
        [sems(n_outer)],
        room=4,
        busy=20,
    )
    att_odd, back = fence(att_odd, back)
    nge, ngo, mixed, comb = call(
        mix_kernel,
        [bf((half_rows, WIDE)), bf((half_rows, WIDE)), hbm((rows, D), F32), hbm((rows, EXTRA), F32)],
        [att_even, att_odd, tok_even, tok_odd, wo],
        scratch=[vm((out_rows, D), BF16)],
        room=8,
    )
    gu_blocks, nge, ngo = fence(gu_blocks, nge, ngo)

    def experts(wide, weights, base):
        outs = [bf((half_rows, HALF)), bf((half_rows, 2 * HALF)), bf((half_rows, WIDE))]
        kernel = functools.partial(expert_kernel, base, ng, n_outer)
        if base:
            outs.append(bf((D, 2 * HALF)))
            return call(kernel, outs, [wide, back], weights, [sems(n_outer)], room=8)
        return call(kernel, outs, [wide, back, weights], room=8)

    acto, gguo, odd, w_gu = experts(ngo, list(gu_blocks), half_rows)
    odd, nge = fence(odd, nge)
    odd_got = links.core(odd)
    acte, ggue, even = experts(nge, w_gu, 0)
    odd_got, even, acte, ggue = fence(odd_got, even, acte, ggue)
    sums = pair(even, odd_got)
    sums = fence(*sums)
    got = spread(sums)
    sums, got = fence(sums, got)
    grad_mixed, grad_wide = call(
        turn_kernel,
        [f32(rows, D), bf((rows, WIDE))],
        [sums[0]] + list(got) + [mixed, cot, comb, wo],
        room=8,
    )
    grad_wide, nge, ngo, acte, acto = fence(grad_wide, nge, ngo, acte, acto)
    grad_near = links.near(grad_wide)
    gu_other, dn_other, gu_mine, dn_mine = call(
        expert_grad_kernel,
        [bf((D // 2, 2 * HALF)), bf((D // 2, HALF))] * 2,
        [cot_even, cot_odd, nge, ngo, acte, acto, ggue, gguo],
        scratch=[vm((half_rows, HALF), BF16), vm((half_rows, HALF), BF16)],
        room=4,
        busy=20,
    )
    out_even, out_odd = call(
        expert_out_kernel, [bf((half_rows, D))] * 2, [w_dn, nge, ngo, acte, acto], room=4, busy=10
    )
    grad_wide, grad_near, out_odd, gu_other, dn_other, gu_mine, dn_mine = fence(
        grad_wide, grad_near, out_odd, gu_other, dn_other, gu_mine, dn_mine
    )
    dn_got = links.outer(dn_other, 1, 0)
    gu_got = links.outer(gu_other, 1, 0)
    grad_even = pack([grad_wide] + list(grad_near))
    grad_even, out_odd = fence(grad_even, out_odd)
    grad_odd = links.core(grad_even)
    out_got = links.core(out_odd)
    grad_odd, out_got = fence(grad_odd, out_got)
    out_sums = pair(out_even, out_got)
    grad_heads = call(
        grad_rows_kernel, [bf((CUBE, rows, QH))], [wo, grad_even, grad_odd], room=3
    )[0]
    grads = call(
        functools.partial(attend_back_kernel, slots, ng),
        [bf((CUBE, rows, QH)), f32(MB, extent, 2 * HD)] + [bf((MB, extent, 2 * HD))] * (ng - 1),
        [q] + kvs + [ot, lse, grad_heads],
        scratch=[vm((extent, 2 * HD), BF16)],
        room=12,
    )
    gq, gkv, grads = grads[0], grads[1], grads[2:]
    gq, gkv, grads, grad_even, grad_odd, out_sums, dn_got, dn_mine = fence(
        gq, gkv, grads, grad_even, grad_odd, out_sums, dn_got, dn_mine
    )
    out_got = spread(out_sums)
    gkv_others = [links.climb(grads[step - 1], -step) for step in range(1, ng)]
    wo_weight = call(
        out_grad_kernel,
        [hbm((D, OUT_SLAB))],
        [grad_even, grad_odd, att, nge, ngo],
        scratch=[vm((half_rows, QH), BF16), vm((half_rows, QH), BF16)],
        room=3,
        busy=20,
    )[0]
    dn_kept = fold(dn_mine, dn_got)
    gkv_others, gq, gkv, out_got, wo_weight, dn_kept = fence(
        gkv_others, gq, gkv, out_got, wo_weight, dn_kept
    )
    dn_groups = send_groups(dn_kept)
    gqkv, even, odd = call(
        functools.partial(close_kernel, ng),
        [bf((out_rows, SLAB)), bf((half_rows, D)), bf((half_rows, D))],
        [gq, wq, gkv] + list(gkv_others),
        room=3,
    )
    odd, gqkv, even = fence(odd, gqkv, even)
    odd_got = links.core(odd)
    gu_kept = fold(gu_mine, gu_got)
    qkvo_other, qkvo_mine = call(
        qkv_grad_kernel,
        [bf((D // 2, SLAB + OUT_SLAB))] * 2,
        [xg, gqkv, wo_weight],
        room=3,
    )
    odd_got, gu_kept, even, dn_groups = fence(odd_got, gu_kept, even, dn_groups)
    gu_groups = send_groups(gu_kept)
    qkvo_got = links.outer(qkvo_other, 1, 0)
    sums = pair(even, odd_got)
    got = spread(sums)
    qkvo_kept = fold(qkvo_mine, qkvo_got)
    sums, got, qkvo_kept = fence(sums, got, qkvo_kept)
    qkvo_groups = send_groups(qkvo_kept)
    grad_tokens = call(
        tokens_kernel, [bf((rows, D))], [sums[0]] + list(got) + [tok, grad_mixed, gain1]
    )[0]
    gu_groups, grad_tokens = fence(gu_groups, grad_tokens)
    moe_sum = call(
        functools.partial(fold_last_kernel, ng),
        [bf((CUBE * wr, 3 * HALF))],
        list(gu_groups) + list(dn_groups),
        room=2,
    )[0]
    expert_parts = links.swap(moe_sum.reshape(CUBE, wr, 3 * HALF))
    cuts = call(
        functools.partial(fold_parts_kernel, ng),
        [bf((wr, SLAB + OUT_SLAB))] * CUBE,
        qkvo_groups,
        scratch=[vm((CUBE, wr, SLAB + OUT_SLAB), BF16)],
        room=2,
    )
    qkvo_parts = [cuts[0]] + [links.cube(cuts[k], k) for k in range(1, CUBE)]
    output = call(output_kernel, [bf((rows, D))], [out_sums[0]] + list(out_got) + [mixed])[0]
    grad_qkv, grad_attn_gain, grad_out, grad_router = call(
        finish_attention_kernel,
        [f32(wr, QW + 2 * KW), f32(1, wr), f32(wr, QW), f32(8, wr)],
        [qkv_weight, attn_gain.reshape(1, wr)] + qkvo_parts,
        scratch=[vm((CUBE, wr, SLAB + OUT_SLAB), BF16)],
        room=3,
    )
    grad_gateup, grad_moe_gain, grad_down = call(
        finish_experts_kernel,
        [f32(E, wr, 2 * FF), f32(1, wr), f32(E, wr, FF)],
        [expert_parts, gateup_weight, grad_router, router.T, moe_gain.reshape(1, wr)],
        room=3,
    )
    return (
        output.reshape(MB, 1, slots, D),
        grad_tokens.reshape(MB, 1, slots, D),
        grad_attn_gain.reshape(wr),
        grad_qkv,
        grad_out.T,
        grad_moe_gain.reshape(wr),
        grad_router[:E].T,
        grad_gateup,
        grad_down.transpose(0, 2, 1),
    )


def solution(mesh):
    in_specs = (
        P(None, "dp", "ctx", None),
        P(None, "dp"),
        P(None, "dp", "ctx", None),
        P(None, "dp", "ctx", None),
        P(("dp", "ctx")),
        P(("dp", "ctx"), None),
        P(None, ("dp", "ctx")),
        P(("dp", "ctx")),
        P(("dp", "ctx"), None),
        P(None, ("dp", "ctx"), None),
        P(None, None, ("dp", "ctx")),
    )
    out_specs = (
        P(None, "dp", "ctx", None),
        P(None, "dp", "ctx", None),
        P(("dp", "ctx")),
        P(("dp", "ctx"), None),
        P(None, ("dp", "ctx")),
        P(("dp", "ctx")),
        P(("dp", "ctx"), None),
        P(None, ("dp", "ctx"), None),
        P(None, None, ("dp", "ctx")),
    )
    return jax.shard_map(body, mesh=mesh, in_specs=in_specs, out_specs=out_specs, check_vma=False)
```

```python
import functools
import math

import jax
import jax.numpy as jnp
from jax import lax
from jax.experimental import pallas as pl
from jax.experimental.pallas import tpu as pltpu
from jax.sharding import PartitionSpec as P

D = 1536
H = 24
KVH = 8
HD = 64
FF = 1024
E = 4
MB = 2
QW = 1536
KW = 512
CUBE = 8
GROUP = H // KVH
HALF = FF // 2
QH = GROUP * HD
SHARD = QH + 2 * HD
SLAB = 384
OUT_SLAB = 256
PAIR = 2 * QH
EXTRA = 128
WIDE = D + EXTRA
ORDER = (0, 4, 2, 6, 1, 5, 3, 7)
LOG2E = 1.4426950408889634
F32 = jnp.float32
BF16 = jnp.bfloat16
NN = (((1,), (0,)), ((), ()))
NT = (((1,), (1,)), ((), ()))
TN = (((0,), (0,)), ((), ()))
AXES = ("dp", "ctx")


def dot(left, right, dims=NN):
    return lax.dot_general(left, right, dims, preferred_element_type=F32)


class Kernels:
    def __init__(self, lengths):
        self.lengths = lengths

    def __call__(self, kernel, outs, ins, far=(), scratch=(), room=0, after=(), busy=0):
        ins, far, after = list(ins), list(far), list(after)
        n_in, n_after = 1 + len(ins) + len(far), len(after)
        vmem = pl.BlockSpec(memory_space=pltpu.VMEM)
        anywhere = pl.BlockSpec(memory_space=pl.ANY)

        def run(lengths, *refs):
            ctx = lax.axis_index("ctx")
            scal = [lax.axis_index("dp"), ctx >> 3, ctx & 7, lengths[0, 0], lengths[1, 0]]
            kernel(scal, *refs[: n_in - 1], *refs[n_in - 1 + n_after :])

        moved = sum(math.prod(a.shape) * a.dtype.itemsize for a in ins + list(outs))
        held = sum(2 * math.prod(s.shape) for s in scratch if hasattr(s, "shape"))
        grant = int(1.1 * moved) + held + (room + 4) * 1024 * 1024
        results = pl.pallas_call(
            run,
            out_shape=list(outs),
            in_specs=[pl.BlockSpec(memory_space=pltpu.SMEM)]
            + [vmem] * len(ins)
            + [anywhere] * (len(far) + n_after),
            out_specs=[vmem] * len(outs),
            scratch_shapes=list(scratch),
            compiler_params=pltpu.CompilerParams(vmem_limit_bytes=min(grant, 56 * 1024 * 1024)),
            cost_estimate=pl.CostEstimate(
                flops=1000 + busy * 10**9, bytes_accessed=1000, transcendentals=0
            ),
        )(
            self.lengths,
            *ins,
            *[pltpu.with_memory_space_constraint(value, pltpu.HBM) for value in far],
            *after,
        )
        return results


def sems(count):
    return pltpu.SemaphoreType.DMA((count,))


def shape(dims, dtype=BF16):
    return jax.ShapeDtypeStruct(dims, dtype)


class Links:
    def __init__(self, nx, nc):
        self.nx, self.nc, self.ng = nx, nc, nc // CUBE

    def _pairs(self, move):
        pairs = []
        for x in range(self.nx):
            for g in range(self.ng):
                for t in range(CUBE):
                    goal = move(x, g, t)
                    if goal is not None:
                        gx, gg, gt = goal
                        pairs.append((x * self.nc + g * CUBE + t, gx * self.nc + gg * CUBE + gt))
        return pairs

    def cube(self, value, bits):
        return lax.ppermute(value, AXES, self._pairs(lambda x, g, t: (x, g, t ^ bits)))

    def outer(self, value, dx, dg):
        return lax.ppermute(value, AXES, self._pairs(lambda x, g, t: (x ^ dx, g ^ dg, t)))

    def climb(self, value, step):
        def move(x, g, t):
            return (x, g + step, t) if 0 <= g + step < self.ng else None

        return lax.ppermute(value, AXES, self._pairs(move))

    def cubes(self):
        return [
            [x * self.nc + g * CUBE + t for t in range(CUBE)]
            for x in range(self.nx)
            for g in range(self.ng)
        ]

    def swap(self, value):
        return lax.all_to_all(
            value, AXES, split_axis=0, concat_axis=0, tiled=True, axis_index_groups=self.cubes()
        )

    def swap_all(self, value):
        return lax.all_to_all(value, AXES, split_axis=0, concat_axis=0, tiled=True)

    def near(self, rows):
        return [self.cube(rows, bits) for bits in ORDER[1:4]]

    def core(self, rows):
        return self.cube(rows, 1)

    def cores(self):
        return [list(range(core, self.nx * self.nc, 2)) for core in range(2)]

    def outers(self):
        return [
            [x * self.nc + g * CUBE + t for x in range(self.nx) for g in range(self.ng)]
            for t in range(CUBE)
        ]

    def outer_direct(self, rows):
        return [rows] + [
            self.outer(rows, dx, dg)
            for dx in range(self.nx)
            for dg in range(self.ng)
            if dx or dg
        ]


def fence(*values):
    return lax.optimization_barrier(values)


def stack_copies(refs, out, sem):
    rows = refs[0].shape[0]
    return [
        pltpu.make_async_copy(ref, out.at[pl.ds(n * rows, rows)], sem.at[n])
        for n, ref in enumerate(refs)
    ]


def outer_copies(refs, out, sem, scal, ng):
    rows = refs[0].shape[0]
    copies = []
    for j, ref in enumerate(refs):
        place = (scal[0] ^ (j // ng)) * ng + (scal[1] ^ (j % ng))
        spot = pl.ds(pl.multiple_of(place * rows, 16), rows)
        copies.append(pltpu.make_async_copy(ref, out.at[spot], sem.at[j]))
    return copies


def start_all(copies):
    for copy in copies:
        copy.start()


def wait_all(copies):
    for copy in copies:
        copy.wait()


def prep_kernel(scal, w_ref, gain_ref, tok_ref, routes_ref, out_ref, tok_out):
    wr = w_ref.shape[0]
    fill = column(gain_ref, SLAB - SHARD).astype(BF16)
    for k in range(CUBE):
        out_ref[k] = jnp.concatenate(
            [
                w_ref[:, k * QH : (k + 1) * QH],
                w_ref[:, QW + k * HD : QW + (k + 1) * HD],
                w_ref[:, QW + KW + k * HD : QW + KW + (k + 1) * HD],
                fill,
            ],
            axis=1,
        )
    rows = tok_ref.shape[0]
    tok_out[:, :D] = tok_ref[...]
    lane = lax.broadcasted_iota(jnp.int32, (rows, EXTRA), 1)
    names = jnp.where(lane == 0, routes_ref[:, 0:1], routes_ref[:, 1:2])
    tok_out[:, D:] = names.astype(F32).astype(BF16)


def column(row_ref, width):
    return jnp.broadcast_to(row_ref[...].astype(F32), (width, row_ref.shape[1])).T


def as_row(values):
    return jnp.broadcast_to(values, (values.shape[0], EXTRA)).T[0:1, :]


def prep_out_kernel(scal, wo_ref, rt_ref, gain_ref, wo_out):
    wr = wo_ref.shape[0]
    rt = rt_ref[...].astype(F32)
    rows = jnp.concatenate(
        [rt, rt, gain_ref[...].astype(F32), jnp.zeros((EXTRA - 2 * E - 1, wr), F32)], axis=0
    )
    wo_out[0, :, :QW] = wo_ref[...]
    wo_out[0, :, QW:] = rows.T.astype(BF16)


def order_kernel(ng, n_outer, scal, even_ref, odd_ref, out_ref):
    for q, k in enumerate(ORDER):
        source = even_ref if q < 4 else odd_ref
        for j in range(n_outer):
            group = (scal[0] ^ (j // ng)) * ng + (scal[1] ^ (j % ng))
            out_ref[group * CUBE + (scal[2] ^ k)] = source[(q % 4) * n_outer + j]


def prep_experts_kernel(scal, gu_ref, dn_ref, moe_out):
    for k in range(CUBE):
        e, h = k // 2, k % 2
        moe_out[k, :, :HALF] = gu_ref[e, :, h * HALF : (h + 1) * HALF]
        moe_out[k, :, HALF : 2 * HALF] = gu_ref[e, :, FF + h * HALF : FF + (h + 1) * HALF]
        moe_out[k, :, 2 * HALF :] = dn_ref[e, :, h * HALF : (h + 1) * HALF]


def split_kernel(scal, both_ref, gu_ref, dn_ref):
    gu_ref[...] = both_ref[:, : 2 * HALF]
    dn_ref[...] = both_ref[:, 2 * HALF :]


def pack_kernel(scal, *refs):
    rows = refs[0].shape[0]
    for n, ref in enumerate(refs[:-1]):
        refs[-1][n * rows : (n + 1) * rows, :] = ref[...]


def qkv_kernel(ng, n_outer, scal, even_ref, odd_ref, *refs):
    t = scal[2]
    weights, (xg, q_out, kv_out, gain_ref, w_ref, sem) = refs[:n_outer], refs[n_outer:]
    copies = outer_copies(weights, w_ref, sem, scal, ng)
    start_all(copies)
    wait_all(copies)
    rows = even_ref.shape[0] // 4
    slots = rows // MB
    blank = jnp.zeros((slots, HD), BF16)
    gain = w_ref[:, 256:].astype(F32).T[SHARD - 256 : SHARD - 248, :]
    gain_ref[...] = gain
    gain = gain[0:1]
    for p, k in enumerate(ORDER):
        source = even_ref if p < 4 else odd_ref
        values = source[(p % 4) * rows : (p % 4 + 1) * rows, :D].astype(F32)
        scale = lax.rsqrt(jnp.mean(values * values, axis=-1, keepdims=True) + 1e-05)
        packed = (values * scale * gain).astype(BF16)
        xg[p * rows : (p + 1) * rows, :] = packed
        y = dot(packed, w_ref[...]).astype(BF16)
        for m in range(MB):
            part = y[m * slots : (m + 1) * slots]
            spot = pl.ds(pl.multiple_of((t ^ k) * slots, 64), slots)
            for h in range(GROUP):
                q_out[m, h, spot, :] = jnp.concatenate(
                    [part[:, h * HD : (h + 1) * HD], blank], axis=1
                )
            kv_out[m, spot, :] = part[:, QH:SHARD]


def key_bias(extent, g, step, length):
    local = lax.broadcasted_iota(jnp.int32, (extent, 1), 0)
    seen = ((g - step) * extent + local < length) & (g >= step)
    return jnp.where(seen, 0.0, -1e30).astype(F32)


def causal_bias(extent):
    keys = lax.broadcasted_iota(jnp.int32, (extent, extent), 0)
    rows = lax.broadcasted_iota(jnp.int32, (extent, extent), 1)
    return jnp.where(keys <= rows, 0.0, -1e30).astype(F32)


def attend_kernel(slots, scal, *refs):
    g = scal[1]
    n_keys = len(refs) - 4
    q_ref, kv_refs, (att_ref, ot_ref, lse_ref) = refs[0], refs[1 : 1 + n_keys], refs[1 + n_keys :]
    extent = q_ref.shape[2]
    causal = causal_bias(extent)
    for m in range(MB):
        length = scal[3 + m]
        biases = [key_bias(extent, g, s, length) for s in range(n_keys)]
        for h in range(GROUP):
            q = q_ref[m, h]
            top = total = acc = None
            for s in range(n_keys):
                kv = kv_refs[s][m]
                st = dot(kv, q, NT) * (0.125 * LOG2E) + biases[s]
                if s == 0:
                    st = st + causal
                peak = jnp.max(st, axis=0, keepdims=True)
                if s == 0:
                    pt = jnp.exp2(st - peak)
                    top, total = peak, jnp.sum(pt, axis=0, keepdims=True)
                    acc = dot(kv, pt.astype(BF16), TN)
                else:
                    fresh = jnp.maximum(top, peak)
                    scale = jnp.exp2(top - fresh)
                    pt = jnp.exp2(st - fresh)
                    total = total * scale + jnp.sum(pt, axis=0, keepdims=True)
                    acc = acc * scale + dot(kv, pt.astype(BF16), TN)
                    top = fresh
            ot = acc[HD:, :] / total
            ot_ref[m, h] = ot
            lse_ref[m, h : h + 1, :] = top + jnp.log2(total)
            o = ot.T.astype(BF16)
            for k in range(CUBE):
                place = (k // 4) * QH + h * HD
                base = (k % 4) * MB * slots + m * slots
                att_ref[base : base + slots, place : place + HD] = o[k * slots : (k + 1) * slots]


def row_valid(scal, rows):
    slots = rows // MB
    spot = lax.broadcasted_iota(jnp.int32, (rows, 1), 0)
    place = (scal[1] * CUBE + scal[2]) * slots
    length = jnp.where(spot < slots, scal[3], scal[4])
    inner = jnp.where(spot < slots, spot, spot - slots)
    return jnp.where(place + inner < length, 1.0, 0.0).astype(F32)


def gain_row(rest):
    return rest.astype(F32).T[2 * E : 2 * E + 1, :]


def att_block(ref, base, rows, j):
    spot = pl.ds(pl.multiple_of(base + (j & 3) * rows, 16), rows)
    both = ref[spot, :]
    return jnp.where(j >= 4, both[:, QH:], both[:, :QH])


def mix_kernel(scal, even_ref, odd_ref, toke_ref, toko_ref, wo_ref, *refs):
    t = scal[2]
    nge, ngo, mixed_ref, comb_ref, att = refs
    rows = mixed_ref.shape[0]
    slots = rows // MB
    for q in range(4):
        head = t ^ ORDER[q]
        lanes = pl.ds(pl.multiple_of((head >> 1) * PAIR, 128), PAIR)
        for p, k in enumerate(ORDER):
            low = att_block(even_ref, q * 4 * rows, rows, t ^ k)
            high = att_block(odd_ref, q * 4 * rows, rows, t ^ k)
            flip = (head & 1) == 1
            att[p * rows : (p + 1) * rows, lanes] = jnp.concatenate(
                [jnp.where(flip, high, low), jnp.where(flip, low, high)], axis=1
            )
    rest = wo_ref[:, QW:]
    gain = gain_row(rest)
    lane = lax.broadcasted_iota(jnp.int32, (2 * rows, EXTRA), 1)
    spot = lax.broadcasted_iota(jnp.int32, (2 * rows, 1), 0)
    inner = spot & (rows - 1)
    second = inner >= slots
    length = jnp.where(second, scal[4], scal[3])
    slot = jnp.where(second, inner - slots, inner)
    for p in range(0, CUBE, 2):
        tok_ref, out_ref = (toke_ref, nge) if p < 4 else (toko_ref, ngo)
        local = slice((p % 4) * rows, (p % 4 + 2) * rows)
        owner = jnp.where(spot < rows, t ^ ORDER[p], t ^ ORDER[p + 1])
        place = (scal[1] * CUBE + owner) * slots + slot
        valid = jnp.where(place < length, 1.0, 0.0).astype(F32)
        branch = dot(att[p * rows : (p + 2) * rows, :], wo_ref[:, :QW], NT)
        mixed = tok_ref[local, :D].astype(F32) + valid * branch
        scale = lax.rsqrt(jnp.mean(mixed * mixed, axis=-1, keepdims=True) + 1e-05)
        low = (mixed * scale * gain).astype(BF16)
        logits = dot(low, rest)
        names = tok_ref[local, D:].astype(F32)
        expert = (lane & (E - 1)).astype(F32)
        chosen = ((expert == names[:, 0:1]) | (expert == names[:, 1:2])) & (lane < 2 * E)
        peak = jnp.max(jnp.where(chosen, logits, -3e38), axis=-1, keepdims=True)
        expo = jnp.where(chosen, jnp.exp(logits - peak), 0.0)
        comb = expo / (0.5 * jnp.sum(expo, axis=-1, keepdims=True))
        if p == 0:
            mixed_ref[...] = mixed[:rows]
            comb_ref[...] = jnp.where(lane < E, comb, 0.0)[:rows]
        comb = comb * valid
        high = comb.astype(BF16)
        tail = (comb - high.astype(F32)).astype(BF16)
        out_ref[local, :D] = low
        out_ref[local, D:] = jnp.where(lane < E, high, tail)


def row_valid(scal, rows):
    slots = rows // MB
    spot = lax.broadcasted_iota(jnp.int32, (rows, 1), 0)
    place = (scal[1] * CUBE + scal[2]) * slots
    length = jnp.where(spot < slots, scal[3], scal[4])
    inner = jnp.where(spot < slots, spot, spot - slots)
    return jnp.where(place + inner < length, 1.0, 0.0).astype(F32)


def cot_kernel(ng, n_outer, scal, even_ref, odd_ref, *refs):
    dn_blocks, (q_ref, w_dn, sem) = refs[:n_outer], refs[n_outer:]
    copies = outer_copies(dn_blocks, w_dn, sem, scal, ng)
    start_all(copies)
    wait_all(copies)
    step = even_ref.shape[0] // 2
    for part, source in enumerate((even_ref, odd_ref)):

        @pl.loop(0, 2)
        def _(i):
            local = pl.ds(pl.multiple_of(i * step, 128), step)
            spot = pl.ds(pl.multiple_of((2 * part + i) * step, 128), step)
            q_ref[spot, :] = dot(source[local, :], w_dn[...])


def own_share(wide, scal):
    lane = lax.broadcasted_iota(jnp.int32, wide.shape, 1)
    expert = scal[2] // 2
    mine = (lane == expert) | (lane == expert + E)
    return jnp.sum(jnp.where(mine, wide.astype(F32), 0.0), axis=-1, keepdims=True)


def expert_kernel(base, ng, n_outer, scal, ngw, q_ref, *refs):
    if base:
        blocks, (act_ref, ggu_ref, out_ref, w_ref, sem) = refs[:n_outer], refs[n_outer:]
        copies = outer_copies(blocks, w_ref, sem, scal, ng)
        start_all(copies)
        wait_all(copies)
    else:
        w_ref, act_ref, ggu_ref, out_ref = refs
    step = ngw.shape[0] // 2
    expert = scal[2] // 2

    @pl.loop(0, 2)
    def _(i):
        spot = pl.ds(pl.multiple_of(i * step, 128), step)
        share = own_share(ngw[spot, D:], scal)
        gu = dot(ngw[spot, :D], w_ref[...])
        gate, up = gu[:, :HALF], gu[:, HALF:]
        sig = 1.0 / (1.0 + jnp.exp(-gate))
        soft = gate * sig
        act = (soft * up).astype(BF16)
        act_ref[spot, :] = act
        back = q_ref[pl.ds(pl.multiple_of(base + i * step, 128), step), :]
        dots = jnp.sum(act.astype(F32) * back, axis=-1, keepdims=True)
        back = back * share
        ggu_ref[spot, :HALF] = (back * up * (sig * (1.0 + gate * (1.0 - sig)))).astype(BF16)
        ggu_ref[spot, HALF:] = (back * soft).astype(BF16)
        out_ref[spot, :D] = dot(ggu_ref[spot, :], w_ref[...], NT).astype(BF16)
        high = dots.astype(BF16)
        rest = (dots - high.astype(F32)).astype(BF16)
        lane = lax.broadcasted_iota(jnp.int32, (step, EXTRA), 1)
        out_ref[spot, D:] = jnp.where(
            lane == expert, high, jnp.where(lane == expert + E, rest, jnp.zeros_like(rest))
        )


def expert_grad_kernel(
    scal, dye, dyo, nge, ngo, acte, acto, ggue, gguo, gu_other, dn_other, gu_mine, dn_mine, cae, cao
):
    for wide, act, out in ((nge, acte, cae), (ngo, acto, cao)):
        out[...] = (act[...].astype(F32) * own_share(wide[:, D:], scal)).astype(BF16)
    cut = D // 6
    for flip, gu_ref, dn_ref in ((1, gu_other, dn_other), (0, gu_mine, dn_mine)):

        @pl.loop(0, 3)
        def _(i):
            cols = pl.ds(pl.multiple_of((scal[0] ^ flip) * (D // 2) + i * cut, 128), cut)
            spot = pl.ds(pl.multiple_of(i * cut, 128), cut)
            total = dot(nge[:, cols], ggue[...], TN) + dot(ngo[:, cols], gguo[...], TN)
            gu_ref[spot, :] = total.astype(BF16)
            total = dot(dye[:, cols], cae[...], TN) + dot(dyo[:, cols], cao[...], TN)
            dn_ref[spot, :] = total.astype(BF16)


def expert_out_kernel(scal, w_ref, nge, ngo, acte, acto, even_ref, odd_ref):
    step = acte.shape[0] // 2
    for wide, act, out_ref in ((nge, acte, even_ref), (ngo, acto, odd_ref)):

        @pl.loop(0, 2)
        def _(i):
            spot = pl.ds(pl.multiple_of(i * step, 128), step)
            share = own_share(wide[spot, D:], scal)
            out_ref[spot, :] = (dot(act[spot, :], w_ref[...], NT) * share).astype(BF16)


def fold_kernel(ng, scal, mine_ref, got_ref, *refs):
    rows = mine_ref.shape[0] // ng
    for dg, out in enumerate(refs):
        spot = pl.ds(pl.multiple_of((scal[1] ^ dg) * rows, 16), rows)
        total = mine_ref[spot, :].astype(F32) + got_ref[spot, :].astype(F32)
        out[...] = total.astype(out.dtype)


def fold_last_kernel(n_in, scal, *refs):
    base = 0
    for ins in (refs[:n_in], refs[n_in:-1]):
        total = ins[0][...]
        for ref in ins[1:]:
            total = total + ref[...].astype(F32)
        refs[-1][:, base : base + total.shape[1]] = total.astype(BF16)
        base += total.shape[1]


def fold_parts_kernel(n_in, scal, *refs):
    ins, outs = refs[:n_in], refs[n_in:]
    wr = outs[0].shape[0]
    for j in range(CUBE):
        spot = slice(j * wr, (j + 1) * wr)
        total = ins[0][spot, :]
        for ref in ins[1:]:
            total = total + ref[spot, :].astype(F32)
        outs[-1][j] = total.astype(BF16)
    for k, out in enumerate(outs[:-1]):
        out[...] = outs[-1][scal[2] ^ k]


def pair_kernel(scal, even_ref, odd_ref, *outs):
    rows = outs[0].shape[0]
    for p, out in enumerate(outs):
        spot = slice(p * rows, (p + 1) * rows)
        out[...] = (even_ref[spot, :].astype(F32) + odd_ref[spot, :].astype(F32)).astype(BF16)


def norm_back(grad, values, scale):
    unit = values * scale
    return scale * (grad - unit * jnp.mean(grad * unit, axis=-1, keepdims=True))


def turn_kernel(scal, a0, a1, a2, a3, mixed_ref, cot_ref, comb_ref, wo_ref, grad_ref, wide_ref):
    rest = wo_ref[:, QW:]
    rows = mixed_ref.shape[0]
    total = (
        a0[...].astype(F32) + a1[...].astype(F32) + a2[...].astype(F32) + a3[...].astype(F32)
    )
    valid = row_valid(scal, rows)
    lane = lax.broadcasted_iota(jnp.int32, (rows, EXTRA), 1)
    dots = total[:, D:]
    dots = (dots + pltpu.roll(dots, EXTRA - E, 1)) * valid
    comb = comb_ref[...]
    inner = jnp.sum(comb * dots, axis=-1, keepdims=True)
    grad_logits = jnp.where(lane < E, comb * (dots - inner), 0.0).astype(BF16)
    grad_normed = (total[:, :D] + dot(grad_logits, rest, NT)) * gain_row(rest)
    mixed = mixed_ref[...]
    scale = lax.rsqrt(jnp.mean(mixed * mixed, axis=-1, keepdims=True) + 1e-05)
    grad_mixed = cot_ref[...].astype(F32) + norm_back(grad_normed, mixed, scale)
    grad_ref[...] = grad_mixed
    branch = (valid * grad_mixed).astype(BF16)
    wide_ref[:, :D] = branch
    wide_ref[:, D:] = grad_logits


def grad_rows_kernel(scal, w_ref, even_ref, odd_ref, ga_ref):
    t = scal[2]
    rows = ga_ref.shape[1]
    window = w_ref[:, pl.ds(pl.multiple_of(((3 * t) >> 1) * 128, 128), 256)]
    weight = jnp.where((t & 1) == 1, window[:, HD:], window[:, :QH])
    for part, wide in enumerate((even_ref, odd_ref)):
        for n in range(2):
            spot = slice(2 * n * rows, 2 * (n + 1) * rows)
            grad = dot(wide[spot, :D], weight).astype(BF16)
            for i in range(2):
                ga_ref[t ^ ORDER[4 * part + 2 * n + i]] = grad[i * rows : (i + 1) * rows]


def attend_back_kernel(slots, n_keys, scal, *refs):
    g = scal[1]
    q_ref, kv_refs, refs = refs[0], refs[1 : 1 + n_keys], refs[1 + n_keys :]
    ot_ref, lse_ref, ga_ref, gq_ref, refs = refs[0], refs[1], refs[2], refs[3], refs[4:]
    gkv_refs, (do_ref,) = refs[:n_keys], refs[n_keys:]
    extent = q_ref.shape[2]
    causal = causal_bias(extent)
    blank = jnp.zeros((slots, HD), BF16)
    for m in range(MB):
        length = scal[3 + m]
        biases = [key_bias(extent, g, s, length) for s in range(n_keys)]
        sums = [None] * n_keys
        for h in range(GROUP):
            for k in range(CUBE):
                part = ga_ref[k, m * slots : (m + 1) * slots, h * HD : (h + 1) * HD]
                do_ref[k * slots : (k + 1) * slots, :] = jnp.concatenate([blank, part], axis=1)
            q = q_ref[m, h]
            do = do_ref[...]
            dot_t = do.astype(F32).T[HD:, :]
            delta = jnp.sum(dot_t * ot_ref[m, h], axis=0, keepdims=True)
            lse = lse_ref[m, h : h + 1, :]
            grad_q = None
            for s in range(n_keys):
                kv = kv_refs[s][m]
                st = dot(kv, q, NT) * (0.125 * LOG2E) + biases[s]
                if s == 0:
                    st = st + causal
                pt = jnp.exp2(st - lse)
                dpt = dot(kv, do, NT)
                dst = (pt * (dpt - delta) * 0.125).astype(BF16)
                part = dot(dst, q) + dot(pt.astype(BF16), do)
                sums[s] = part if sums[s] is None else sums[s] + part
                part = dot(kv, dst, TN)
                grad_q = part if grad_q is None else grad_q + part
            gq = grad_q[:HD, :].T.astype(BF16)
            for k in range(CUBE):
                gq_ref[k, m * slots : (m + 1) * slots, h * HD : (h + 1) * HD] = gq[
                    k * slots : (k + 1) * slots
                ]
        for s in range(n_keys):
            gkv_refs[s][m] = sums[s].astype(gkv_refs[s].dtype)


def close_kernel(n_keys, scal, gq_ref, w_ref, own_ref, *refs):
    t = scal[2]
    others, (gqkv, even_ref, odd_ref) = refs[: n_keys - 1], refs[n_keys - 1 :]
    rows = gq_ref.shape[1]
    slots = rows // MB
    gqkv[:, SHARD:] = jnp.zeros((CUBE * rows, SLAB - SHARD), BF16)
    for p, k in enumerate(ORDER):
        gqkv[p * rows : (p + 1) * rows, :QH] = gq_ref[t ^ k]
        for m in range(MB):
            spot = pl.ds(pl.multiple_of((t ^ k) * slots, 64), slots)
            total = own_ref[m, spot, :]
            for other in others:
                total = total + other[m, spot, :].astype(F32)
            base = p * rows + m * slots
            gqkv[base : base + slots, QH:SHARD] = total.astype(BF16)
    step = 2 * rows
    for part, out_ref in enumerate((even_ref, odd_ref)):

        @pl.loop(0, 2)
        def _(i):
            local = pl.ds(pl.multiple_of(i * step, 128), step)
            spot = pl.ds(pl.multiple_of(part * 2 * step + i * step, 128), step)
            out_ref[local, :] = dot(gqkv[spot, :], w_ref[...], NT).astype(BF16)


def qkv_grad_kernel(scal, xg, gqkv, wo_ref, other_ref, mine_ref):
    cut = D // 6
    for flip, out_ref in ((1, other_ref), (0, mine_ref)):

        @pl.loop(0, 3)
        def _(i):
            cols = pl.ds(pl.multiple_of((scal[0] ^ flip) * (D // 2) + i * cut, 128), cut)
            spot = pl.ds(pl.multiple_of(i * cut, 128), cut)
            out_ref[spot, :SLAB] = dot(xg[:, cols], gqkv[...], TN).astype(BF16)
            out_ref[spot, SLAB:] = wo_ref[cols, :]


def out_grad_kernel(scal, ge_ref, go_ref, att_ref, nge, ngo, w_out, ate, ato):
    rows = ge_ref.shape[0] // 4
    for p, k in enumerate(ORDER):
        out = ate if p < 4 else ato
        out[(p % 4) * rows : (p % 4 + 1) * rows, :] = att_block(att_ref, 0, rows, scal[2] ^ k)
    cut = D // 4

    @pl.loop(0, 4)
    def _(i):
        cols = pl.ds(pl.multiple_of(i * cut, 128), cut)
        total = dot(ge_ref[:, cols], ate[...], TN) + dot(go_ref[:, cols], ato[...], TN)
        w_out[cols, :QH] = total.astype(BF16)
        low = dot(nge[:, cols], ge_ref[:, D:], TN) + dot(ngo[:, cols], go_ref[:, D:], TN)
        w_out[cols, QH:] = low[:, : OUT_SLAB - QH].astype(BF16)


def finish_attention_kernel(scal, w_ref, gain_ref, *refs):
    parts, (out_ref, gain_out, wo_out, rt_out, got) = refs[:CUBE], refs[CUBE:]
    for k, ref in enumerate(parts):
        got[scal[2] ^ k] = ref[...]
    for k in range(CUBE):
        part = got[k].astype(F32)
        out_ref[:, k * QH : (k + 1) * QH] = part[:, :QH]
        out_ref[:, QW + k * HD : QW + (k + 1) * HD] = part[:, QH : QH + HD]
        out_ref[:, QW + KW + k * HD : QW + KW + (k + 1) * HD] = part[:, QH + HD : SHARD]
        wo_out[:, k * QH : (k + 1) * QH] = part[:, SLAB : SLAB + QH]
        if k == 0:
            rt_out[...] = part[:, SLAB + EXTRA :].T[QH - EXTRA : QH - EXTRA + 8]
    total = jnp.sum(out_ref[...] * w_ref[...].astype(F32), axis=-1, keepdims=True)
    gain_out[...] = as_row(total) / gain_ref[...].astype(F32)


def finish_experts_kernel(
    scal, got, w_ref, rg_ref, rt_ref, gain_ref, out_ref, gain_out, dn_out
):
    total = jnp.zeros((out_ref.shape[1], 1), F32)
    for k in range(CUBE):
        e, h = k // 2, k % 2
        for at, base in ((h * HALF, 0), (FF + h * HALF, HALF)):
            part = got[k, :, base : base + HALF].astype(F32)
            out_ref[e, :, at : at + HALF] = part
            weight = w_ref[e, :, at : at + HALF].astype(F32)
            total = total + jnp.sum(part * weight, axis=-1, keepdims=True)
        dn_out[e, :, h * HALF : (h + 1) * HALF] = got[k, :, 2 * HALF :].astype(F32)
    router = jnp.sum(rg_ref[:E] * rt_ref[...].astype(F32), axis=0, keepdims=True)
    gain_out[...] = (as_row(total) + router) / gain_ref[...].astype(F32)


def output_kernel(scal, a0, a1, a2, a3, mixed_ref, out_ref):
    total = (
        a0[...].astype(F32) + a1[...].astype(F32) + a2[...].astype(F32) + a3[...].astype(F32)
    )
    out_ref[...] = (mixed_ref[...] + total).astype(BF16)


def tokens_kernel(scal, a0, a1, a2, a3, x_ref, grad_ref, gain_ref, out_ref):
    total = (
        a0[...].astype(F32) + a1[...].astype(F32) + a2[...].astype(F32) + a3[...].astype(F32)
    )
    x = x_ref[...].astype(F32)
    scale = lax.rsqrt(jnp.mean(x * x, axis=-1, keepdims=True) + 1e-05)
    out_ref[...] = (grad_ref[...] + norm_back(total * gain_ref[0:1, :], x, scale)).astype(BF16)


def body(
    tokens,
    lengths,
    routes,
    cotangent,
    attn_gain,
    qkv_weight,
    out_weight,
    moe_gain,
    router,
    gateup_weight,
    down_weight,
):
    nx, nc = lax.axis_size("dp"), lax.axis_size("ctx")
    links = Links(nx, nc)
    ng = links.ng
    n_outer = nx * ng
    slots = tokens.shape[2]
    rows = MB * slots
    extent = CUBE * slots
    wr = attn_gain.shape[0]
    out_rows = CUBE * rows

    half_rows = out_rows // 2
    tok = tokens.reshape(rows, D)
    cot = cotangent.reshape(rows, D)
    call = Kernels(lengths)
    bf, vm = shape, pltpu.VMEM

    def hbm(dims, dtype=BF16):
        return pltpu.HBM(dims, dtype)

    def f32(*dims):
        return shape(dims, F32)

    def pair(even, got):
        return call(pair_kernel, [bf((rows, even.shape[1]))] * 4, [even, got])

    def spread(parts):
        return [links.cube(part, bits) for part, bits in zip(parts[1:], ORDER[1:4])]

    def fold(mine, got):
        part = (CUBE * wr, mine.shape[1])
        kept = call(
            functools.partial(fold_kernel, ng),
            [shape(part, F32)] + [bf(part)] * (ng - 1),
            [mine, got],
            room=2,
        )
        return list(kept)

    def send_groups(kept):
        return [kept[0]] + [links.outer(kept[dg], 0, dg) for dg in range(1, ng)]

    def pack(blocks):
        own = blocks[0].shape
        return call(pack_kernel, [bf((4 * own[0], own[1]))], blocks)[0]

    def pile(blocks):
        own = blocks[0].shape
        return call(pack_kernel, [bf((len(blocks) * own[0],) + own[1:])], blocks)[0]

    wq_parts, tok_wide = call(
        prep_kernel,
        [bf((CUBE, wr, SLAB)), bf((rows, WIDE))],
        [qkv_weight, attn_gain.reshape(1, wr), tok, routes.reshape(rows, 2)],
        room=3,
    )
    tok_wide, wq_parts, out_in = fence(tok_wide, wq_parts, out_weight.T)
    tok_near = links.near(tok_wide)
    wq_group = links.swap(wq_parts).reshape(CUBE * wr, SLAB)
    wo_part = call(
        prep_out_kernel,
        [bf((1, wr, WIDE))],
        [out_in, router.T, moe_gain.reshape(1, wr)],
        room=3,
        busy=20,
    )[0]
    wq_group, gateup_in, down_in = fence(
        wq_group, gateup_weight, down_weight.transpose(0, 2, 1)
    )
    moe_parts = call(
        prep_experts_kernel, [bf((CUBE, wr, 3 * HALF))], [gateup_in, down_in], room=3
    )[0]
    tok_wide, tok_near, wo_part = fence(tok_wide, tok_near, wo_part)
    tok_even = pack([tok_wide] + list(tok_near))
    tok_odd = links.core(tok_even)
    wq_far = [links.outer(wq_group, 0, dg) for dg in range(1, ng)]
    wo_far = [links.outer(wo_part, 0, dg) for dg in range(1, ng)]
    wq_blocks = [wq_group] + wq_far
    for dx in range(1, nx):
        wq_blocks += [links.outer(block, dx, 0) for block in wq_blocks[:ng]]
    moe_group = links.swap(moe_parts).reshape(CUBE * wr, 3 * HALF)
    tok_even, tok_odd, wq_blocks, moe_group, cot, wo_far = fence(
        tok_even, tok_odd, wq_blocks, moe_group, cot, wo_far
    )
    wo_row = pile([wo_part] + list(wo_far))
    wo_block = pile([wo_row] + [links.outer(wo_row, dx, 0) for dx in range(1, nx)])
    wo_even = pile([wo_block] + links.near(wo_block))
    xg, q, kv, gain1, wq = call(
        functools.partial(qkv_kernel, ng, n_outer),
        [
            hbm((out_rows, D)),
            bf((MB, GROUP, extent, 2 * HD)),
            bf((MB, extent, 2 * HD)),
            hbm((8, D), F32),
            hbm((D, SLAB)),
        ],
        [tok_even, tok_odd],
        wq_blocks,
        [sems(n_outer)],
        room=4,
    )
    gu_group, dn_group = call(
        split_kernel, [bf((CUBE * wr, 2 * HALF)), bf((CUBE * wr, HALF))], [moe_group]
    )
    dn_group, gu_group, cot = fence(dn_group, gu_group, cot)
    kvs = [links.climb(kv, step) for step in range(1, ng)]
    cot_near = links.near(cot)
    dn_far = [links.outer(dn_group, 0, dg) for dg in range(1, ng)]
    gu_side = [links.outer(gu_group, dx, 0) for dx in range(1, nx)]
    kv, kvs, dn_group, dn_far, gu_group, gu_side, cot, cot_near, wo_even = fence(
        kv, kvs, dn_group, dn_far, gu_group, gu_side, cot, cot_near, wo_even
    )
    wo_odd = links.core(wo_even)
    kvs = [kv] + list(kvs)
    cot_even = pack([cot] + list(cot_near))
    att, ot, lse = call(
        functools.partial(attend_kernel, slots),
        [bf((4 * rows, PAIR)), hbm((MB, GROUP, HD, extent), F32), hbm((MB, GROUP, extent), F32)],
        [q] + kvs,
        room=10,
    )
    cot_even, dn_group, dn_far, gu_group = fence(cot_even, dn_group, dn_far, gu_group)
    att_near = links.near(att)
    cot_odd = links.core(cot_even)
    dn_blocks = [dn_group] + list(dn_far)
    for dx in range(1, nx):
        dn_blocks += [links.outer(block, dx, 0) for block in dn_blocks[:ng]]
    gu_far = [links.outer(gu_group, 0, dg) for dg in range(1, ng)]
    att, att_near, cot_odd, dn_blocks, gu_far = fence(att, att_near, cot_odd, dn_blocks, gu_far)
    att_even = pack([att] + list(att_near))
    att_even, gu_far = fence(att_even, gu_far)
    att_odd = links.core(att_even)
    gu_blocks = [gu_group] + list(gu_far)
    for dx in range(1, nx):
        gu_blocks += [gu_side[dx - 1]] + [links.outer(block, dx, 0) for block in gu_far]
    wo = call(
        functools.partial(order_kernel, ng, n_outer),
        [bf((n_outer * CUBE, wr, WIDE))],
        [wo_even, wo_odd],
        room=2,
    )[0].reshape(D, WIDE)
    back, w_dn = call(
        functools.partial(cot_kernel, ng, n_outer),
        [f32(out_rows, HALF), bf((D, HALF))],
        [cot_even, cot_odd],
        list(dn_blocks),
        [sems(n_outer)],
        room=4,
        busy=20,
    )
    att_odd, back = fence(att_odd, back)
    nge, ngo, mixed, comb = call(
        mix_kernel,
        [bf((half_rows, WIDE)), bf((half_rows, WIDE)), hbm((rows, D), F32), hbm((rows, EXTRA), F32)],
        [att_even, att_odd, tok_even, tok_odd, wo],
        scratch=[vm((out_rows, D), BF16)],
        room=8,
    )
    gu_blocks, nge, ngo = fence(gu_blocks, nge, ngo)

    def experts(wide, weights, base):
        outs = [bf((half_rows, HALF)), bf((half_rows, 2 * HALF)), bf((half_rows, WIDE))]
        kernel = functools.partial(expert_kernel, base, ng, n_outer)
        if base:
            outs.append(bf((D, 2 * HALF)))
            return call(kernel, outs, [wide, back], weights, [sems(n_outer)], room=8)
        return call(kernel, outs, [wide, back, weights], room=8)

    acto, gguo, odd, w_gu = experts(ngo, list(gu_blocks), half_rows)
    odd, nge = fence(odd, nge)
    odd_got = links.core(odd)
    acte, ggue, even = experts(nge, w_gu, 0)
    odd_got, even, acte, ggue = fence(odd_got, even, acte, ggue)
    sums = pair(even, odd_got)
    sums = fence(*sums)
    got = spread(sums)
    sums, got = fence(sums, got)
    grad_mixed, grad_wide = call(
        turn_kernel,
        [f32(rows, D), bf((rows, WIDE))],
        [sums[0]] + list(got) + [mixed, cot, comb, wo],
        room=8,
    )
    grad_wide, nge, ngo, acte, acto = fence(grad_wide, nge, ngo, acte, acto)
    grad_near = links.near(grad_wide)
    gu_other, dn_other, gu_mine, dn_mine = call(
        expert_grad_kernel,
        [bf((D // 2, 2 * HALF)), bf((D // 2, HALF))] * 2,
        [cot_even, cot_odd, nge, ngo, acte, acto, ggue, gguo],
        scratch=[vm((half_rows, HALF), BF16), vm((half_rows, HALF), BF16)],
        room=4,
        busy=20,
    )
    out_even, out_odd = call(
        expert_out_kernel, [bf((half_rows, D))] * 2, [w_dn, nge, ngo, acte, acto], room=4, busy=10
    )
    grad_wide, grad_near, out_odd, gu_other, dn_other, gu_mine, dn_mine = fence(
        grad_wide, grad_near, out_odd, gu_other, dn_other, gu_mine, dn_mine
    )
    dn_got = links.outer(dn_other, 1, 0)
    gu_got = links.outer(gu_other, 1, 0)
    grad_even = pack([grad_wide] + list(grad_near))
    grad_even, out_odd = fence(grad_even, out_odd)
    grad_odd = links.core(grad_even)
    out_got = links.core(out_odd)
    grad_odd, out_got = fence(grad_odd, out_got)
    out_sums = pair(out_even, out_got)
    grad_heads = call(
        grad_rows_kernel, [bf((CUBE, rows, QH))], [wo, grad_even, grad_odd], room=3
    )[0]
    grads = call(
        functools.partial(attend_back_kernel, slots, ng),
        [bf((CUBE, rows, QH)), f32(MB, extent, 2 * HD)] + [bf((MB, extent, 2 * HD))] * (ng - 1),
        [q] + kvs + [ot, lse, grad_heads],
        scratch=[vm((extent, 2 * HD), BF16)],
        room=12,
    )
    gq, gkv, grads = grads[0], grads[1], grads[2:]
    gq, gkv, grads, grad_even, grad_odd, out_sums, dn_got, dn_mine = fence(
        gq, gkv, grads, grad_even, grad_odd, out_sums, dn_got, dn_mine
    )
    out_got = spread(out_sums)
    gkv_others = [links.climb(grads[step - 1], -step) for step in range(1, ng)]
    wo_weight = call(
        out_grad_kernel,
        [hbm((D, OUT_SLAB))],
        [grad_even, grad_odd, att, nge, ngo],
        scratch=[vm((half_rows, QH), BF16), vm((half_rows, QH), BF16)],
        room=3,
        busy=20,
    )[0]
    dn_kept = fold(dn_mine, dn_got)
    gkv_others, gq, gkv, out_got, wo_weight, dn_kept = fence(
        gkv_others, gq, gkv, out_got, wo_weight, dn_kept
    )
    dn_groups = send_groups(dn_kept)
    gqkv, even, odd = call(
        functools.partial(close_kernel, ng),
        [bf((out_rows, SLAB)), bf((half_rows, D)), bf((half_rows, D))],
        [gq, wq, gkv] + list(gkv_others),
        room=3,
    )
    odd, gqkv, even = fence(odd, gqkv, even)
    odd_got = links.core(odd)
    gu_kept = fold(gu_mine, gu_got)
    qkvo_other, qkvo_mine = call(
        qkv_grad_kernel,
        [bf((D // 2, SLAB + OUT_SLAB))] * 2,
        [xg, gqkv, wo_weight],
        room=3,
    )
    odd_got, gu_kept, even, dn_groups = fence(odd_got, gu_kept, even, dn_groups)
    gu_groups = send_groups(gu_kept)
    qkvo_got = links.outer(qkvo_other, 1, 0)
    sums = pair(even, odd_got)
    got = spread(sums)
    qkvo_kept = fold(qkvo_mine, qkvo_got)
    sums, got, qkvo_kept = fence(sums, got, qkvo_kept)
    qkvo_groups = send_groups(qkvo_kept)
    grad_tokens = call(
        tokens_kernel, [bf((rows, D))], [sums[0]] + list(got) + [tok, grad_mixed, gain1]
    )[0]
    gu_groups, grad_tokens = fence(gu_groups, grad_tokens)
    moe_sum = call(
        functools.partial(fold_last_kernel, ng),
        [bf((CUBE * wr, 3 * HALF))],
        list(gu_groups) + list(dn_groups),
        room=2,
    )[0]
    expert_parts = links.swap(moe_sum.reshape(CUBE, wr, 3 * HALF))
    cuts = call(
        functools.partial(fold_parts_kernel, ng),
        [bf((wr, SLAB + OUT_SLAB))] * CUBE,
        qkvo_groups,
        scratch=[vm((CUBE, wr, SLAB + OUT_SLAB), BF16)],
        room=2,
    )
    qkvo_parts = [cuts[0]] + [links.cube(cuts[k], k) for k in range(1, CUBE)]
    output = call(output_kernel, [bf((rows, D))], [out_sums[0]] + list(out_got) + [mixed])[0]
    grad_qkv, grad_attn_gain, grad_out, grad_router = call(
        finish_attention_kernel,
        [f32(wr, QW + 2 * KW), f32(1, wr), f32(wr, QW), f32(8, wr)],
        [qkv_weight, attn_gain.reshape(1, wr)] + qkvo_parts,
        scratch=[vm((CUBE, wr, SLAB + OUT_SLAB), BF16)],
        room=3,
    )
    grad_gateup, grad_moe_gain, grad_down = call(
        finish_experts_kernel,
        [f32(E, wr, 2 * FF), f32(1, wr), f32(E, wr, FF)],
        [expert_parts, gateup_weight, grad_router, router.T, moe_gain.reshape(1, wr)],
        room=3,
    )
    return (
        output.reshape(MB, 1, slots, D),
        grad_tokens.reshape(MB, 1, slots, D),
        grad_attn_gain.reshape(wr),
        grad_qkv,
        grad_out.T,
        grad_moe_gain.reshape(wr),
        grad_router[:E].T,
        grad_gateup,
        grad_down.transpose(0, 2, 1),
    )


def solution(mesh):
    in_specs = (
        P(None, "dp", "ctx", None),
        P(None, "dp"),
        P(None, "dp", "ctx", None),
        P(None, "dp", "ctx", None),
        P(("dp", "ctx")),
        P(("dp", "ctx"), None),
        P(None, ("dp", "ctx")),
        P(("dp", "ctx")),
        P(("dp", "ctx"), None),
        P(None, ("dp", "ctx"), None),
        P(None, None, ("dp", "ctx")),
    )
    out_specs = (
        P(None, "dp", "ctx", None),
        P(None, "dp", "ctx", None),
        P(("dp", "ctx")),
        P(("dp", "ctx"), None),
        P(None, ("dp", "ctx")),
        P(("dp", "ctx")),
        P(("dp", "ctx"), None),
        P(None, ("dp", "ctx"), None),
        P(None, None, ("dp", "ctx")),
    )
    return jax.shard_map(body, mesh=mesh, in_specs=in_specs, out_specs=out_specs, check_vma=False)
```

```python
import functools
import math

import jax
import jax.numpy as jnp
from jax import lax
from jax.experimental import pallas as pl
from jax.experimental.pallas import tpu as pltpu
from jax.sharding import PartitionSpec as P

D = 1536
H = 24
KVH = 8
HD = 64
FF = 1024
E = 4
MB = 2
QW = 1536
KW = 512
CUBE = 8
GROUP = H // KVH
HALF = FF // 2
QH = GROUP * HD
SHARD = QH + 2 * HD
SLAB = 384
OUT_SLAB = 256
PAIR = 2 * QH
EXTRA = 128
WIDE = D + EXTRA
ORDER = (0, 4, 2, 6, 1, 5, 3, 7)
LOG2E = 1.4426950408889634
F32 = jnp.float32
BF16 = jnp.bfloat16
NN = (((1,), (0,)), ((), ()))
NT = (((1,), (1,)), ((), ()))
TN = (((0,), (0,)), ((), ()))
AXES = ("dp", "ctx")


def dot(left, right, dims=NN):
    return lax.dot_general(left, right, dims, preferred_element_type=F32)


class Kernels:
    def __init__(self, lengths):
        self.lengths = lengths

    def __call__(self, kernel, outs, ins, far=(), scratch=(), room=0, after=(), busy=0):
        ins, far, after = list(ins), list(far), list(after)
        n_in, n_after = 1 + len(ins) + len(far), len(after)
        vmem = pl.BlockSpec(memory_space=pltpu.VMEM)
        anywhere = pl.BlockSpec(memory_space=pl.ANY)

        def run(lengths, *refs):
            ctx = lax.axis_index("ctx")
            scal = [lax.axis_index("dp"), ctx >> 3, ctx & 7, lengths[0, 0], lengths[1, 0]]
            kernel(scal, *refs[: n_in - 1], *refs[n_in - 1 + n_after :])

        moved = sum(math.prod(a.shape) * a.dtype.itemsize for a in ins + list(outs))
        held = sum(2 * math.prod(s.shape) for s in scratch if hasattr(s, "shape"))
        grant = int(1.1 * moved) + held + (room + 4) * 1024 * 1024
        results = pl.pallas_call(
            run,
            out_shape=list(outs),
            in_specs=[pl.BlockSpec(memory_space=pltpu.SMEM)]
            + [vmem] * len(ins)
            + [anywhere] * (len(far) + n_after),
            out_specs=[vmem] * len(outs),
            scratch_shapes=list(scratch),
            compiler_params=pltpu.CompilerParams(vmem_limit_bytes=min(grant, 56 * 1024 * 1024)),
            cost_estimate=pl.CostEstimate(
                flops=1000 + busy * 10**9, bytes_accessed=1000, transcendentals=0
            ),
        )(
            self.lengths,
            *ins,
            *[pltpu.with_memory_space_constraint(value, pltpu.HBM) for value in far],
            *after,
        )
        return results


def sems(count):
    return pltpu.SemaphoreType.DMA((count,))


def shape(dims, dtype=BF16):
    return jax.ShapeDtypeStruct(dims, dtype)


class Links:
    def __init__(self, nx, nc):
        self.nx, self.nc, self.ng = nx, nc, nc // CUBE

    def _pairs(self, move):
        pairs = []
        for x in range(self.nx):
            for g in range(self.ng):
                for t in range(CUBE):
                    goal = move(x, g, t)
                    if goal is not None:
                        gx, gg, gt = goal
                        pairs.append((x * self.nc + g * CUBE + t, gx * self.nc + gg * CUBE + gt))
        return pairs

    def cube(self, value, bits):
        return lax.ppermute(value, AXES, self._pairs(lambda x, g, t: (x, g, t ^ bits)))

    def outer(self, value, dx, dg):
        return lax.ppermute(value, AXES, self._pairs(lambda x, g, t: (x ^ dx, g ^ dg, t)))

    def climb(self, value, step):
        def move(x, g, t):
            return (x, g + step, t) if 0 <= g + step < self.ng else None

        return lax.ppermute(value, AXES, self._pairs(move))

    def cubes(self):
        return [
            [x * self.nc + g * CUBE + t for t in range(CUBE)]
            for x in range(self.nx)
            for g in range(self.ng)
        ]

    def swap(self, value):
        return lax.all_to_all(
            value, AXES, split_axis=0, concat_axis=0, tiled=True, axis_index_groups=self.cubes()
        )

    def swap_all(self, value):
        return lax.all_to_all(value, AXES, split_axis=0, concat_axis=0, tiled=True)

    def near(self, rows):
        return [self.cube(rows, bits) for bits in ORDER[1:4]]

    def core(self, rows):
        return self.cube(rows, 1)

    def cores(self):
        return [list(range(core, self.nx * self.nc, 2)) for core in range(2)]

    def outers(self):
        return [
            [x * self.nc + g * CUBE + t for x in range(self.nx) for g in range(self.ng)]
            for t in range(CUBE)
        ]

    def outer_direct(self, rows):
        return [rows] + [
            self.outer(rows, dx, dg)
            for dx in range(self.nx)
            for dg in range(self.ng)
            if dx or dg
        ]


def fence(*values):
    return lax.optimization_barrier(values)


def stack_copies(refs, out, sem):
    rows = refs[0].shape[0]
    return [
        pltpu.make_async_copy(ref, out.at[pl.ds(n * rows, rows)], sem.at[n])
        for n, ref in enumerate(refs)
    ]


def outer_copies(refs, out, sem, scal, ng):
    rows = refs[0].shape[0]
    copies = []
    for j, ref in enumerate(refs):
        place = (scal[0] ^ (j // ng)) * ng + (scal[1] ^ (j % ng))
        spot = pl.ds(pl.multiple_of(place * rows, 16), rows)
        copies.append(pltpu.make_async_copy(ref, out.at[spot], sem.at[j]))
    return copies


def start_all(copies):
    for copy in copies:
        copy.start()


def wait_all(copies):
    for copy in copies:
        copy.wait()


def prep_kernel(scal, w_ref, gain_ref, tok_ref, routes_ref, out_ref, tok_out):
    wr = w_ref.shape[0]
    fill = column(gain_ref, SLAB - SHARD).astype(BF16)
    for k in range(CUBE):
        out_ref[k] = jnp.concatenate(
            [
                w_ref[:, k * QH : (k + 1) * QH],
                w_ref[:, QW + k * HD : QW + (k + 1) * HD],
                w_ref[:, QW + KW + k * HD : QW + KW + (k + 1) * HD],
                fill,
            ],
            axis=1,
        )
    rows = tok_ref.shape[0]
    tok_out[:, :D] = tok_ref[...]
    lane = lax.broadcasted_iota(jnp.int32, (rows, EXTRA), 1)
    names = jnp.where(lane == 0, routes_ref[:, 0:1], routes_ref[:, 1:2])
    tok_out[:, D:] = names.astype(F32).astype(BF16)


def column(row_ref, width):
    return jnp.broadcast_to(row_ref[...].astype(F32), (width, row_ref.shape[1])).T


def as_row(values):
    return jnp.broadcast_to(values, (values.shape[0], EXTRA)).T[0:1, :]


def prep_out_kernel(scal, wo_ref, rt_ref, gain_ref, wo_out):
    wr = wo_ref.shape[0]
    rt = rt_ref[...].astype(F32)
    rows = jnp.concatenate(
        [rt, rt, gain_ref[...].astype(F32), jnp.zeros((EXTRA - 2 * E - 1, wr), F32)], axis=0
    )
    wo_out[0, :, :QW] = wo_ref[...]
    wo_out[0, :, QW:] = rows.T.astype(BF16)


def order_kernel(ng, n_outer, scal, even_ref, odd_ref, out_ref):
    for q, k in enumerate(ORDER):
        source = even_ref if q < 4 else odd_ref
        for j in range(n_outer):
            group = (scal[0] ^ (j // ng)) * ng + (scal[1] ^ (j % ng))
            out_ref[group * CUBE + (scal[2] ^ k)] = source[(q % 4) * n_outer + j]


def prep_experts_kernel(scal, gu_ref, dn_ref, moe_out):
    for k in range(CUBE):
        e, h = k // 2, k % 2
        moe_out[k, :, :HALF] = gu_ref[e, :, h * HALF : (h + 1) * HALF]
        moe_out[k, :, HALF : 2 * HALF] = gu_ref[e, :, FF + h * HALF : FF + (h + 1) * HALF]
        moe_out[k, :, 2 * HALF :] = dn_ref[e, :, h * HALF : (h + 1) * HALF]


def split_kernel(scal, both_ref, gu_ref, dn_ref):
    gu_ref[...] = both_ref[:, : 2 * HALF]
    dn_ref[...] = both_ref[:, 2 * HALF :]


def pack_kernel(scal, *refs):
    rows = refs[0].shape[0]
    for n, ref in enumerate(refs[:-1]):
        refs[-1][n * rows : (n + 1) * rows, :] = ref[...]


def qkv_kernel(ng, n_outer, scal, even_ref, odd_ref, *refs):
    t = scal[2]
    weights, (xg, q_out, kv_out, gain_ref, w_ref, sem) = refs[:n_outer], refs[n_outer:]
    copies = outer_copies(weights, w_ref, sem, scal, ng)
    start_all(copies)
    wait_all(copies)
    rows = even_ref.shape[0] // 4
    slots = rows // MB
    blank = jnp.zeros((slots, HD), BF16)
    gain = w_ref[:, 256:].astype(F32).T[SHARD - 256 : SHARD - 248, :]
    gain_ref[...] = gain
    gain = gain[0:1]
    for p, k in enumerate(ORDER):
        source = even_ref if p < 4 else odd_ref
        values = source[(p % 4) * rows : (p % 4 + 1) * rows, :D].astype(F32)
        scale = lax.rsqrt(jnp.mean(values * values, axis=-1, keepdims=True) + 1e-05)
        packed = (values * scale * gain).astype(BF16)
        xg[p * rows : (p + 1) * rows, :] = packed
        y = dot(packed, w_ref[...]).astype(BF16)
        for m in range(MB):
            part = y[m * slots : (m + 1) * slots]
            spot = pl.ds(pl.multiple_of((t ^ k) * slots, 64), slots)
            for h in range(GROUP):
                q_out[m, h, spot, :] = jnp.concatenate(
                    [part[:, h * HD : (h + 1) * HD], blank], axis=1
                )
            kv_out[m, spot, :] = part[:, QH:SHARD]


def key_bias(extent, g, step, length):
    local = lax.broadcasted_iota(jnp.int32, (extent, 1), 0)
    seen = ((g - step) * extent + local < length) & (g >= step)
    return jnp.where(seen, 0.0, -1e30).astype(F32)


def causal_bias(extent):
    keys = lax.broadcasted_iota(jnp.int32, (extent, extent), 0)
    rows = lax.broadcasted_iota(jnp.int32, (extent, extent), 1)
    return jnp.where(keys <= rows, 0.0, -1e30).astype(F32)


def attend_kernel(slots, scal, *refs):
    g = scal[1]
    n_keys = len(refs) - 4
    q_ref, kv_refs, (att_ref, ot_ref, lse_ref) = refs[0], refs[1 : 1 + n_keys], refs[1 + n_keys :]
    extent = q_ref.shape[2]
    causal = causal_bias(extent)
    for m in range(MB):
        length = scal[3 + m]
        biases = [key_bias(extent, g, s, length) for s in range(n_keys)]
        for h in range(GROUP):
            q = q_ref[m, h]
            top = total = acc = None
            for s in range(n_keys):
                kv = kv_refs[s][m]
                st = dot(kv, q, NT) * (0.125 * LOG2E) + biases[s]
                if s == 0:
                    st = st + causal
                peak = jnp.max(st, axis=0, keepdims=True)
                if s == 0:
                    pt = jnp.exp2(st - peak)
                    top, total = peak, jnp.sum(pt, axis=0, keepdims=True)
                    acc = dot(kv, pt.astype(BF16), TN)
                else:
                    fresh = jnp.maximum(top, peak)
                    scale = jnp.exp2(top - fresh)
                    pt = jnp.exp2(st - fresh)
                    total = total * scale + jnp.sum(pt, axis=0, keepdims=True)
                    acc = acc * scale + dot(kv, pt.astype(BF16), TN)
                    top = fresh
            ot = acc[HD:, :] / total
            ot_ref[m, h] = ot
            lse_ref[m, h : h + 1, :] = top + jnp.log2(total)
            o = ot.T.astype(BF16)
            for k in range(CUBE):
                place = (k // 4) * QH + h * HD
                base = (k % 4) * MB * slots + m * slots
                att_ref[base : base + slots, place : place + HD] = o[k * slots : (k + 1) * slots]


def row_valid(scal, rows):
    slots = rows // MB
    spot = lax.broadcasted_iota(jnp.int32, (rows, 1), 0)
    place = (scal[1] * CUBE + scal[2]) * slots
    length = jnp.where(spot < slots, scal[3], scal[4])
    inner = jnp.where(spot < slots, spot, spot - slots)
    return jnp.where(place + inner < length, 1.0, 0.0).astype(F32)


def gain_row(rest):
    return rest.astype(F32).T[2 * E : 2 * E + 1, :]


def att_block(ref, base, rows, j):
    spot = pl.ds(pl.multiple_of(base + (j & 3) * rows, 16), rows)
    both = ref[spot, :]
    return jnp.where(j >= 4, both[:, QH:], both[:, :QH])


def mix_kernel(scal, even_ref, odd_ref, toke_ref, toko_ref, wo_ref, *refs):
    t = scal[2]
    nge, ngo, mixed_ref, comb_ref, att = refs
    rows = mixed_ref.shape[0]
    slots = rows // MB
    for q in range(4):
        head = t ^ ORDER[q]
        lanes = pl.ds(pl.multiple_of((head >> 1) * PAIR, 128), PAIR)
        for p, k in enumerate(ORDER):
            low = att_block(even_ref, q * 4 * rows, rows, t ^ k)
            high = att_block(odd_ref, q * 4 * rows, rows, t ^ k)
            flip = (head & 1) == 1
            att[p * rows : (p + 1) * rows, lanes] = jnp.concatenate(
                [jnp.where(flip, high, low), jnp.where(flip, low, high)], axis=1
            )
    rest = wo_ref[:, QW:]
    gain = gain_row(rest)
    lane = lax.broadcasted_iota(jnp.int32, (2 * rows, EXTRA), 1)
    spot = lax.broadcasted_iota(jnp.int32, (2 * rows, 1), 0)
    inner = spot & (rows - 1)
    second = inner >= slots
    length = jnp.where(second, scal[4], scal[3])
    slot = jnp.where(second, inner - slots, inner)
    for p in range(0, CUBE, 2):
        tok_ref, out_ref = (toke_ref, nge) if p < 4 else (toko_ref, ngo)
        local = slice((p % 4) * rows, (p % 4 + 2) * rows)
        owner = jnp.where(spot < rows, t ^ ORDER[p], t ^ ORDER[p + 1])
        place = (scal[1] * CUBE + owner) * slots + slot
        valid = jnp.where(place < length, 1.0, 0.0).astype(F32)
        branch = dot(att[p * rows : (p + 2) * rows, :], wo_ref[:, :QW], NT)
        mixed = tok_ref[local, :D].astype(F32) + valid * branch
        scale = lax.rsqrt(jnp.mean(mixed * mixed, axis=-1, keepdims=True) + 1e-05)
        low = (mixed * scale * gain).astype(BF16)
        logits = dot(low, rest)
        names = tok_ref[local, D:].astype(F32)
        expert = (lane & (E - 1)).astype(F32)
        chosen = ((expert == names[:, 0:1]) | (expert == names[:, 1:2])) & (lane < 2 * E)
        peak = jnp.max(jnp.where(chosen, logits, -3e38), axis=-1, keepdims=True)
        expo = jnp.where(chosen, jnp.exp(logits - peak), 0.0)
        comb = expo / (0.5 * jnp.sum(expo, axis=-1, keepdims=True))
        if p == 0:
            mixed_ref[...] = mixed[:rows]
            comb_ref[...] = jnp.where(lane < E, comb, 0.0)[:rows]
        comb = comb * valid
        high = comb.astype(BF16)
        tail = (comb - high.astype(F32)).astype(BF16)
        out_ref[local, :D] = low
        out_ref[local, D:] = jnp.where(lane < E, high, tail)


def row_valid(scal, rows):
    slots = rows // MB
    spot = lax.broadcasted_iota(jnp.int32, (rows, 1), 0)
    place = (scal[1] * CUBE + scal[2]) * slots
    length = jnp.where(spot < slots, scal[3], scal[4])
    inner = jnp.where(spot < slots, spot, spot - slots)
    return jnp.where(place + inner < length, 1.0, 0.0).astype(F32)


def cot_kernel(ng, n_outer, scal, even_ref, odd_ref, *refs):
    dn_blocks, (q_ref, w_dn, sem) = refs[:n_outer], refs[n_outer:]
    copies = outer_copies(dn_blocks, w_dn, sem, scal, ng)
    start_all(copies)
    wait_all(copies)
    step = even_ref.shape[0] // 2
    for part, source in enumerate((even_ref, odd_ref)):

        @pl.loop(0, 2)
        def _(i):
            local = pl.ds(pl.multiple_of(i * step, 128), step)
            spot = pl.ds(pl.multiple_of((2 * part + i) * step, 128), step)
            q_ref[spot, :] = dot(source[local, :], w_dn[...])


def own_share(wide, scal):
    lane = lax.broadcasted_iota(jnp.int32, wide.shape, 1)
    expert = scal[2] // 2
    mine = (lane == expert) | (lane == expert + E)
    return jnp.sum(jnp.where(mine, wide.astype(F32), 0.0), axis=-1, keepdims=True)


def expert_kernel(base, ng, n_outer, scal, ngw, q_ref, *refs):
    if base:
        blocks, (act_ref, ggu_ref, out_ref, w_ref, sem) = refs[:n_outer], refs[n_outer:]
        copies = outer_copies(blocks, w_ref, sem, scal, ng)
        start_all(copies)
        wait_all(copies)
    else:
        w_ref, act_ref, ggu_ref, out_ref = refs
    step = ngw.shape[0] // 2
    expert = scal[2] // 2

    @pl.loop(0, 2)
    def _(i):
        spot = pl.ds(pl.multiple_of(i * step, 128), step)
        share = own_share(ngw[spot, D:], scal)
        gu = dot(ngw[spot, :D], w_ref[...])
        gate, up = gu[:, :HALF], gu[:, HALF:]
        sig = 1.0 / (1.0 + jnp.exp(-gate))
        soft = gate * sig
        act = (soft * up).astype(BF16)
        act_ref[spot, :] = act
        back = q_ref[pl.ds(pl.multiple_of(base + i * step, 128), step), :]
        dots = jnp.sum(act.astype(F32) * back, axis=-1, keepdims=True)
        back = back * share
        ggu_ref[spot, :HALF] = (back * up * (sig * (1.0 + gate * (1.0 - sig)))).astype(BF16)
        ggu_ref[spot, HALF:] = (back * soft).astype(BF16)
        out_ref[spot, :D] = dot(ggu_ref[spot, :], w_ref[...], NT).astype(BF16)
        high = dots.astype(BF16)
        rest = (dots - high.astype(F32)).astype(BF16)
        lane = lax.broadcasted_iota(jnp.int32, (step, EXTRA), 1)
        out_ref[spot, D:] = jnp.where(
            lane == expert, high, jnp.where(lane == expert + E, rest, jnp.zeros_like(rest))
        )


def expert_grad_kernel(
    scal, dye, dyo, nge, ngo, acte, acto, ggue, gguo, gu_other, dn_other, gu_mine, dn_mine, cae, cao
):
    for wide, act, out in ((nge, acte, cae), (ngo, acto, cao)):
        out[...] = (act[...].astype(F32) * own_share(wide[:, D:], scal)).astype(BF16)
    cut = D // 6
    for flip, gu_ref, dn_ref in ((1, gu_other, dn_other), (0, gu_mine, dn_mine)):

        @pl.loop(0, 3)
        def _(i):
            cols = pl.ds(pl.multiple_of((scal[0] ^ flip) * (D // 2) + i * cut, 128), cut)
            spot = pl.ds(pl.multiple_of(i * cut, 128), cut)
            total = dot(nge[:, cols], ggue[...], TN) + dot(ngo[:, cols], gguo[...], TN)
            gu_ref[spot, :] = total.astype(BF16)
            total = dot(dye[:, cols], cae[...], TN) + dot(dyo[:, cols], cao[...], TN)
            dn_ref[spot, :] = total.astype(BF16)


def expert_out_kernel(scal, w_ref, nge, ngo, acte, acto, even_ref, odd_ref):
    step = acte.shape[0] // 2
    for wide, act, out_ref in ((nge, acte, even_ref), (ngo, acto, odd_ref)):

        @pl.loop(0, 2)
        def _(i):
            spot = pl.ds(pl.multiple_of(i * step, 128), step)
            share = own_share(wide[spot, D:], scal)
            out_ref[spot, :] = (dot(act[spot, :], w_ref[...], NT) * share).astype(BF16)


def fold_kernel(ng, scal, mine_ref, got_ref, *refs):
    rows = mine_ref.shape[0] // ng
    for dg, out in enumerate(refs):
        spot = pl.ds(pl.multiple_of((scal[1] ^ dg) * rows, 16), rows)
        total = mine_ref[spot, :].astype(F32) + got_ref[spot, :].astype(F32)
        out[...] = total.astype(out.dtype)


def fold_last_kernel(n_in, scal, *refs):
    base = 0
    for ins in (refs[:n_in], refs[n_in:-1]):
        total = ins[0][...]
        for ref in ins[1:]:
            total = total + ref[...].astype(F32)
        refs[-1][:, base : base + total.shape[1]] = total.astype(BF16)
        base += total.shape[1]


def fold_parts_kernel(n_in, scal, *refs):
    ins, outs = refs[:n_in], refs[n_in:]
    wr = outs[0].shape[0]
    for j in range(CUBE):
        spot = slice(j * wr, (j + 1) * wr)
        total = ins[0][spot, :]
        for ref in ins[1:]:
            total = total + ref[spot, :].astype(F32)
        outs[-1][j] = total.astype(BF16)
    for k, out in enumerate(outs[:-1]):
        out[...] = outs[-1][scal[2] ^ k]


def pair_kernel(scal, even_ref, odd_ref, *outs):
    rows = outs[0].shape[0]
    for p, out in enumerate(outs):
        spot = slice(p * rows, (p + 1) * rows)
        out[...] = (even_ref[spot, :].astype(F32) + odd_ref[spot, :].astype(F32)).astype(BF16)


def norm_back(grad, values, scale):
    unit = values * scale
    return scale * (grad - unit * jnp.mean(grad * unit, axis=-1, keepdims=True))


def turn_kernel(scal, a0, a1, a2, a3, mixed_ref, cot_ref, comb_ref, wo_ref, grad_ref, wide_ref):
    rest = wo_ref[:, QW:]
    rows = mixed_ref.shape[0]
    total = (
        a0[...].astype(F32) + a1[...].astype(F32) + a2[...].astype(F32) + a3[...].astype(F32)
    )
    valid = row_valid(scal, rows)
    lane = lax.broadcasted_iota(jnp.int32, (rows, EXTRA), 1)
    dots = total[:, D:]
    dots = (dots + pltpu.roll(dots, EXTRA - E, 1)) * valid
    comb = comb_ref[...]
    inner = jnp.sum(comb * dots, axis=-1, keepdims=True)
    grad_logits = jnp.where(lane < E, comb * (dots - inner), 0.0).astype(BF16)
    grad_normed = (total[:, :D] + dot(grad_logits, rest, NT)) * gain_row(rest)
    mixed = mixed_ref[...]
    scale = lax.rsqrt(jnp.mean(mixed * mixed, axis=-1, keepdims=True) + 1e-05)
    grad_mixed = cot_ref[...].astype(F32) + norm_back(grad_normed, mixed, scale)
    grad_ref[...] = grad_mixed
    branch = (valid * grad_mixed).astype(BF16)
    wide_ref[:, :D] = branch
    wide_ref[:, D:] = grad_logits


def grad_rows_kernel(scal, w_ref, even_ref, odd_ref, ga_ref):
    t = scal[2]
    rows = ga_ref.shape[1]
    window = w_ref[:, pl.ds(pl.multiple_of(((3 * t) >> 1) * 128, 128), 256)]
    weight = jnp.where((t & 1) == 1, window[:, HD:], window[:, :QH])
    for part, wide in enumerate((even_ref, odd_ref)):
        for n in range(2):
            spot = slice(2 * n * rows, 2 * (n + 1) * rows)
            grad = dot(wide[spot, :D], weight).astype(BF16)
            for i in range(2):
                ga_ref[t ^ ORDER[4 * part + 2 * n + i]] = grad[i * rows : (i + 1) * rows]


def attend_back_kernel(slots, n_keys, scal, *refs):
    g = scal[1]
    q_ref, kv_refs, refs = refs[0], refs[1 : 1 + n_keys], refs[1 + n_keys :]
    ot_ref, lse_ref, ga_ref, gq_ref, refs = refs[0], refs[1], refs[2], refs[3], refs[4:]
    gkv_refs, (do_ref,) = refs[:n_keys], refs[n_keys:]
    extent = q_ref.shape[2]
    causal = causal_bias(extent)
    blank = jnp.zeros((slots, HD), BF16)
    for m in range(MB):
        length = scal[3 + m]
        biases = [key_bias(extent, g, s, length) for s in range(n_keys)]
        sums = [None] * n_keys
        for h in range(GROUP):
            for k in range(CUBE):
                part = ga_ref[k, m * slots : (m + 1) * slots, h * HD : (h + 1) * HD]
                do_ref[k * slots : (k + 1) * slots, :] = jnp.concatenate([blank, part], axis=1)
            q = q_ref[m, h]
            do = do_ref[...]
            dot_t = do.astype(F32).T[HD:, :]
            delta = jnp.sum(dot_t * ot_ref[m, h], axis=0, keepdims=True)
            lse = lse_ref[m, h : h + 1, :]
            grad_q = None
            for s in range(n_keys):
                kv = kv_refs[s][m]
                st = dot(kv, q, NT) * (0.125 * LOG2E) + biases[s]
                if s == 0:
                    st = st + causal
                pt = jnp.exp2(st - lse)
                dpt = dot(kv, do, NT)
                dst = (pt * (dpt - delta) * 0.125).astype(BF16)
                part = dot(dst, q) + dot(pt.astype(BF16), do)
                sums[s] = part if sums[s] is None else sums[s] + part
                part = dot(kv, dst, TN)
                grad_q = part if grad_q is None else grad_q + part
            gq = grad_q[:HD, :].T.astype(BF16)
            for k in range(CUBE):
                gq_ref[k, m * slots : (m + 1) * slots, h * HD : (h + 1) * HD] = gq[
                    k * slots : (k + 1) * slots
                ]
        for s in range(n_keys):
            gkv_refs[s][m] = sums[s].astype(gkv_refs[s].dtype)


def close_kernel(n_keys, scal, gq_ref, w_ref, own_ref, *refs):
    t = scal[2]
    others, (gqkv, even_ref, odd_ref) = refs[: n_keys - 1], refs[n_keys - 1 :]
    rows = gq_ref.shape[1]
    slots = rows // MB
    gqkv[:, SHARD:] = jnp.zeros((CUBE * rows, SLAB - SHARD), BF16)
    for p, k in enumerate(ORDER):
        gqkv[p * rows : (p + 1) * rows, :QH] = gq_ref[t ^ k]
        for m in range(MB):
            spot = pl.ds(pl.multiple_of((t ^ k) * slots, 64), slots)
            total = own_ref[m, spot, :]
            for other in others:
                total = total + other[m, spot, :].astype(F32)
            base = p * rows + m * slots
            gqkv[base : base + slots, QH:SHARD] = total.astype(BF16)
    step = 2 * rows
    for part, out_ref in enumerate((even_ref, odd_ref)):

        @pl.loop(0, 2)
        def _(i):
            local = pl.ds(pl.multiple_of(i * step, 128), step)
            spot = pl.ds(pl.multiple_of(part * 2 * step + i * step, 128), step)
            out_ref[local, :] = dot(gqkv[spot, :], w_ref[...], NT).astype(BF16)


def qkv_grad_kernel(scal, xg, gqkv, wo_ref, other_ref, mine_ref):
    cut = D // 6
    for flip, out_ref in ((1, other_ref), (0, mine_ref)):

        @pl.loop(0, 3)
        def _(i):
            cols = pl.ds(pl.multiple_of((scal[0] ^ flip) * (D // 2) + i * cut, 128), cut)
            spot = pl.ds(pl.multiple_of(i * cut, 128), cut)
            out_ref[spot, :SLAB] = dot(xg[:, cols], gqkv[...], TN).astype(BF16)
            out_ref[spot, SLAB:] = wo_ref[cols, :]


def out_grad_kernel(scal, ge_ref, go_ref, att_ref, nge, ngo, w_out, ate, ato):
    rows = ge_ref.shape[0] // 4
    for p, k in enumerate(ORDER):
        out = ate if p < 4 else ato
        out[(p % 4) * rows : (p % 4 + 1) * rows, :] = att_block(att_ref, 0, rows, scal[2] ^ k)
    cut = D // 4

    @pl.loop(0, 4)
    def _(i):
        cols = pl.ds(pl.multiple_of(i * cut, 128), cut)
        total = dot(ge_ref[:, cols], ate[...], TN) + dot(go_ref[:, cols], ato[...], TN)
        w_out[cols, :QH] = total.astype(BF16)
        low = dot(nge[:, cols], ge_ref[:, D:], TN) + dot(ngo[:, cols], go_ref[:, D:], TN)
        w_out[cols, QH:] = low[:, : OUT_SLAB - QH].astype(BF16)


def finish_attention_kernel(scal, w_ref, gain_ref, *refs):
    parts, (out_ref, gain_out, wo_out, rt_out, got) = refs[:CUBE], refs[CUBE:]
    for k, ref in enumerate(parts):
        got[scal[2] ^ k] = ref[...]
    for k in range(CUBE):
        part = got[k].astype(F32)
        out_ref[:, k * QH : (k + 1) * QH] = part[:, :QH]
        out_ref[:, QW + k * HD : QW + (k + 1) * HD] = part[:, QH : QH + HD]
        out_ref[:, QW + KW + k * HD : QW + KW + (k + 1) * HD] = part[:, QH + HD : SHARD]
        wo_out[:, k * QH : (k + 1) * QH] = part[:, SLAB : SLAB + QH]
        if k == 0:
            rt_out[...] = part[:, SLAB + EXTRA :].T[QH - EXTRA : QH - EXTRA + 8]
    total = jnp.sum(out_ref[...] * w_ref[...].astype(F32), axis=-1, keepdims=True)
    gain_out[...] = as_row(total) / gain_ref[...].astype(F32)


def finish_experts_kernel(
    scal, got, w_ref, rg_ref, rt_ref, gain_ref, out_ref, gain_out, dn_out
):
    total = jnp.zeros((out_ref.shape[1], 1), F32)
    for k in range(CUBE):
        e, h = k // 2, k % 2
        for at, base in ((h * HALF, 0), (FF + h * HALF, HALF)):
            part = got[k, :, base : base + HALF].astype(F32)
            out_ref[e, :, at : at + HALF] = part
            weight = w_ref[e, :, at : at + HALF].astype(F32)
            total = total + jnp.sum(part * weight, axis=-1, keepdims=True)
        dn_out[e, :, h * HALF : (h + 1) * HALF] = got[k, :, 2 * HALF :].astype(F32)
    router = jnp.sum(rg_ref[:E] * rt_ref[...].astype(F32), axis=0, keepdims=True)
    gain_out[...] = (as_row(total) + router) / gain_ref[...].astype(F32)


def output_kernel(scal, a0, a1, a2, a3, mixed_ref, out_ref):
    total = (
        a0[...].astype(F32) + a1[...].astype(F32) + a2[...].astype(F32) + a3[...].astype(F32)
    )
    out_ref[...] = (mixed_ref[...] + total).astype(BF16)


def tokens_kernel(scal, a0, a1, a2, a3, x_ref, grad_ref, gain_ref, out_ref):
    total = (
        a0[...].astype(F32) + a1[...].astype(F32) + a2[...].astype(F32) + a3[...].astype(F32)
    )
    x = x_ref[...].astype(F32)
    scale = lax.rsqrt(jnp.mean(x * x, axis=-1, keepdims=True) + 1e-05)
    out_ref[...] = (grad_ref[...] + norm_back(total * gain_ref[0:1, :], x, scale)).astype(BF16)


def body(
    tokens,
    lengths,
    routes,
    cotangent,
    attn_gain,
    qkv_weight,
    out_weight,
    moe_gain,
    router,
    gateup_weight,
    down_weight,
):
    nx, nc = lax.axis_size("dp"), lax.axis_size("ctx")
    links = Links(nx, nc)
    ng = links.ng
    n_outer = nx * ng
    slots = tokens.shape[2]
    rows = MB * slots
    extent = CUBE * slots
    wr = attn_gain.shape[0]
    out_rows = CUBE * rows

    half_rows = out_rows // 2
    tok = tokens.reshape(rows, D)
    cot = cotangent.reshape(rows, D)
    call = Kernels(lengths)
    bf, vm = shape, pltpu.VMEM

    def hbm(dims, dtype=BF16):
        return pltpu.HBM(dims, dtype)

    def f32(*dims):
        return shape(dims, F32)

    def pair(even, got):
        return call(pair_kernel, [bf((rows, even.shape[1]))] * 4, [even, got])

    def spread(parts):
        return [links.cube(part, bits) for part, bits in zip(parts[1:], ORDER[1:4])]

    def fold(mine, got):
        part = (CUBE * wr, mine.shape[1])
        kept = call(
            functools.partial(fold_kernel, ng),
            [shape(part, F32)] + [bf(part)] * (ng - 1),
            [mine, got],
            room=2,
        )
        return list(kept)

    def send_groups(kept):
        return [kept[0]] + [links.outer(kept[dg], 0, dg) for dg in range(1, ng)]

    def pack(blocks):
        own = blocks[0].shape
        return call(pack_kernel, [bf((4 * own[0], own[1]))], blocks)[0]

    def pile(blocks):
        own = blocks[0].shape
        return call(pack_kernel, [bf((len(blocks) * own[0],) + own[1:])], blocks)[0]

    wq_parts, tok_wide = call(
        prep_kernel,
        [bf((CUBE, wr, SLAB)), bf((rows, WIDE))],
        [qkv_weight, attn_gain.reshape(1, wr), tok, routes.reshape(rows, 2)],
        room=3,
    )
    tok_wide, wq_parts, out_in = fence(tok_wide, wq_parts, out_weight.T)
    tok_near = links.near(tok_wide)
    wq_group = links.swap(wq_parts).reshape(CUBE * wr, SLAB)
    wo_part = call(
        prep_out_kernel,
        [bf((1, wr, WIDE))],
        [out_in, router.T, moe_gain.reshape(1, wr)],
        room=3,
        busy=20,
    )[0]
    wq_group, gateup_in, down_in = fence(
        wq_group, gateup_weight, down_weight.transpose(0, 2, 1)
    )
    moe_parts = call(
        prep_experts_kernel, [bf((CUBE, wr, 3 * HALF))], [gateup_in, down_in], room=3
    )[0]
    tok_wide, tok_near, wo_part = fence(tok_wide, tok_near, wo_part)
    tok_even = pack([tok_wide] + list(tok_near))
    tok_odd = links.core(tok_even)
    wq_far = [links.outer(wq_group, 0, dg) for dg in range(1, ng)]
    wo_far = [links.outer(wo_part, 0, dg) for dg in range(1, ng)]
    wq_blocks = [wq_group] + wq_far
    for dx in range(1, nx):
        wq_blocks += [links.outer(block, dx, 0) for block in wq_blocks[:ng]]
    moe_group = links.swap(moe_parts).reshape(CUBE * wr, 3 * HALF)
    tok_even, tok_odd, wq_blocks, moe_group, cot, wo_far = fence(
        tok_even, tok_odd, wq_blocks, moe_group, cot, wo_far
    )
    wo_row = pile([wo_part] + list(wo_far))
    wo_block = pile([wo_row] + [links.outer(wo_row, dx, 0) for dx in range(1, nx)])
    wo_even = pile([wo_block] + links.near(wo_block))
    xg, q, kv, gain1, wq = call(
        functools.partial(qkv_kernel, ng, n_outer),
        [
            hbm((out_rows, D)),
            bf((MB, GROUP, extent, 2 * HD)),
            bf((MB, extent, 2 * HD)),
            hbm((8, D), F32),
            hbm((D, SLAB)),
        ],
        [tok_even, tok_odd],
        wq_blocks,
        [sems(n_outer)],
        room=4,
    )
    gu_group, dn_group = call(
        split_kernel, [bf((CUBE * wr, 2 * HALF)), bf((CUBE * wr, HALF))], [moe_group]
    )
    dn_group, gu_group, cot = fence(dn_group, gu_group, cot)
    kvs = [links.climb(kv, step) for step in range(1, ng)]
    cot_near = links.near(cot)
    dn_far = [links.outer(dn_group, 0, dg) for dg in range(1, ng)]
    gu_side = [links.outer(gu_group, dx, 0) for dx in range(1, nx)]
    kv, kvs, dn_group, dn_far, gu_group, gu_side, cot, cot_near = fence(
        kv, kvs, dn_group, dn_far, gu_group, gu_side, cot, cot_near
    )
    wo_odd = links.core(wo_even)
    kvs = [kv] + list(kvs)
    cot_even = pack([cot] + list(cot_near))
    att, ot, lse = call(
        functools.partial(attend_kernel, slots),
        [bf((4 * rows, PAIR)), hbm((MB, GROUP, HD, extent), F32), hbm((MB, GROUP, extent), F32)],
        [q] + kvs,
        room=10,
    )
    cot_even, dn_group, dn_far, gu_group = fence(cot_even, dn_group, dn_far, gu_group)
    att_near = links.near(att)
    cot_odd = links.core(cot_even)
    dn_blocks = [dn_group] + list(dn_far)
    for dx in range(1, nx):
        dn_blocks += [links.outer(block, dx, 0) for block in dn_blocks[:ng]]
    gu_far = [links.outer(gu_group, 0, dg) for dg in range(1, ng)]
    att, att_near, cot_odd, dn_blocks, gu_far = fence(att, att_near, cot_odd, dn_blocks, gu_far)
    att_even = pack([att] + list(att_near))
    att_even, gu_far = fence(att_even, gu_far)
    att_odd = links.core(att_even)
    gu_blocks = [gu_group] + list(gu_far)
    for dx in range(1, nx):
        gu_blocks += [gu_side[dx - 1]] + [links.outer(block, dx, 0) for block in gu_far]
    wo = call(
        functools.partial(order_kernel, ng, n_outer),
        [bf((n_outer * CUBE, wr, WIDE))],
        [wo_even, wo_odd],
        room=2,
    )[0].reshape(D, WIDE)
    back, w_dn = call(
        functools.partial(cot_kernel, ng, n_outer),
        [f32(out_rows, HALF), bf((D, HALF))],
        [cot_even, cot_odd],
        list(dn_blocks),
        [sems(n_outer)],
        room=4,
        busy=20,
    )
    att_odd, back = fence(att_odd, back)
    nge, ngo, mixed, comb = call(
        mix_kernel,
        [bf((half_rows, WIDE)), bf((half_rows, WIDE)), hbm((rows, D), F32), hbm((rows, EXTRA), F32)],
        [att_even, att_odd, tok_even, tok_odd, wo],
        scratch=[vm((out_rows, D), BF16)],
        room=8,
    )
    gu_blocks, nge, ngo = fence(gu_blocks, nge, ngo)

    def experts(wide, weights, base):
        outs = [bf((half_rows, HALF)), bf((half_rows, 2 * HALF)), bf((half_rows, WIDE))]
        kernel = functools.partial(expert_kernel, base, ng, n_outer)
        if base:
            outs.append(bf((D, 2 * HALF)))
            return call(kernel, outs, [wide, back], weights, [sems(n_outer)], room=8)
        return call(kernel, outs, [wide, back, weights], room=8)

    acto, gguo, odd, w_gu = experts(ngo, list(gu_blocks), half_rows)
    odd, nge = fence(odd, nge)
    odd_got = links.core(odd)
    acte, ggue, even = experts(nge, w_gu, 0)
    odd_got, even, acte, ggue = fence(odd_got, even, acte, ggue)
    sums = pair(even, odd_got)
    sums = fence(*sums)
    got = spread(sums)
    sums, got = fence(sums, got)
    grad_mixed, grad_wide = call(
        turn_kernel,
        [f32(rows, D), bf((rows, WIDE))],
        [sums[0]] + list(got) + [mixed, cot, comb, wo],
        room=8,
    )
    grad_wide, nge, ngo, acte, acto = fence(grad_wide, nge, ngo, acte, acto)
    grad_near = links.near(grad_wide)
    gu_other, dn_other, gu_mine, dn_mine = call(
        expert_grad_kernel,
        [bf((D // 2, 2 * HALF)), bf((D // 2, HALF))] * 2,
        [cot_even, cot_odd, nge, ngo, acte, acto, ggue, gguo],
        scratch=[vm((half_rows, HALF), BF16), vm((half_rows, HALF), BF16)],
        room=4,
        busy=20,
    )
    out_even, out_odd = call(
        expert_out_kernel, [bf((half_rows, D))] * 2, [w_dn, nge, ngo, acte, acto], room=4, busy=10
    )
    grad_wide, grad_near, out_odd, gu_other, dn_other, gu_mine, dn_mine = fence(
        grad_wide, grad_near, out_odd, gu_other, dn_other, gu_mine, dn_mine
    )
    dn_got = links.outer(dn_other, 1, 0)
    gu_got = links.outer(gu_other, 1, 0)
    grad_even = pack([grad_wide] + list(grad_near))
    grad_even, out_odd = fence(grad_even, out_odd)
    grad_odd = links.core(grad_even)
    out_got = links.core(out_odd)
    grad_odd, out_got = fence(grad_odd, out_got)
    out_sums = pair(out_even, out_got)
    grad_heads = call(
        grad_rows_kernel, [bf((CUBE, rows, QH))], [wo, grad_even, grad_odd], room=3
    )[0]
    grads = call(
        functools.partial(attend_back_kernel, slots, ng),
        [bf((CUBE, rows, QH)), f32(MB, extent, 2 * HD)] + [bf((MB, extent, 2 * HD))] * (ng - 1),
        [q] + kvs + [ot, lse, grad_heads],
        scratch=[vm((extent, 2 * HD), BF16)],
        room=12,
    )
    gq, gkv, grads = grads[0], grads[1], grads[2:]
    gq, gkv, grads, grad_even, grad_odd, out_sums, dn_got, dn_mine = fence(
        gq, gkv, grads, grad_even, grad_odd, out_sums, dn_got, dn_mine
    )
    out_got = spread(out_sums)
    gkv_others = [links.climb(grads[step - 1], -step) for step in range(1, ng)]
    wo_weight = call(
        out_grad_kernel,
        [hbm((D, OUT_SLAB))],
        [grad_even, grad_odd, att, nge, ngo],
        scratch=[vm((half_rows, QH), BF16), vm((half_rows, QH), BF16)],
        room=3,
        busy=20,
    )[0]
    dn_kept = fold(dn_mine, dn_got)
    gkv_others, gq, gkv, out_got, wo_weight, dn_kept = fence(
        gkv_others, gq, gkv, out_got, wo_weight, dn_kept
    )
    dn_groups = send_groups(dn_kept)
    gqkv, even, odd = call(
        functools.partial(close_kernel, ng),
        [bf((out_rows, SLAB)), bf((half_rows, D)), bf((half_rows, D))],
        [gq, wq, gkv] + list(gkv_others),
        room=3,
    )
    odd, gqkv, even = fence(odd, gqkv, even)
    odd_got = links.core(odd)
    gu_kept = fold(gu_mine, gu_got)
    qkvo_other, qkvo_mine = call(
        qkv_grad_kernel,
        [bf((D // 2, SLAB + OUT_SLAB))] * 2,
        [xg, gqkv, wo_weight],
        room=3,
    )
    odd_got, gu_kept, even, dn_groups = fence(odd_got, gu_kept, even, dn_groups)
    gu_groups = send_groups(gu_kept)
    qkvo_got = links.outer(qkvo_other, 1, 0)
    sums = pair(even, odd_got)
    got = spread(sums)
    qkvo_kept = fold(qkvo_mine, qkvo_got)
    sums, got, qkvo_kept = fence(sums, got, qkvo_kept)
    qkvo_groups = send_groups(qkvo_kept)
    grad_tokens = call(
        tokens_kernel, [bf((rows, D))], [sums[0]] + list(got) + [tok, grad_mixed, gain1]
    )[0]
    gu_groups, grad_tokens = fence(gu_groups, grad_tokens)
    moe_sum = call(
        functools.partial(fold_last_kernel, ng),
        [bf((CUBE * wr, 3 * HALF))],
        list(gu_groups) + list(dn_groups),
        room=2,
    )[0]
    expert_parts = links.swap(moe_sum.reshape(CUBE, wr, 3 * HALF))
    cuts = call(
        functools.partial(fold_parts_kernel, ng),
        [bf((wr, SLAB + OUT_SLAB))] * CUBE,
        qkvo_groups,
        scratch=[vm((CUBE, wr, SLAB + OUT_SLAB), BF16)],
        room=2,
    )
    qkvo_parts = [cuts[0]] + [links.cube(cuts[k], k) for k in range(1, CUBE)]
    output = call(output_kernel, [bf((rows, D))], [out_sums[0]] + list(out_got) + [mixed])[0]
    grad_qkv, grad_attn_gain, grad_out, grad_router = call(
        finish_attention_kernel,
        [f32(wr, QW + 2 * KW), f32(1, wr), f32(wr, QW), f32(8, wr)],
        [qkv_weight, attn_gain.reshape(1, wr)] + qkvo_parts,
        scratch=[vm((CUBE, wr, SLAB + OUT_SLAB), BF16)],
        room=3,
    )
    grad_gateup, grad_moe_gain, grad_down = call(
        finish_experts_kernel,
        [f32(E, wr, 2 * FF), f32(1, wr), f32(E, wr, FF)],
        [expert_parts, gateup_weight, grad_router, router.T, moe_gain.reshape(1, wr)],
        room=3,
    )
    return (
        output.reshape(MB, 1, slots, D),
        grad_tokens.reshape(MB, 1, slots, D),
        grad_attn_gain.reshape(wr),
        grad_qkv,
        grad_out.T,
        grad_moe_gain.reshape(wr),
        grad_router[:E].T,
        grad_gateup,
        grad_down.transpose(0, 2, 1),
    )


def solution(mesh):
    in_specs = (
        P(None, "dp", "ctx", None),
        P(None, "dp"),
        P(None, "dp", "ctx", None),
        P(None, "dp", "ctx", None),
        P(("dp", "ctx")),
        P(("dp", "ctx"), None),
        P(None, ("dp", "ctx")),
        P(("dp", "ctx")),
        P(("dp", "ctx"), None),
        P(None, ("dp", "ctx"), None),
        P(None, None, ("dp", "ctx")),
    )
    out_specs = (
        P(None, "dp", "ctx", None),
        P(None, "dp", "ctx", None),
        P(("dp", "ctx")),
        P(("dp", "ctx"), None),
        P(None, ("dp", "ctx")),
        P(("dp", "ctx")),
        P(("dp", "ctx"), None),
        P(None, ("dp", "ctx"), None),
        P(None, None, ("dp", "ctx")),
    )
    return jax.shard_map(body, mesh=mesh, in_specs=in_specs, out_specs=out_specs, check_vma=False)
```
